32 devices in a mesh: tower: 16 (over z, x, core), batch: 2 (over y).
Axes of the slice: x: 2, y: 2, z: 4, core: 2. Of those that a mesh axis runs over, the one named last changes fastest.
Arguments:
- image_rows: bfloat16 [32, 197, 768], P(('tower', 'batch')), may hold values from -6 to 6
- text_rows: bfloat16 [32, 512, 768], P(('tower', 'batch')), may hold values from -6 to 6
- caption_lengths: int32 [32], replicated, may hold values from 8 to 512, as said below
- concat_cot: bfloat16 [32, 711, 768], P(('tower', 'batch')), may hold values from -6 to 6
- tile_slot: int32 [234], replicated, may hold values from 0 to 255, as said below
- tile_weight: float32 [256, 256, 256], P(('tower', 'batch'))
- tile_first: float32 [256, 256, 256], P(('tower', 'batch'))
- tile_second: float32 [256, 256, 256], P(('tower', 'batch')), as said below
- left_stat: float32 [256, 256, 256], P(('tower', 'batch')), as said below
- right_stat: float32 [256, 256, 256], P(('tower', 'batch')), as said below
- left_basis: float32 [256, 256, 256], P(('tower', 'batch')), as said below
- right_basis: float32 [256, 256, 256], P(('tower', 'batch')), as said below
- vec_weight: float32 [32, 768], P(('tower', 'batch'))
- vec_first: float32 [32, 768], P(('tower', 'batch'))
- vec_second: float32 [32, 768], P(('tower', 'batch')), as said below
Outputs:
- concat: bfloat16 [32, 711, 768], P(('tower', 'batch'))
- image_grad: bfloat16 [32, 197, 768], P(('tower', 'batch'))
- text_grad: bfloat16 [32, 512, 768], P(('tower', 'batch'))
- tile_weight_new: float32 [256, 256, 256], P(('tower', 'batch'))
- tile_first_new: float32 [256, 256, 256], P(('tower', 'batch'))
- tile_second_new: float32 [256, 256, 256], P(('tower', 'batch'))
- left_stat_new: float32 [256, 256, 256], P(('tower', 'batch'))
- right_stat_new: float32 [256, 256, 256], P(('tower', 'batch'))
- left_basis_new: float32 [256, 256, 256], P(('tower', 'batch'))
- right_basis_new: float32 [256, 256, 256], P(('tower', 'batch'))
- vec_weight_new: float32 [32, 768], P(('tower', 'batch'))
- vec_first_new: float32 [32, 768], P(('tower', 'batch'))
- vec_second_new: float32 [32, 768], P(('tower', 'batch'))
The draws below stay inside these ranges and needn't reach their ends.
Inputs may be any that keep to these rules, and one draw needn't show every extreme that they name: `caption_lengths`: some caption has 512 real rows and some has 8. `tile_slot`: distinct slots; slot 0 and slot 255 are among them; slot s is row s of the tile arrays. `left_basis`: each slot's matrix is orthogonal. `right_basis`: each slot's matrix is orthogonal. `left_stat`: each slot's matrix is symmetric positive definite. `right_stat`: each slot's matrix is symmetric positive definite. `tile_second`: positive entries. `vec_second`: positive entries.
All inputs are finite; a program needn't handle non-finite values.
Results may differ from the reference program's by a relative error of at most 0.014.
The reference program's roundings to bfloat16 on the way count: a program that leaves them out, or rounds other values in their place, can miss the bound.
Values may be sent and summed in bfloat16 or wider, within the bound.
A program may use at most 360 MiB of HBM per device.

```python
import jax
import jax.numpy as jnp
from jax import lax

D = 768
FF = 3072
HEADS = 12
HEAD_DIM = 64
IMG = 197
TXT = 512
MMROWS = 2
TILE_ORDER = 256
STEP = 10
PAIRS_DEV = 1
PAIRS = 32
CAT = 711
TILES_TOWER = 117
TILES_COMBINED = 234
SLOT_TOTAL = 256
VEC_TOWER = 15
VROWS = 32
N_TOWER = 16
N_BATCH = 2


def slot_table(key):
    key = jax.random.fold_in(key, 77)
    key_inner_draw, key_order = jax.random.split(key)
    inner_product = 1 + jax.random.permutation(key_inner_draw, SLOT_TOTAL - 2)[:TILES_COMBINED - 2]
    selected_slots = jnp.concatenate([jnp.array([0, SLOT_TOTAL - 1], jnp.int32), inner_product.astype(jnp.int32)])
    return jax.random.permutation(key_order, selected_slots)


def slot_scales(key):
    slot_index_list = slot_table(key)
    owning_tile = jnp.full((SLOT_TOTAL,), -1, jnp.int32).at[slot_index_list].set(jnp.arange(TILES_COMBINED, dtype=jnp.int32))
    local = owning_tile % TILES_TOWER
    square = (D // TILE_ORDER) ** 2
    oblong = D // TILE_ORDER * (FF // TILE_ORDER)
    bounds = jnp.array([square, 2 * square, 3 * square, 4 * square, 4 * square + oblong, 4 * square + 2 * oblong], jnp.int32)
    kind = jnp.sum((local[:, None] >= bounds[None, :]).astype(jnp.int32), 1)
    spread_table = jnp.array([1.5, 1.5, 1.0, 4.0, 1.0, (D / FF) ** 0.5, 1.0], jnp.float32) * D ** (-0.5)
    grad_table = jnp.array([0.3, 0.3, 0.3, 0.5, 0.3, 0.6, 1.0], jnp.float32)
    tokens = jnp.where(owning_tile >= TILES_TOWER, 0.5 * PAIRS * TXT, 1.0 * PAIRS * IMG)
    grad_size = grad_table[kind] * jnp.sqrt(tokens)
    return (spread_table[kind], grad_size)


def statistic(key, grad_size):
    key_diagonal_draw, key_cross_draw = jax.random.split(key)
    diagonal_part = jax.random.uniform(key_diagonal_draw, (SLOT_TOTAL, TILE_ORDER), jnp.float32, 1.0, 4.0)
    cross_terms = jax.random.normal(key_cross_draw, (SLOT_TOTAL, TILE_ORDER, TILE_ORDER), jnp.float32)
    mixed_part = jnp.einsum('nij,nkj->nik', cross_terms, cross_terms, precision=lax.Precision.HIGHEST) / TILE_ORDER
    scale_rows = 0.05 / 0.95 * TILE_ORDER * grad_size * grad_size
    return scale_rows[:, None, None] * (mixed_part + diagonal_part[:, :, None] * jnp.eye(TILE_ORDER, dtype=jnp.float32))


def rotation(key):
    key_row_draw, key_column_draw, key_row_signs, key_column_signs = jax.random.split(key, 4)
    position = jnp.arange(TILE_ORDER, dtype=jnp.int32)
    angles = position[:, None] * (2 * position[None, :] + 1) % (4 * TILE_ORDER)
    cosines = jnp.cos(angles.astype(jnp.float32) * (jnp.pi / (2 * TILE_ORDER))) * (2.0 / TILE_ORDER) ** 0.5
    cosines = jnp.where(position[:, None] == 0, (1.0 / TILE_ORDER) ** 0.5, cosines)
    row_permute = jax.vmap(lambda slot_number: jax.random.permutation(slot_number, TILE_ORDER))(jax.random.split(key_row_draw, SLOT_TOTAL))
    column_permute = jax.vmap(lambda slot_number: jax.random.permutation(slot_number, TILE_ORDER))(jax.random.split(key_column_draw, SLOT_TOTAL))
    row_signs = (2 * jax.random.randint(key_row_signs, (SLOT_TOTAL, TILE_ORDER), 0, 2) - 1).astype(jnp.float32)
    column_signs = (2 * jax.random.randint(key_column_signs, (SLOT_TOTAL, TILE_ORDER), 0, 2) - 1).astype(jnp.float32)
    picked = cosines[row_permute[:, :, None], column_permute[:, None, :]]
    return picked * row_signs[:, :, None] * column_signs[:, None, :]


def vector_sizes():
    rows = jnp.arange(VROWS)
    image_size = 0.7 * (1.0 * PAIRS * IMG) ** 0.5
    text_size = 0.7 * (0.5 * PAIRS * TXT) ** 0.5
    other_size = (1.0 * PAIRS) ** 0.5
    return jnp.where(rows < VEC_TOWER, image_size, jnp.where(rows < 2 * VEC_TOWER, text_size, other_size))


def draw_caption_lengths(key, part):
    key = jax.random.fold_in(key, 11)
    keys = jax.random.split(key, 7)
    half_size = N_TOWER // 2
    pair_ids = jnp.arange(PAIRS, dtype=jnp.int32)
    rank = pair_ids // PAIRS_DEV // N_BATCH % half_size
    top_len = 8 + (TXT - 8) * (half_size + 2 * rank) // (3 * half_size - 2)
    lengths = jax.random.randint(keys[0], (PAIRS,), jnp.maximum(top_len // 2, 8), top_len + 1)
    tower_high = half_size - 1 + half_size * jax.random.randint(keys[1], (), 0, 2)
    high_pair = (tower_high * N_BATCH + jax.random.randint(keys[2], (), 0, N_BATCH)) * PAIRS_DEV + jax.random.randint(keys[3], (), 0, PAIRS_DEV)
    tower_low = half_size * jax.random.randint(keys[4], (), 0, 2)
    low_pair = (tower_low * N_BATCH + jax.random.randint(keys[5], (), 0, N_BATCH)) * PAIRS_DEV + jax.random.randint(keys[6], (), 0, PAIRS_DEV)
    lengths = lengths.at[high_pair].set(TXT).at[low_pair].set(8)
    return lengths.astype(jnp.int32)


def draw_tile_slot(key, part):
    return slot_table(key)


def draw_tile_weight(key, part):
    spread, grad_size = slot_scales(key)
    key = jax.random.fold_in(key, 2)
    random_jitter = jax.random.normal(key, (SLOT_TOTAL, TILE_ORDER, TILE_ORDER), jnp.float32)
    return random_jitter * spread[:, None, None]


def draw_tile_first(key, part):
    spread, grad_size = slot_scales(key)
    key = jax.random.fold_in(key, 3)
    random_jitter = jax.random.normal(key, (SLOT_TOTAL, TILE_ORDER, TILE_ORDER), jnp.float32)
    return 0.1 / 0.9 * grad_size[:, None, None] * random_jitter


def draw_tile_second(key, part):
    spread, grad_size = slot_scales(key)
    key = jax.random.fold_in(key, 4)
    factor_matrix = jnp.exp(jax.random.uniform(key, (SLOT_TOTAL, TILE_ORDER, TILE_ORDER), jnp.float32, 0.0, 1.3862944))
    return 0.05 / 0.95 * (grad_size * grad_size)[:, None, None] * factor_matrix


def draw_left_stat(key, part):
    spread, grad_size = slot_scales(key)
    key = jax.random.fold_in(key, 5)
    return statistic(key, grad_size)


def draw_right_stat(key, part):
    spread, grad_size = slot_scales(key)
    key = jax.random.fold_in(key, 6)
    return statistic(key, grad_size)


def draw_left_basis(key, part):
    key = jax.random.fold_in(key, 7)
    return rotation(key)


def draw_right_basis(key, part):
    key = jax.random.fold_in(key, 8)
    return rotation(key)


def draw_vec_weight(key, part):
    key = jax.random.fold_in(key, 9)
    key_gain, key_bias = jax.random.split(key)
    rows = jnp.arange(VROWS)
    local = rows % VEC_TOWER
    after = 7 + FF // D
    is_gain = ((local == 0) | (local == 5) | (local == after + 1)) & (rows < 2 * VEC_TOWER)
    is_learned = (rows >= 2 * VEC_TOWER) & (rows < 2 * VEC_TOWER + MMROWS)
    gains = jax.random.uniform(key_gain, (VROWS, D), jnp.float32, 0.6, 1.4)
    random_jitter = jax.random.normal(key_bias, (VROWS, D), jnp.float32)
    return jnp.where(is_gain[:, None], gains, jnp.where(is_learned[:, None], random_jitter, 0.3 * random_jitter))


def draw_vec_first(key, part):
    key = jax.random.fold_in(key, 10)
    random_jitter = jax.random.normal(key, (VROWS, D), jnp.float32)
    return 0.1 / 0.9 * vector_sizes()[:, None] * random_jitter


def draw_vec_second(key, part):
    key = jax.random.fold_in(key, 12)
    factor_matrix = jnp.exp(jax.random.uniform(key, (VROWS, D), jnp.float32, 0.0, 1.3862944))
    sizes_rows = vector_sizes()
    return 0.05 / 0.95 * (sizes_rows * sizes_rows)[:, None] * factor_matrix


def levels(rng, dims, cuts, smallest, top_value):
    def one(dim, blocks):
        steps = jax.random.uniform(jax.random.fold_in(jax.random.fold_in(rng, 6), dim), (blocks,), jnp.float32, smallest / len(cuts), top_value / len(cuts))
        return jnp.repeat(jnp.exp(steps), dims[dim] // blocks).reshape((-1,) + (1,) * (len(dims) - dim - 1))

    loudness = one(*cuts[0])
    for cut in cuts[1:]:
        loudness = loudness * one(*cut)
    return loudness


def scatter_about(own_key, dims, scale, most, pieces=(), kind=jnp.bfloat16):
    values = jax.random.normal(own_key, dims, jnp.float32) * scale
    if len(pieces) > 0:
        values = levels(own_key, dims, pieces, -0.22, 0.18) * values
    return jnp.clip(values, min=-most, max=most).astype(kind)


def setup_inputs(seed: int = 0) -> dict:
    streams_of = jax.random.split(jax.random.key(seed), 16)
    image_rows = scatter_about(streams_of[0], (PAIRS, IMG, D), 1.0, 6.0, ((0, 32),))
    text_rows = scatter_about(streams_of[1], (PAIRS, TXT, D), 1.0, 6.0, ((0, 32),))
    caption_lengths = draw_caption_lengths(jax.random.fold_in(streams_of[15], 71), 0)
    concat_cot = scatter_about(streams_of[3], (PAIRS, CAT, D), 1.0, 6.0, ((0, 32),))
    tile_slot = draw_tile_slot(jax.random.fold_in(streams_of[15], 71), 0)
    tile_weight = draw_tile_weight(jax.random.fold_in(streams_of[15], 71), 0)
    tile_first = draw_tile_first(jax.random.fold_in(streams_of[15], 71), 0)
    tile_second = draw_tile_second(jax.random.fold_in(streams_of[15], 71), 0)
    left_stat = draw_left_stat(jax.random.fold_in(streams_of[15], 71), 0)
    right_stat = draw_right_stat(jax.random.fold_in(streams_of[15], 71), 0)
    left_basis = draw_left_basis(jax.random.fold_in(streams_of[15], 71), 0)
    right_basis = draw_right_basis(jax.random.fold_in(streams_of[15], 71), 0)
    vec_weight = draw_vec_weight(jax.random.fold_in(streams_of[15], 71), 0)
    vec_first = draw_vec_first(jax.random.fold_in(streams_of[15], 71), 0)
    vec_second = draw_vec_second(jax.random.fold_in(streams_of[15], 71), 0)
    return {"image_rows": image_rows, "text_rows": text_rows, "caption_lengths": caption_lengths, "concat_cot": concat_cot, "tile_slot": tile_slot, "tile_weight": tile_weight, "tile_first": tile_first, "tile_second": tile_second, "left_stat": left_stat, "right_stat": right_stat, "left_basis": left_basis, "right_basis": right_basis, "vec_weight": vec_weight, "vec_first": vec_first, "vec_second": vec_second}


BETA_ONE = 0.9
BETA_TWO = 0.95
EPSILON = 1e-08
RATE_MATRIX = 0.05
RATE_VECTOR = 0.6
DECAY = 0.01
MASKED = -1000000000.0
HIGH = lax.Precision.HIGHEST

@jax.custom_vjp
def low(v):
    return lax.optimization_barrier(v.astype(jnp.bfloat16)).astype(jnp.float32)

@jax.custom_vjp
def low_back(v):
    return v

def low_keep(v):
    return (low(v), None)

def low_pass(kept, grad):
    return (grad,)

def back_keep(v):
    return (v, None)

def back_low(kept, grad):
    return (low(grad),)
low.defvjp(low_keep, low_pass)
low_back.defvjp(back_keep, back_low)

def both_round(values):
    return low(low_back(values))

def layer_norm(values):
    center = values - lax.optimization_barrier(jnp.mean(values, -1, keepdims=True))
    return center * lax.rsqrt(lax.optimization_barrier(jnp.mean(center * center, -1, keepdims=True)) + 1e-05)

def product(left_rows, matrix):
    return jnp.einsum('srd,de->sre', left_rows, matrix, precision=HIGH)

def shapes_list():
    return ((D, D), (D, D), (D, D), (D, D), (D, FF), (FF, D), (D, D))

def matrix_of(tile_set, rows_count, cols_count):
    blocks = tile_set.reshape(rows_count // TILE_ORDER, cols_count // TILE_ORDER, TILE_ORDER, TILE_ORDER)
    return blocks.transpose(0, 2, 1, 3).reshape(rows_count, cols_count)

def tiles_of(matrix):
    rows_count, cols_count = matrix.shape
    blocks = matrix.reshape(rows_count // TILE_ORDER, TILE_ORDER, cols_count // TILE_ORDER, TILE_ORDER)
    return blocks.transpose(0, 2, 1, 3).reshape(-1, TILE_ORDER, TILE_ORDER)

def matrices_from(tile_set):
    result = []
    offset = 0
    for rows_count, cols_count in shapes_list():
        amount = rows_count // TILE_ORDER * (cols_count // TILE_ORDER)
        result.append(matrix_of(tile_set[offset:offset + amount], rows_count, cols_count))
        offset = offset + amount
    return tuple(result)

def tiles_from(matrices):
    return jnp.concatenate([tiles_of(matrix) for matrix in matrices], 0)

def split_vectors(vectors):
    after = 7 + FF // D
    return (vectors[0], vectors[1], vectors[2], vectors[3], vectors[4], vectors[5], vectors[6], vectors[7:after].reshape(FF), vectors[after], vectors[after + 1], vectors[after + 2], vectors[after + 3])

def tower_forward(matrices, vectors, rows, valid):
    w_query, w_key, w_value, w_out, w_up, w_down, w_proj = matrices
    gain_one, shift_one, bias_query, bias_value, bias_out, gain_two, shift_two, bias_up, bias_down, gain_three, shift_three, bias_proj = split_vectors(vectors)
    seq_count, length = (rows.shape[0], rows.shape[1])
    head_shape = (seq_count, length, HEADS, HEAD_DIM)
    input_one = low(layer_norm(rows) * gain_one + shift_one)
    queries = both_round(product(input_one, w_query) + bias_query).reshape(head_shape)
    keys_rows = both_round(product(input_one, w_key)).reshape(head_shape)
    values_rows = both_round(product(input_one, w_value) + bias_value).reshape(head_shape)
    penalty = jnp.where(valid[:, None, None, :], 0.0, MASKED)
    scores = jnp.einsum('sqhe,skhe->shqk', queries, keys_rows, precision=HIGH) * HEAD_DIM ** (-0.5)
    scores = low_back(scores + penalty)
    weights_soft = low(jax.nn.softmax(scores, -1))
    mixed_rows = both_round(jnp.einsum('shqk,skhe->sqhe', weights_soft, values_rows, precision=HIGH))
    mixed_rows = mixed_rows.reshape(seq_count, length, D)
    attended = rows + low_back(product(mixed_rows, w_out) + bias_out)
    input_two = low(layer_norm(attended) * gain_two + shift_two)
    upper_pre = low_back(product(input_two, w_up) + bias_up)
    hidden = low(jax.nn.gelu(upper_pre, approximate=False))
    final_rows = attended + low_back(product(hidden, w_down) + bias_down)
    input_three = low(layer_norm(final_rows) * gain_three + shift_three)
    return (product(input_three, w_proj) + bias_proj) * valid.astype(jnp.float32)[..., None]

def tower_run(matrices, vectors, rows, cotangent, valid):
    group_size = 8
    steps_count = rows.shape[0] // group_size
    row_groups = rows.reshape((steps_count, group_size) + rows.shape[1:])
    cot_groups = cotangent.reshape((steps_count, group_size) + cotangent.shape[1:])
    valid_groups = valid.reshape((steps_count, group_size) + valid.shape[1:])

    def one_group(running, inputs):
        rows_group, cot_group, valid_group = inputs

        def forward(params, values):
            return tower_forward(params[0], params[1], values, valid_group)
        outputs, pullback = jax.vjp(forward, (matrices, vectors), rows_group)
        grad_params, grad_rows = pullback(cot_group)
        return (jax.tree.map(jnp.add, running, grad_params), (outputs, grad_rows))
    empty_sums = jax.tree.map(jnp.zeros_like, (matrices, vectors))
    totals, (outputs, grad_rows_all) = lax.scan(one_group, empty_sums, (row_groups, cot_groups, valid_groups))
    return (outputs.reshape(rows.shape), grad_rows_all.reshape(rows.shape), totals)

def orthonormal(matrix):
    gram_matrix = jnp.einsum('nij,nik->njk', matrix, matrix, precision=HIGH)
    lower_factor = jnp.linalg.cholesky(gram_matrix)
    solved = jax.scipy.linalg.solve_triangular(lower_factor, jnp.swapaxes(matrix, 1, 2), lower=True)
    return jnp.swapaxes(solved, 1, 2)

def tile_update(grad_tiles, weight, first_moment, second_moment, left_side, right_side, left_rot, right_rot):
    left_new = BETA_TWO * left_side + (1.0 - BETA_TWO) * jnp.einsum('nij,nkj->nik', grad_tiles, grad_tiles, precision=HIGH)
    right_new = BETA_TWO * right_side + (1.0 - BETA_TWO) * jnp.einsum('nji,njk->nik', grad_tiles, grad_tiles, precision=HIGH)
    half_turn = jnp.einsum('nji,njk->nik', left_rot, grad_tiles, precision=HIGH)
    turned = jnp.einsum('nij,njk->nik', half_turn, right_rot, precision=HIGH)
    first_new = BETA_ONE * first_moment + (1.0 - BETA_ONE) * turned
    second_new = BETA_TWO * second_moment + (1.0 - BETA_TWO) * turned * turned
    scaled = first_new / (1.0 - BETA_ONE ** STEP) / (jnp.sqrt(second_new / (1.0 - BETA_TWO ** STEP)) + EPSILON)
    back_half = jnp.einsum('nij,njk->nik', left_rot, scaled, precision=HIGH)
    direction = jnp.einsum('nij,nkj->nik', back_half, right_rot, precision=HIGH)
    weight_new = weight - RATE_MATRIX * (direction + DECAY * weight)
    left_rot_new = orthonormal(jnp.einsum('nij,njk->nik', left_new, left_rot, precision=HIGH))
    right_rot_new = orthonormal(jnp.einsum('nij,njk->nik', right_new, right_rot, precision=HIGH))
    return (weight_new, first_new, second_new, left_new, right_new, left_rot_new, right_rot_new)

def vector_update(grad_rows, weight, first_moment, second_moment):
    first_new = BETA_ONE * first_moment + (1.0 - BETA_ONE) * grad_rows
    second_new = BETA_TWO * second_moment + (1.0 - BETA_TWO) * grad_rows * grad_rows
    step_size = first_new / (1.0 - BETA_ONE ** STEP) / (jnp.sqrt(second_new / (1.0 - BETA_TWO ** STEP)) + EPSILON)
    return (weight - RATE_VECTOR * step_size, first_new, second_new)

def tower_matrices(tiles_all, slot_index_list, tower):
    selected_slots = tiles_all[slot_index_list[tower * TILES_TOWER:(tower + 1) * TILES_TOWER]]
    return matrices_from(selected_slots)

def reference(image_rows, text_rows, caption_lengths, concat_cot, tile_slot, tile_weight, tile_first, tile_second, left_stat, right_stat, left_basis, right_basis, vec_weight, vec_first, vec_second):
    compute_tiles = low(tile_weight)
    compute_vectors = low(vec_weight)
    vec_tower = 11 + FF // D
    image_valid = jnp.ones((PAIRS, IMG), jnp.bool_)
    text_valid = jnp.arange(TXT, dtype=jnp.int32)[None, :] < caption_lengths[:, None]
    cot_float = concat_cot.astype(jnp.float32)
    image_out, image_back, image_params = tower_run(tower_matrices(compute_tiles, tile_slot, 0), compute_vectors[0:vec_tower], image_rows.astype(jnp.float32), cot_float[:, MMROWS:MMROWS + IMG], image_valid)
    text_out, text_back, text_params = tower_run(tower_matrices(compute_tiles, tile_slot, 1), compute_vectors[vec_tower:2 * vec_tower], text_rows.astype(jnp.float32), cot_float[:, MMROWS + IMG:], text_valid)
    learned = jnp.broadcast_to(compute_vectors[2 * vec_tower:2 * vec_tower + MMROWS][None], (PAIRS, MMROWS, D))
    concat = jnp.concatenate([learned, image_out, text_out], 1).astype(jnp.bfloat16)
    tile_grads = jnp.concatenate([tiles_from(image_params[0]), tiles_from(text_params[0])], 0)
    slot_grads = jnp.zeros(tile_weight.shape, jnp.float32).at[tile_slot].set(tile_grads)
    vec_grads = jnp.zeros(vec_weight.shape, jnp.float32)
    vec_grads = vec_grads.at[0:vec_tower].set(image_params[1])
    vec_grads = vec_grads.at[vec_tower:2 * vec_tower].set(text_params[1])
    vec_grads = vec_grads.at[2 * vec_tower:2 * vec_tower + MMROWS].set(lax.optimization_barrier(jnp.sum(cot_float[:, :MMROWS], 0)))
    tile_states = tile_update(slot_grads, tile_weight, tile_first, tile_second, left_stat, right_stat, left_basis, right_basis)
    vec_states = vector_update(vec_grads, vec_weight, vec_first, vec_second)
    return (concat, image_back.astype(jnp.bfloat16), text_back.astype(jnp.bfloat16), tile_states[0], tile_states[1], tile_states[2], tile_states[3], tile_states[4], tile_states[5], tile_states[6], vec_states[0], vec_states[1], vec_states[2])
```

```python
import functools
import heapq
import itertools

import jax
import jax.numpy as jnp
from jax import lax
from jax.experimental import pallas as pl
from jax.experimental.pallas import tpu as pltpu
from jax.sharding import PartitionSpec as P

BETA_ONE = 0.9
BETA_TWO = 0.95
EPSILON = 1e-08
RATE_MATRIX = 0.05
RATE_VECTOR = 0.6
DECAY = 0.01
STEP = 10
D = 768
FF = 3072
HEADS = 12
HEAD_DIM = 64
IMG = 197
TXT = 512
MMROWS = 2
T = 256
EXTRA = 16
VECS = 11 + FF // D
MASKED = -1000000000.0
NN = (((1,), (0,)), ((), ()))
NT = (((1,), (1,)), ((), ()))
TN = (((0,), (0,)), ((), ()))
KB = D // T
FB = FF // T
WIDE = 2 * T
SET = 2 * KB * WIDE // T


def mm(a, b, dims=NN):
    return lax.dot_general(a, b, dims, preferred_element_type=jnp.float32)


def rounded(v):
    return v.astype(jnp.bfloat16)


def stats(v):
    center = v - jnp.mean(v, -1, keepdims=True)
    inverse = lax.rsqrt(jnp.mean(center * center, -1, keepdims=True) + 1e-05)
    return center * inverse, inverse


def norm_back(grad, normed, inverse):
    return inverse * (
        grad
        - jnp.mean(grad, -1, keepdims=True)
        - normed * jnp.mean(grad * normed, -1, keepdims=True)
    )


def thirds(v):
    high = rounded(v)
    v = v - high.astype(jnp.float32)
    middle = rounded(v)
    return high, middle, rounded(v - middle.astype(jnp.float32))


def tower_body(is_text, rows, slots, slot_ref, length_ref, x_ref, cot_ref, copies, *rest):
    if is_text:
        zi_ref, _, cat_ref, dx_ref, grads = rest[:5]
        z_ref = None
    else:
        z_ref, dx_ref, grads = rest[:3]
        blank, blank_sem = rest[-2:]
        rest = rest[:-2]
    (wqkv, wo, wu, wd, wp, n1, n1t, qkv, qt, o, ot, a, n2, n2t, slope, h, ht, y, n3, n3t,
     cat, da, dqkv, logs, stage, vec_low, vec_all, bias_up, vec_out,
     wsem, stage_sem, vec_sem, vec_out_sem) = rest[5 if is_text else 3 :]
    dy = cat.at[pl.ds(0, rows)]
    dyb, dab, do, dot_, du = n3, n2, o, n3t, h
    first_tile = slot_ref.shape[0] // 2 if is_text else 0
    first_vec = VECS if is_text else 0
    real = TXT if is_text else IMG
    chunk = 64 if is_text else 16
    chunks = [(i * chunk, min((i + 1) * chunk, real)) for i in range(rows // chunk)]
    if is_text:
        length = length_ref[lax.axis_index("tower") * lax.axis_size("batch") + lax.axis_index("batch")]
    else:
        length = IMG
    tile_rows = slots * T

    def padded(value):
        short = chunk - value.shape[0]
        if short:
            value = jnp.concatenate([value, jnp.zeros((short, D), value.dtype)], 0)
        return value

    def x_of(c):
        return padded(x_ref[0, c[0] : c[1], :].astype(jnp.float32))

    def g_of(c):
        begin = c[0] + MMROWS + (IMG if is_text else 0)
        base = begin // 16 * 16
        end = min(-(-(begin + chunk) // 16) * 16, begin + c[1] - c[0])
        value = cot_ref[0, base:end, :].astype(jnp.float32)
        return padded(value[begin - base : begin - base + c[1] - c[0]])

    def at_slot(ref, slot):
        return ref.at[slot // slots, pl.ds(pl.multiple_of(slot % slots * T, T), T), :]

    extra = pl.ds(tile_rows, EXTRA)
    vec_count = VECS + MMROWS if is_text else VECS
    for i in range(vec_count):
        pltpu.make_async_copy(copies.at[first_vec + i, extra], vec_low.at[i], vec_sem).start()
    mats = [(wqkv, 0), (wqkv, D), (wqkv, 2 * D), (wo, 0), (wu, 0), (wd, 0), (wp, 0)]
    shapes = [(KB, KB)] * 4 + [(KB, FB), (FB, KB), (KB, KB)]
    starts = [0]
    for rb, cb in shapes:
        starts.append(starts[-1] + rb * cb)

    def load(which, sem):
        ref, shift = mats[which]
        rb, cb = shapes[which]

        def one(i, _):
            slot = slot_ref[first_tile + starts[which] + i]
            r, c = i // cb, i % cb
            pltpu.make_async_copy(
                at_slot(copies, slot),
                ref.at[pl.ds(pl.multiple_of(r * T, T), T), pl.ds(pl.multiple_of(shift + c * T, T), T)],
                wsem.at[sem],
            ).start()
            return 0

        lax.fori_loop(0, rb * cb, one, 0)

    def drain(ref, sem):
        pltpu.make_async_copy(ref, ref, sem).wait()

    for which, sem in enumerate((0, 0, 0, 1, 2, 3, 4)):
        load(which, sem)
    if not is_text:
        blank[...] = jnp.zeros(blank.shape, blank.dtype)

        def clear(i, _):
            pltpu.make_async_copy(blank, grads.at[i], blank_sem).start()
            return 0

        lax.fori_loop(0, grads.shape[0], clear, 0)

    def put(place, tiles):
        for n, (_, value) in enumerate(tiles):
            stage[place, n] = rounded(value)
        for n, (tile, _) in enumerate(tiles):
            slot = slot_ref[first_tile + tile]
            pltpu.make_async_copy(stage.at[place, n], at_slot(grads, slot), stage_sem.at[place]).start()

    def free(place, count):
        drain(stage.at[place, pl.ds(0, count)], stage_sem.at[place])

    def square(which, product):
        return [
            (starts[which] + r * KB + k, product[r * T : (r + 1) * T, k * T : (k + 1) * T])
            for r in range(KB)
            for k in range(KB)
        ]

    drain(vec_low.at[pl.ds(0, vec_count)], vec_sem)
    for i in range(vec_count):
        line = jnp.concatenate([vec_low[i, k : k + 1, :] for k in range(KB)], 1).astype(jnp.float32)
        vec_all[i : i + 1, :] = line
        if 7 <= i < 7 + FF // D:
            bias_up[:, (i - 7) * D : (i - 6) * D] = line

    def vec(i):
        return vec_all[i : i + 1, :]

    def vec_grad(i, line):
        line = rounded(line)
        parts = [line[:, k * T : (k + 1) * T] for k in range(KB)]
        parts.append(jnp.zeros((EXTRA - KB, T), jnp.bfloat16))
        vec_out[i] = jnp.concatenate(parts, 0)
        pltpu.make_async_copy(vec_out.at[i], grads.at[first_vec + i, extra], vec_out_sem).start()

    for c in chunks:
        normed, _ = stats(x_of(c))
        n1[c[0] : c[0] + chunk, :] = rounded(normed * vec(0) + vec(1))
    n1t[...] = n1[...].T
    drain(wqkv, wsem.at[0])
    scale = HEAD_DIM ** (-0.5)
    qkv[:, :D] = rounded((mm(n1[...], wqkv[:, :D]) + vec(2))) * jnp.asarray(scale, jnp.bfloat16)
    qkv[:, D : 2 * D] = rounded(mm(n1[...], wqkv[:, D : 2 * D]))
    qkv[:, 2 * D :] = rounded(mm(n1[...], wqkv[:, 2 * D :]) + vec(3))
    qt[...] = qkv[:, :D].T
    lane = lax.broadcasted_iota(jnp.int32, (rows, 2 * HEAD_DIM), 1)
    keys = lax.broadcasted_iota(jnp.int32, (rows, 2 * HEAD_DIM), 0)
    penalty = jnp.where(keys < length, 0.0, MASKED).astype(jnp.bfloat16)
    one = jnp.ones((rows, 2 * HEAD_DIM), jnp.bfloat16)
    zero = jnp.zeros((rows, 2 * HEAD_DIM), jnp.bfloat16)

    def pair_cols(p, base):
        return pl.ds(pl.multiple_of(base + p * 2 * HEAD_DIM, 2 * HEAD_DIM), 2 * HEAD_DIM)

    def beside(side, value, others):
        base = HEAD_DIM * (1 - side)
        result = zero
        for n, other in enumerate(others):
            result = jnp.where(lane == base + n, other, result)
        return jnp.where((lane < HEAD_DIM) if side == 0 else (lane >= HEAD_DIM), value, result)

    def attend(p, _):
        q = qkv[:, pair_cols(p, 0)]
        k = qkv[:, pair_cols(p, D)]
        v = qkv[:, pair_cols(p, 2 * D)]
        outs = []
        for side in range(2):
            s = mm(beside(side, q, [one]), beside(side, k, [penalty]), NT)
            top = jnp.max(s, -1, keepdims=True)
            s = jnp.exp(s - top)
            total = jnp.sum(s, -1, keepdims=True)
            logs[2 * p + side] = jnp.broadcast_to(top + jnp.log(total), (rows, 128))
            outs.append(mm(rounded(s * (1.0 / total)), v))
        o[:, pair_cols(p, 0)] = rounded(jnp.where(lane < HEAD_DIM, outs[0], outs[1]))
        return 0

    lax.fori_loop(0, HEADS // 2, attend, 0)
    ot[...] = o[...].T
    drain(wo, wsem.at[1])
    a[...] = mm(o[...], wo[...])
    for c in chunks:
        at = slice(c[0], c[0] + chunk)
        value = x_of(c) + (a[at, :] + vec(4))
        a[at, :] = value
        normed, _ = stats(value)
        n2[at, :] = rounded(normed * vec(5) + vec(6))
    n2t[...] = n2[...].T
    drain(wu, wsem.at[2])

    def up(i, _):
        cols = pl.ds(pl.multiple_of(i * WIDE, WIDE), WIDE)
        u = mm(n2[...], wu[:, cols]) + bias_up[:, cols]
        cumulative = 0.5 * (1.0 + lax.erf(u * 0.7071067811865476))
        hidden = rounded(u * cumulative)
        slope[:, cols] = cumulative + u * (jnp.exp(-0.5 * u * u) * 0.3989422804014327)
        h[:, cols] = hidden
        ht[cols, :] = hidden.T
        return 0

    lax.fori_loop(0, FF // WIDE, up, 0)
    drain(wd, wsem.at[3])
    y[...] = mm(h[...], wd[...])
    for c in chunks:
        at = slice(c[0], c[0] + chunk)
        value = a[at, :] + (y[at, :] + vec(11))
        y[at, :] = value
        normed, _ = stats(value)
        n3[at, :] = rounded(normed * vec(12) + vec(13))
    n3t[...] = n3[...].T
    drain(wp, wsem.at[4])
    keep = lax.broadcasted_iota(jnp.int32, (rows, 1), 0) < length
    z = jnp.where(keep, mm(n3[...], wp[...]) + vec(14), 0.0)
    if is_text:
        begin = MMROWS + IMG
        cat[:MMROWS, :] = vec_all[VECS : VECS + MMROWS, :]
        cat[MMROWS:begin, :] = zi_ref[0].astype(jnp.float32)
        cat[begin : begin + TXT, :] = z
        cat_ref[0] = rounded(cat[...])
    else:
        even = IMG // 16 * 16
        z_ref[0, :even, :] = rounded(z[:even])
        z_ref[0, even:IMG, :] = rounded(z[even:IMG])

    if not is_text:
        drain(grads, blank_sem)
    zeros = jnp.zeros((1, D), jnp.float32)
    total = zeros
    for c in chunks:
        at = slice(c[0], c[0] + chunk)
        g = jnp.where(keep[at, :], g_of(c), 0.0)
        total = total + jnp.sum(g, 0, keepdims=True)
        dyb[at, :] = rounded(g)
    vec_grad(14, total)
    put(1, square(6, mm(n3t[...], dyb[...])))
    dy[...] = mm(dyb[...], wp[...], NT)
    gain, shift, bias = zeros, zeros, zeros
    for c in chunks:
        at = slice(c[0], c[0] + chunk)
        normed, inverse = stats(y[at, :])
        g = dy[at, :]
        gain = gain + jnp.sum(g * normed, 0, keepdims=True)
        shift = shift + jnp.sum(g, 0, keepdims=True)
        g = norm_back(g * vec(12), normed, inverse)
        dy[at, :] = g
        low = rounded(g)
        dyb[at, :] = low
        bias = bias + jnp.sum(low.astype(jnp.float32), 0, keepdims=True)
    vec_grad(12, gain)
    vec_grad(13, shift)
    vec_grad(11, bias)

    def down(i, _):
        place = i % 2
        pl.when(i == 1)(functools.partial(free, 1, KB * KB))
        pl.when(i >= 2)(functools.partial(free, place, SET))
        cols = pl.ds(pl.multiple_of(i * WIDE, WIDE), WIDE)
        low = rounded(mm(dyb[...], wd[cols, :], NT) * slope[:, cols])
        du[:, cols] = low
        bias_up[:, cols] = jnp.sum(low.astype(jnp.float32), 0, keepdims=True)
        down_grad = mm(ht[cols, :], dyb[...])
        up_grad = mm(n2t[...], low)
        tiles = []
        for w in range(WIDE // T):
            band = slice(w * T, (w + 1) * T)
            number = i * (WIDE // T) + w
            for k in range(KB):
                other = slice(k * T, (k + 1) * T)
                tiles.append((starts[5] + number * KB + k, down_grad[band, other]))
                tiles.append((starts[4] + k * FB + number, up_grad[other, band]))
        put(place, tiles)
        return 0

    lax.fori_loop(0, FF // WIDE, down, 0)
    for i in range(FF // D):
        vec_grad(7 + i, bias_up[:, i * D : (i + 1) * D])
    da[...] = mm(du[...], wu[...], NT)
    gain, shift, bias = zeros, zeros, zeros
    for c in chunks:
        at = slice(c[0], c[0] + chunk)
        normed, inverse = stats(a[at, :])
        g = da[at, :]
        gain = gain + jnp.sum(g * normed, 0, keepdims=True)
        shift = shift + jnp.sum(g, 0, keepdims=True)
        g = dy[at, :] + norm_back(g * vec(5), normed, inverse)
        da[at, :] = g
        low = rounded(g)
        dab[at, :] = low
        bias = bias + jnp.sum(low.astype(jnp.float32), 0, keepdims=True)
    vec_grad(5, gain)
    vec_grad(6, shift)
    vec_grad(4, bias)
    dout = mm(dab[...], wo[...], NT)
    free(0, SET)
    put(0, square(3, mm(ot[...], dab[...])))
    low = rounded(dout)
    y[...] = low.astype(jnp.float32) * o[...].astype(jnp.float32)
    do[...] = low
    dot_[...] = low.T

    def attend_back(p, _):
        q = qkv[:, pair_cols(p, 0)]
        k = qkv[:, pair_cols(p, D)]
        v = qkv[:, pair_cols(p, 2 * D)]
        g = do[:, pair_cols(p, 0)]
        each = y[:, pair_cols(p, 0)]
        dqs, dks, dvs = [], [], []
        for side in range(2):
            half = pl.ds(pl.multiple_of((2 * p + side) * HEAD_DIM, HEAD_DIM), HEAD_DIM)
            mine = (lane < HEAD_DIM) if side == 0 else (lane >= HEAD_DIM)
            minus = [-one] * 3
            w = jnp.exp(
                mm(
                    beside(side, q, [one, *thirds(logs[2 * p + side])]),
                    beside(side, k, [penalty, *minus]),
                    NT,
                )
            )
            dvs.append(mm(dot_[half, :], rounded(w)))
            c = jnp.sum(jnp.where(mine, each, 0.0), -1, keepdims=True)
            dw = mm(
                beside(side, g, thirds(jnp.broadcast_to(c, (rows, 2 * HEAD_DIM)))),
                beside(side, v, minus),
                NT,
            )
            ds = rounded(w * dw)
            dqs.append(mm(ds, k))
            dks.append(mm(qt[half, :], ds))
        dqkv[:, pair_cols(p, 0)] = rounded(jnp.where(lane < HEAD_DIM, dqs[0], dqs[1]) * scale)
        dqkv[:, pair_cols(p, D)] = rounded(jnp.concatenate(dks, 0).T)
        dqkv[:, pair_cols(p, 2 * D)] = rounded(jnp.concatenate(dvs, 0).T)
        return 0

    lax.fori_loop(0, HEADS // 2, attend_back, 0)
    for m, number in ((0, 2), (2, 3)):
        vec_grad(number, jnp.sum(dqkv[:, m * D : (m + 1) * D].astype(jnp.float32), 0, keepdims=True))
    for m in range(3):
        free((1 + m) % 2, SET if m == 0 else KB * KB)
        put((1 + m) % 2, square(m, mm(n1t[...], dqkv[:, m * D : (m + 1) * D])))
    dy[...] = mm(dqkv[...], wqkv[...], NT)
    gain, shift = zeros, zeros
    for c in chunks:
        at = slice(c[0], c[0] + chunk)
        normed, inverse = stats(x_of(c))
        g = dy[at, :]
        gain = gain + jnp.sum(g * normed, 0, keepdims=True)
        shift = shift + jnp.sum(g, 0, keepdims=True)
        low = rounded(da[at, :] + norm_back(g * vec(0), normed, inverse))
        dx_ref[0, c[0] : c[1], :] = low[: c[1] - c[0]]
    vec_grad(0, gain)
    vec_grad(1, shift)
    if is_text:
        learned = cot_ref[0, :16, :].astype(jnp.float32)
        for i in range(MMROWS):
            vec_grad(VECS + i, learned[i : i + 1])
    free(0, KB * KB)
    free(1, KB * KB)
    drain(vec_out.at[pl.ds(0, vec_count)], vec_out_sem)


def tower(is_text, slots, tile_slot, lengths, x, cot, copies, before=()):
    bf, f32 = jnp.bfloat16, jnp.float32
    smem = pl.BlockSpec(memory_space=pltpu.SMEM)
    vmem = pl.BlockSpec(memory_space=pltpu.VMEM)
    hbm = pl.BlockSpec(memory_space=pl.ANY)
    dma = pltpu.SemaphoreType.DMA
    rows = -(-x.shape[1] // 16) * 16
    outs = [
        jax.ShapeDtypeStruct(cot.shape if is_text else x.shape, bf),
        jax.ShapeDtypeStruct(x.shape, bf),
        jax.ShapeDtypeStruct(copies.shape, bf),
    ]
    scratch = [
        pltpu.VMEM((D, 3 * D), bf), pltpu.VMEM((D, D), bf), pltpu.VMEM((D, FF), bf),
        pltpu.VMEM((FF, D), bf), pltpu.VMEM((D, D), bf),
        pltpu.VMEM((rows, D), bf), pltpu.VMEM((D, rows), bf),
        pltpu.VMEM((rows, 3 * D), bf), pltpu.VMEM((D, rows), bf),
        pltpu.VMEM((rows, D), bf), pltpu.VMEM((D, rows), bf),
        pltpu.VMEM((rows, D), f32),
        pltpu.VMEM((rows, D), bf), pltpu.VMEM((D, rows), bf),
        pltpu.VMEM((rows, FF), f32),
        pltpu.VMEM((rows, FF), bf), pltpu.VMEM((FF, rows), bf),
        pltpu.VMEM((rows, D), f32),
        pltpu.VMEM((rows, D), bf), pltpu.VMEM((D, rows), bf),
        pltpu.VMEM((cot.shape[1] if is_text else rows, D), f32),
        pltpu.VMEM((rows, D), f32),
        pltpu.VMEM((rows, 3 * D), bf),
        pltpu.VMEM((HEADS, rows, 128), f32),
        pltpu.VMEM((2, SET, T, T), bf),
        pltpu.VMEM((VECS + MMROWS, EXTRA, T), bf), pltpu.VMEM((VECS + MMROWS, D), f32),
        pltpu.VMEM((1, FF), f32), pltpu.VMEM((VECS + MMROWS, EXTRA, T), bf),
        dma((5,)), dma((2,)), dma, dma,
    ]
    if not is_text:
        scratch += [pltpu.VMEM((slots * T + EXTRA, T), bf), dma]
    return pl.pallas_call(
        functools.partial(tower_body, is_text, rows, slots),
        in_specs=[smem, smem, vmem, vmem, hbm] + ([vmem, hbm] if is_text else []),
        out_specs=[vmem, vmem, hbm],
        out_shape=outs,
        scratch_shapes=scratch,
        input_output_aliases={6: 2} if is_text else {},
        compiler_params=pltpu.CompilerParams(vmem_limit_bytes=63 << 20),
        name="text_tower" if is_text else "image_tower",
    )(tile_slot, lengths, x, cot, copies, *before)


def split(x):
    hi = x.astype(jnp.bfloat16)
    lo = (x - hi.astype(jnp.float32)).astype(jnp.bfloat16)
    return hi, lo


def dot(a, b, dims):
    return lax.dot_general(a, b, dims, preferred_element_type=jnp.float32)


def mm3(a, b, dims):
    return dot(a[0], b[0], dims) + (dot(a[0], b[1], dims) + dot(a[1], b[0], dims))


def adam_step(first, second):
    return (
        first
        / (1.0 - BETA_ONE**STEP)
        / (jnp.sqrt(second / (1.0 - BETA_TWO**STEP)) + EPSILON)
    )


def refine(i, slots, g_ref, w_ref, m1_ref, m2_ref, ls_ref, rs_ref, lb_ref, rb_ref,
           wn_ref, m1n_ref, m2n_ref, lsn_ref, rsn_ref, work):
    e = split(g_ref[...])
    ql = split(lb_ref[0])
    qr = split(rb_ref[0])
    left = BETA_TWO * ls_ref[0] + (1.0 - BETA_TWO) * mm3(e, e, NT)
    right = BETA_TWO * rs_ref[0] + (1.0 - BETA_TWO) * mm3(e, e, TN)
    lsn_ref[0] = left
    rsn_ref[0] = right
    turned = mm3(split(mm3(ql, e, TN)), qr, NN)
    first = BETA_ONE * m1_ref[0] + (1.0 - BETA_ONE) * turned
    second = BETA_TWO * m2_ref[0] + (1.0 - BETA_TWO) * turned * turned
    m1n_ref[0] = first
    m2n_ref[0] = second
    direction = mm3(split(mm3(ql, split(adam_step(first, second)), NN)), qr, NT)
    w = w_ref[0]
    wn_ref[0] = w - RATE_MATRIX * (direction + DECAY * w)
    for side, (basis, stat) in enumerate(((ql, left), (qr, right))):
        y = mm3(basis, split(stat), TN)
        y = y * lax.rsqrt(jnp.sum(y * y, axis=1, keepdims=True))
        work[side * slots + i, :, T:] = y
        y = split(y)
        work[side * slots + i, :, :T] = mm3(y, y, NT)


B = 64
GROUP = 8
ABREAST = 4


def eliminate(count, diag):
    shape = (GROUP, 2 * B)
    subs = lax.broadcasted_iota(jnp.int32, shape, 0)
    for jg in range(B // GROUP):
        top = slice(jg * GROUP, jg * GROUP + GROUP)
        tops = [diag[m, top, :] for m in range(count)]
        for jj in range(0, GROUP, 2):
            j = jg * GROUP + jj
            for m in range(count):
                tile = tops[m]
                first = jnp.broadcast_to(tile[:, j : j + 1], shape)
                second = jnp.broadcast_to(tile[:, j + 1 : j + 2], shape)
                p00, p01, p11 = first[jj : jj + 1], second[jj : jj + 1], second[jj + 1 : jj + 2]
                r0, r1 = tile[jj : jj + 1], tile[jj + 1 : jj + 2]
                inverse = 1.0 / (p00 * p11 - p01 * p01)
                cross = p01 * inverse
                t0 = (p11 * inverse) * r0 - cross * r1
                t1 = (p00 * inverse) * r1 - cross * r0
                lower = tile - first * t0 - second * t1
                tops[m] = jnp.where(
                    subs > jj + 1, lower, jnp.where(subs == jj + 1, tile - (p01 / p00) * r0, tile)
                )
                if jg < B // GROUP - 1:
                    rest = diag[m, jg * GROUP + GROUP :, :]
                    diag[m, jg * GROUP + GROUP :, :] = (
                        rest - rest[:, j : j + 1] * t0 - rest[:, j + 1 : j + 2] * t1
                    )
        for m in range(count):
            diag[m, top, :] = tops[m]


def orthonormal(count, work, diag):
    row = lax.broadcasted_iota(jnp.int32, (B, 2 * B), 0)
    lane = lax.broadcasted_iota(jnp.int32, (B, 2 * B), 1)
    def load(k):
        low = k * B
        edge = low // (2 * B) * 2 * B
        for m in range(count):
            block = work[m, low : low + B, edge : edge + 2 * B]
            if low % (2 * B):
                block = pltpu.roll(block, B, 1)
            diag[m] = jnp.where(lane < B, block, jnp.where(lane == row + B, 1.0, 0.0))

    def products(k):
        low = k * B
        edge = low // (2 * B) * 2 * B

        def apply(step, _):
            for n in range(ABREAST):
                m = step * ABREAST + n
                d = diag[m]
                pivots = jnp.sum(jnp.where(lane == row, d, 0.0), axis=1, keepdims=True)
                high, rest = split(d[:, B:] * lax.rsqrt(pivots))
                inverse = jnp.concatenate([high, rest, high], 1)
                high, rest = split(work[m, low : low + B, edge:])
                new = dot(inverse, jnp.concatenate([high, high, rest], 0), NN)
                work[m, low : low + B, edge:] = new
                if low + B < T:
                    high, rest = split(new)
                    after = low + B - edge
                    begin = (low + B) // (2 * B) * 2 * B
                    left = jnp.concatenate([high, rest, high], 0)[:, after : T - edge]
                    right = jnp.concatenate([high, high, rest], 0)[:, begin - edge :]
                    work[m, low + B :, begin:] = work[m, low + B :, begin:] - dot(left, right, TN)
            return 0

        lax.fori_loop(0, count // ABREAST, apply, 0)

    def block(k, _):
        for which in range(T // B):
            pl.when(k == which)(functools.partial(load, which))
        eliminate(count, diag)
        for which in range(T // B):
            pl.when(k == which)(functools.partial(products, which))
        return 0

    lax.fori_loop(0, T // B, block, 0)


def optimizer_body(slots, g_ref, vg_ref, w_ref, m1_ref, m2_ref, ls_ref, rs_ref, lb_ref, rb_ref, vw_ref, v1_ref, v2_ref,
                   wn_ref, m1n_ref, m2n_ref, lsn_ref, rsn_ref, lbn_ref, rbn_ref, vwn_ref, v1n_ref, v2n_ref, work, diag):
    i = pl.program_id(0)

    @pl.when(i == 0)
    def _():
        for k in range(vw_ref.shape[1] // T):
            cols = slice(k * T, (k + 1) * T)
            g = vg_ref[k : k + 1, :]
            first = BETA_ONE * v1_ref[:, cols] + (1.0 - BETA_ONE) * g
            second = BETA_TWO * v2_ref[:, cols] + (1.0 - BETA_TWO) * g * g
            v1n_ref[:, cols] = first
            v2n_ref[:, cols] = second
            vwn_ref[:, cols] = vw_ref[:, cols] - RATE_VECTOR * adam_step(first, second)

    refine(i, slots, g_ref, w_ref, m1_ref, m2_ref, ls_ref, rs_ref, lb_ref, rb_ref,
           wn_ref, m1n_ref, m2n_ref, lsn_ref, rsn_ref, work)

    @pl.when(i == slots - 1)
    def _():
        orthonormal(work.shape[0], work, diag)

        def finish(m, _):
            lbn_ref[m] = work[m, :, T:].T
            rbn_ref[m] = work[slots + m, :, T:].T
            return 0

        lax.fori_loop(0, slots, finish, 0)


def optimizer(g, w, m1, m2, ls, rs, lb, rb, vw, v1, v2):
    slots = w.shape[0]
    count = -(-2 * slots // ABREAST) * ABREAST
    one = pl.BlockSpec((1, T, T), lambda i: (i, 0, 0))
    every = pl.BlockSpec((slots, T, T), lambda i: (0, 0, 0))
    line = pl.BlockSpec(vw.shape, lambda i: (0, 0))
    f32 = jnp.float32
    return pl.pallas_call(
        functools.partial(optimizer_body, slots),
        grid=(slots,),
        in_specs=[
            pl.BlockSpec((T, T), lambda i: (i, 0)),
            pl.BlockSpec((EXTRA, T), lambda i: (slots * T // EXTRA, 0)),
        ]
        + [one] * 7
        + [line] * 3,
        out_specs=[one] * 5 + [every] * 2 + [line] * 3,
        out_shape=[jax.ShapeDtypeStruct(w.shape, f32)] * 7 + [jax.ShapeDtypeStruct(vw.shape, f32)] * 3,
        scratch_shapes=[
            pltpu.VMEM((count, T, 2 * T), f32),
            pltpu.VMEM((count, B, 2 * B), f32),
        ],
        compiler_params=pltpu.CompilerParams(vmem_limit_bytes=60 << 20),
        name="optimizer",
    )(g, g, w, m1, m2, ls, rs, lb, rb, vw, v1, v2)


ORDERS = ("xzy", "yzx", "zxy", "zyx")


def part_rows(slots):
    quarter = slots * T // 4
    sizes = [quarter, quarter, quarter, quarter + EXTRA]
    return [(sum(sizes[:i]), sizes[i]) for i in range(4)]


def last_step(order, key):
    away = {"z": key[0], "x": key[1], "y": key[2]}
    steps = [i for i in range(3) if away[order[i]]]
    return steps[-1] if steps else -1


def plan_of(depth):
    cells = list(itertools.product(range(depth), range(2), range(2)))
    queues, free, events, arrived = {}, {}, [], {}
    ticket = itertools.count()

    def onward(cell, part, source, now):
        order = ORDERS[part]
        key = (source[0] - cell[0], source[1] ^ cell[1], source[2] ^ cell[2])
        step = last_step(order, key)
        for i in range(3):
            z, x, y = cell
            if order[i] == "z":
                if i > step:
                    ways = (1, -1)
                elif i == step:
                    ways = (1,) if key[0] < 0 else (-1,)
                else:
                    ways = ()
                targets = [(z + w, x, y) for w in ways if 0 <= z + w < depth]
            elif i > step:
                targets = [(z, 1 - x, y) if order[i] == "x" else (z, x, 1 - y)]
            else:
                targets = []
            for target in targets:
                heapq.heappush(queues.setdefault((cell, target), []), (now, next(ticket), part, source))
                heapq.heappush(events, (now, next(ticket), 0, (cell, target)))

    for cell in cells:
        for part in range(4):
            onward(cell, part, cell, 0.0)
    while events:
        now, _, kind, what = heapq.heappop(events)
        if kind == 0:
            if queues[what] and free.get(what, 0.0) <= now:
                _, _, part, source = heapq.heappop(queues[what])
                free[what] = now + 2.0
                heapq.heappush(events, (now + 2.0, next(ticket), 0, what))
                heapq.heappush(events, (now + 2.5, next(ticket), 1, (what[1], part, source)))
        else:
            cell, part, source = what
            key = (part, source[0] - cell[0], source[1] ^ cell[1], source[2] ^ cell[2])
            arrived.setdefault(key, []).append(now)
            onward(cell, part, source, now)
    times = {k: sum(v) / len(v) for k, v in arrived.items()}
    fixed = {}

    def time_of(key):
        if key not in fixed:
            part, dz, dx, dy = key
            step = last_step(ORDERS[part], key[1:])
            if step < 0:
                return 0.0
            dim = ORDERS[part][step]
            if dim == "z":
                parent = (part, dz - (1 if dz > 0 else -1), dx, dy)
            else:
                parent = (part, dz, 0 if dim == "x" else dx, 0 if dim == "y" else dy)
            fixed[key] = max(times[key], time_of(parent) + 0.01)
        return fixed[key]

    return sorted(times, key=lambda k: (time_of(k), k))


class Place:
    def __init__(self, depth):
        tower = lax.axis_index("tower")
        self.depth = depth
        self.core = tower % 2
        self.x = tower // 2 % 2
        self.z = tower // 4
        self.y = lax.axis_index("batch")

    def at(self, dz=0, dx=0, dy=0):
        return (
            self.z + dz,
            1 - self.x if dx else self.x,
            1 - self.y if dy else self.y,
        )

    def device(self, cell, other=False):
        core = 1 - self.core if other else self.core
        return ((cell[0] * 2 + cell[1]) * 2 + core, cell[2])

    def block(self, cell, other=False):
        core = 1 - self.core if other else self.core
        return ((cell[0] * 2 + cell[1]) * 2 + core) * 2 + cell[2]

    def spot(self, cell):
        return (cell[0] * 2 + cell[1]) * 2 + cell[2]

    def inside(self, dz):
        if dz == 0:
            return None
        return self.z + dz < self.depth if dz > 0 else self.z + dz >= 0

    def meet(self):
        barrier = pltpu.get_barrier_semaphore()

        def greet(device):
            pl.semaphore_signal(barrier, inc=1, device_id=device, device_id_type=pl.DeviceIdType.MESH)

        greet(self.device(self.at(), True))
        greet(self.device(self.at(dx=1)))
        greet(self.device(self.at(dy=1)))
        for way in (1, -1):
            pl.when(self.inside(way))(functools.partial(greet, self.device(self.at(dz=way))))
        low = (self.z > 0).astype(jnp.int32)
        high = (self.z < self.depth - 1).astype(jnp.int32)
        pl.semaphore_wait(barrier, 3 + low + high)


def guarded(conditions, action):
    conditions = [c for c in conditions if c is not None]
    if not conditions:
        action()
    else:
        both = conditions[0]
        for c in conditions[1:]:
            both = jnp.logical_and(both, c)
        pl.when(both)(action)


def remote(src, dst, send, recv, device):
    return pltpu.make_async_remote_copy(
        src_ref=src, dst_ref=dst, send_sem=send, recv_sem=recv,
        device_id=device, device_id_type=pl.DeviceIdType.MESH,
    )


def drain(ref, sem):
    pltpu.make_async_copy(ref, ref, sem).wait()


def gather_body(
    depth, parts, plan, tiles_ref, vec_ref, out_ref, wide, own_ref, wide_sem, own_sem, z_sem, flat_sem, twin_sem, recv_sem
):
    slots = tiles_ref.shape[0]
    for slot in range(slots):
        pltpu.make_async_copy(tiles_ref.at[slot], wide.at[slot], wide_sem.at[slot]).start()
    here = Place(depth)
    here.meet()
    line = vec_ref[...].astype(jnp.bfloat16)
    pieces = [line[:, k * T : (k + 1) * T] for k in range(line.shape[1] // T)]
    pieces.append(jnp.zeros((EXTRA - len(pieces), T), jnp.bfloat16))
    own_ref[slots * T :, :] = jnp.concatenate(pieces, 0)
    for slot in range(slots):
        drain(wide.at[slot], wide_sem.at[slot])
        own_ref[slot * T : (slot + 1) * T, :] = wide[slot].astype(jnp.bfloat16)
    mine = pltpu.make_async_copy(own_ref, out_ref.at[here.block(here.at())], own_sem)
    mine.start()
    waits = []

    def handle(part, key):
        start, size = parts[part]
        rows = pl.ds(start, size)
        order = ORDERS[part]
        step = last_step(order, key)
        cell = here.at(*key)
        present = here.inside(key[0])
        block = here.block(cell)
        spot = here.spot(cell)
        place = out_ref.at[block, rows]
        source = own_ref.at[rows] if step < 0 else place

        def arrive():
            if step >= 0:
                drain(place, recv_sem.at[part, spot])

        guarded([present], arrive)
        for i in range(3):
            dim = order[i]
            if dim == "z":
                ways = (1, -1) if i > step else ()
                if i == step:
                    ways = (1,) if key[0] < 0 else (-1,)
                for way in ways:
                    sem = z_sem.at[part, spot, 0 if way > 0 else 1]
                    copy = remote(source, place, sem, recv_sem.at[part, spot], here.device(here.at(dz=way)))
                    conditions = [present, here.inside(way)]
                    guarded(conditions, copy.start)
                    waits.append((conditions, copy.wait_send))
            elif i > step:
                target = here.at(dx=1) if dim == "x" else here.at(dy=1)
                guarded(
                    [present],
                    remote(
                        source, place, flat_sem.at[part, 0 if dim == "x" else 1],
                        recv_sem.at[part, spot], here.device(target),
                    ).start,
                )
        guarded(
            [present],
            remote(source, place, twin_sem.at[0], twin_sem.at[1], here.device(here.at(), True)).start,
        )

    for part in range(4):
        handle(part, (0, 0, 0))
    for part, *key in plan:
        handle(part, tuple(key))
    for conditions, action in waits:
        guarded(conditions, action)
    for part in range(4):
        rows = pl.ds(*parts[part])
        sent = 1
        for dim in ORDERS[part]:
            if dim != "z":
                drain(out_ref.at[pl.ds(0, sent), rows], flat_sem.at[part, 0 if dim == "x" else 1])
            sent *= depth if dim == "z" else 2
    mine.wait()
    half = pl.ds(0, 4 * depth)
    drain(out_ref.at[half], twin_sem.at[0])
    drain(out_ref.at[half], twin_sem.at[1])


def gather(depth, tiles, vec):
    slots = tiles.shape[0]
    parts = part_rows(slots)
    rows = slots * T + EXTRA
    hbm = pl.BlockSpec(memory_space=pl.ANY)
    dma = pltpu.SemaphoreType.DMA
    return pl.pallas_call(
        functools.partial(gather_body, depth, parts, plan_of(depth)),
        in_specs=[hbm, pl.BlockSpec(memory_space=pltpu.VMEM)],
        out_specs=hbm,
        out_shape=jax.ShapeDtypeStruct((8 * depth, rows, T), jnp.bfloat16),
        scratch_shapes=[
            pltpu.VMEM(tiles.shape, jnp.float32),
            pltpu.VMEM((rows, T), jnp.bfloat16),
            dma((slots,)),
            dma,
            dma((4, 4 * depth, 2)),
            dma((4, 2)),
            dma((2,)),
            dma((4, 4 * depth)),
        ],
        compiler_params=pltpu.CompilerParams(
            collective_id=0, has_side_effects=True, vmem_limit_bytes=60 << 20
        ),
        name="gather",
    )(tiles, vec)


def add_rows(size, target, start, sources):
    def piece(at, count):
        total = sources[0][pl.ds(at, count), :].astype(jnp.float32)
        for source in sources[1:]:
            total = total + source[pl.ds(at, count), :].astype(jnp.float32)
        target[pl.ds(start + at, count), :] = total.astype(target.dtype)

    whole = size // 128

    def body(i, _):
        piece(pl.multiple_of(i * 128, 128), 128)
        return 0

    lax.fori_loop(0, whole, body, 0)
    if size % 128:
        piece(whole * 128, size % 128)


def reduce_body(depth, parts, plan, grads_ref, out_ref, acc, twin, flat0, flat1, line, *sems):
    load_sem, twin_send, twin_recv, flat0_send, flat0_recv, flat1_send, flat1_recv, line_send, line_recv = sems
    here = Place(depth)
    keys = [(part, tuple(key)) for part, *key in reversed(plan)] + [(part, (0, 0, 0)) for part in range(4)]
    loads = []
    for part, key in keys:
        if key not in loads:
            loads.append(key)
    for key in loads:
        cell = here.at(*key)
        guarded(
            [here.inside(key[0])],
            pltpu.make_async_copy(
                grads_ref.at[here.block(cell)], acc.at[here.spot(cell)], load_sem.at[here.spot(cell)]
            ).start,
        )
    here.meet()
    other = here.device(here.at(), True)
    for part, key in keys:
        cell = here.at(*key)
        rows = pl.ds(*parts[part])
        spot = here.spot(cell)
        guarded(
            [here.inside(key[0])],
            remote(
                grads_ref.at[here.block(cell, True), rows], twin.at[spot, rows], twin_send,
                twin_recv.at[part, spot], other,
            ).start,
        )
    for end, shift in ((0, 1), (depth - 1, 0)):

        def clear():
            for part in range(4):
                columns = 2 if ORDERS[part][1] == "z" else 1
                for column in range(columns):
                    for target in range(depth):
                        place = line.at[part, column, target + shift]
                        place[...] = jnp.zeros(place.shape, place.dtype)

        pl.when(here.z == end)(clear)
    waits = []
    loaded = set()
    for part, key in keys:
        start, size = parts[part]
        rows = pl.ds(start, size)
        short = pl.ds(0, size)
        first, second, third = reversed(ORDERS[part])
        away = {"z": key[0], "x": key[1], "y": key[2]}
        cell = here.at(*key)
        spot = here.spot(cell)
        present = here.inside(key[0])
        step = last_step(ORDERS[part], key)
        index0 = cell[0] * 2 + (cell[1] if first == "y" else cell[2])

        def task(part=part, key=key, start=start, size=size, rows=rows, short=short, step=step, cell=cell,
                 spot=spot, first=first, second=second, third=third, away=away, index0=index0):
            if key not in loaded:
                drain(acc.at[spot], load_sem.at[spot])
            drain(twin.at[spot, rows], twin_recv.at[part, spot])
            mine = acc.at[spot, rows]
            sources = [mine, twin.at[spot, rows]]
            order = ORDERS[part]
            column = 0
            if order[1] == "z":
                column = cell[1] if order[0] == "x" else cell[2]
            for i in (2, 1, 0):
                if i <= step - 1 or (i == step and order[i] != "z"):
                    break
                if i == 2 and order[i] != "z":
                    drain(flat0.at[part, index0, short], flat0_recv.at[part, index0])
                    sources.append(flat0.at[part, index0, short])
                elif order[i] != "z":
                    which = cell[0] if i == 1 else 0
                    drain(flat1.at[part, which, short], flat1_recv.at[part, which])
                    sources.append(flat1.at[part, which, short])
                else:
                    ways = (1, 0)
                    if i == step:
                        ways = (1,) if key[0] > 0 else (0,)
                    for way in ways:
                        place = line.at[part, column, cell[0] + way, short]

                        def arrive(place=place, way=way):
                            drain(place, line_recv.at[part, column, cell[0] + way])

                        pl.when(here.z > 0 if way else here.z < depth - 1)(arrive)
                        sources.append(place)
                    if i == step:
                        break
            if step < 0:
                add_rows(size, out_ref, start, sources)
                return
            add_rows(size, acc.at[spot], start, sources)
            dim = order[step]
            if dim == "z":
                way = 1 if key[0] > 0 else 0
                remote(
                    mine, line.at[part, column, cell[0] + way, short], line_send.at[part, column, cell[0]],
                    line_recv.at[part, column, cell[0] + way], here.device(here.at(dz=1 if way else -1)),
                ).start()
                return
            target = here.device(here.at(dx=1) if dim == "x" else here.at(dy=1))
            if step == 2:
                remote(
                    mine, flat0.at[part, index0, short], flat0_send.at[part], flat0_recv.at[part, index0], target
                ).start()
            else:
                which = cell[0] if step == 1 else 0
                remote(
                    mine, flat1.at[part, which, short], flat1_send.at[part], flat1_recv.at[part, which], target
                ).start()

        guarded([present], task)
        loaded.add(key)
        if step >= 0 and ORDERS[part][step] == "z":
            column = 0
            if ORDERS[part][1] == "z":
                column = cell[1] if ORDERS[part][0] == "x" else cell[2]
            waits.append(
                ([present], functools.partial(drain, acc.at[spot, rows], line_send.at[part, column, cell[0]]))
            )
    for conditions, action in waits:
        guarded(conditions, action)
    for part in range(4):
        rows = pl.ds(*parts[part])
        order = ORDERS[part]
        sent = 1
        for i, dim in enumerate(order):
            if dim != "z":
                sem = flat0_send if i == 2 else flat1_send
                drain(acc.at[pl.ds(0, sent), rows], sem.at[part])
            sent *= depth if dim == "z" else 2
    drain(acc, twin_send)


def reduce_blocks(depth, slots, grads):
    parts = part_rows(slots)
    rows = grads.shape[1]
    longest = max(size for _, size in parts)
    dma = pltpu.SemaphoreType.DMA
    bf = jnp.bfloat16
    return pl.pallas_call(
        functools.partial(reduce_body, depth, parts, plan_of(depth)),
        in_specs=[pl.BlockSpec(memory_space=pl.ANY)],
        out_specs=pl.BlockSpec(memory_space=pltpu.VMEM),
        out_shape=jax.ShapeDtypeStruct((rows, T), jnp.float32),
        scratch_shapes=[
            pltpu.VMEM((4 * depth, rows, T), bf),
            pltpu.VMEM((4 * depth, rows, T), bf),
            pltpu.VMEM((4, 2 * depth, longest, T), bf),
            pltpu.VMEM((4, depth, longest, T), bf),
            pltpu.VMEM((4, 2, depth + 1, longest, T), bf),
            dma((4 * depth,)),
            dma,
            dma((4, 4 * depth)),
            dma((4,)),
            dma((4, 2 * depth)),
            dma((4,)),
            dma((4, depth)),
            dma((4, 2, depth)),
            dma((4, 2, depth + 1)),
        ],
        compiler_params=pltpu.CompilerParams(
            collective_id=1, has_side_effects=True, vmem_limit_bytes=63 << 20
        ),
        name="reduce_blocks",
    )(grads)


def grid_depth():
    towers = lax.axis_size("tower")
    if lax.axis_size("batch") != 2 or towers % 4 or towers > 16 or towers < 8:
        return None
    return towers // 4


def all_blocks(tiles, vec):
    depth = grid_depth()
    if depth is not None:
        return gather(depth, tiles, vec)
    own = jnp.concatenate([tiles.reshape(-1, T), vec.reshape(-1, T)], 0)
    own = jnp.pad(own, ((0, EXTRA - vec.size // T), (0, 0))).astype(jnp.bfloat16)
    return lax.all_gather(own, ("tower", "batch"), axis=0)


def own_sums(slots, grads):
    depth = grid_depth()
    if depth is not None:
        return reduce_blocks(depth, slots, grads)
    return lax.psum_scatter(grads, ("tower", "batch"), scatter_dimension=0).astype(jnp.float32)


def per_device(
    image_rows,
    text_rows,
    caption_lengths,
    concat_cot,
    tile_slot,
    tile_weight,
    tile_first,
    tile_second,
    left_stat,
    right_stat,
    left_basis,
    right_basis,
    vec_weight,
    vec_first,
    vec_second,
):
    slots = tile_weight.shape[0]
    copies = all_blocks(tile_weight, vec_weight)
    projected, image_grad, grads = tower(
        False, slots, tile_slot, caption_lengths, image_rows, concat_cot, copies
    )
    concat, text_grad, grads = tower(
        True, slots, tile_slot, caption_lengths, text_rows, concat_cot, copies, (projected, grads)
    )
    states = optimizer(
        own_sums(slots, grads),
        tile_weight,
        tile_first,
        tile_second,
        left_stat,
        right_stat,
        left_basis,
        right_basis,
        vec_weight,
        vec_first,
        vec_second,
    )
    return (concat, image_grad, text_grad, *states)


def solution(mesh):
    return jax.shard_map(
        per_device,
        mesh=mesh,
        in_specs=(
            P(("tower", "batch"), None, None),
            P(("tower", "batch"), None, None),
            P(),
            P(("tower", "batch"), None, None),
            P(),
            P(("tower", "batch"), None, None),
            P(("tower", "batch"), None, None),
            P(("tower", "batch"), None, None),
            P(("tower", "batch"), None, None),
            P(("tower", "batch"), None, None),
            P(("tower", "batch"), None, None),
            P(("tower", "batch"), None, None),
            P(("tower", "batch"), None),
            P(("tower", "batch"), None),
            P(("tower", "batch"), None),
        ),
        out_specs=(
            P(("tower", "batch"), None, None),
            P(("tower", "batch"), None, None),
            P(("tower", "batch"), None, None),
            P(("tower", "batch"), None, None),
            P(("tower", "batch"), None, None),
            P(("tower", "batch"), None, None),
            P(("tower", "batch"), None, None),
            P(("tower", "batch"), None, None),
            P(("tower", "batch"), None, None),
            P(("tower", "batch"), None, None),
            P(("tower", "batch"), None),
            P(("tower", "batch"), None),
            P(("tower", "batch"), None),
        ),
        check_vma=False,
    )
```

```python
import functools
import heapq
import itertools

import jax
import jax.numpy as jnp
from jax import lax
from jax.experimental import pallas as pl
from jax.experimental.pallas import tpu as pltpu
from jax.sharding import PartitionSpec as P

BETA_ONE = 0.9
BETA_TWO = 0.95
EPSILON = 1e-08
RATE_MATRIX = 0.05
RATE_VECTOR = 0.6
DECAY = 0.01
STEP = 10
D = 768
FF = 3072
HEADS = 12
HEAD_DIM = 64
IMG = 197
TXT = 512
MMROWS = 2
T = 256
EXTRA = 16
VECS = 11 + FF // D
MASKED = -1000000000.0
NN = (((1,), (0,)), ((), ()))
NT = (((1,), (1,)), ((), ()))
TN = (((0,), (0,)), ((), ()))
KB = D // T
FB = FF // T
WIDE = 2 * T
SET = 2 * KB * WIDE // T


def mm(a, b, dims=NN):
    return lax.dot_general(a, b, dims, preferred_element_type=jnp.float32)


def rounded(v):
    return v.astype(jnp.bfloat16)


def stats(v):
    center = v - jnp.mean(v, -1, keepdims=True)
    inverse = lax.rsqrt(jnp.mean(center * center, -1, keepdims=True) + 1e-05)
    return center * inverse, inverse


def norm_back(grad, normed, inverse):
    return inverse * (
        grad
        - jnp.mean(grad, -1, keepdims=True)
        - normed * jnp.mean(grad * normed, -1, keepdims=True)
    )


def thirds(v):
    high = rounded(v)
    v = v - high.astype(jnp.float32)
    middle = rounded(v)
    return high, middle, rounded(v - middle.astype(jnp.float32))


def tower_body(is_text, rows, slots, slot_ref, length_ref, x_ref, cot_ref, copies, *rest):
    if is_text:
        zi_ref, _, cat_ref, dx_ref, grads = rest[:5]
        z_ref = None
    else:
        z_ref, dx_ref, grads = rest[:3]
        blank, blank_sem = rest[-2:]
        rest = rest[:-2]
    (wqkv, wo, wu, wd, wp, n1, n1t, qkv, qt, o, ot, a, n2, n2t, slope, h, ht, y, n3, n3t,
     cat, da, dqkv, logs, stage, vec_low, vec_all, bias_up, vec_out,
     wsem, stage_sem, vec_sem, vec_out_sem) = rest[5 if is_text else 3 :]
    dy = cat.at[pl.ds(0, rows)]
    dyb, dab, do, dot_, du = n3, n2, o, n3t, h
    first_tile = slot_ref.shape[0] // 2 if is_text else 0
    first_vec = VECS if is_text else 0
    real = TXT if is_text else IMG
    chunk = 64 if is_text else 16
    chunks = [(i * chunk, min((i + 1) * chunk, real)) for i in range(rows // chunk)]
    if is_text:
        length = length_ref[lax.axis_index("tower") * lax.axis_size("batch") + lax.axis_index("batch")]
    else:
        length = IMG
    tile_rows = slots * T

    def padded(value):
        short = chunk - value.shape[0]
        if short:
            value = jnp.concatenate([value, jnp.zeros((short, D), value.dtype)], 0)
        return value

    def x_of(c):
        return padded(x_ref[0, c[0] : c[1], :].astype(jnp.float32))

    def g_of(c):
        begin = c[0] + MMROWS + (IMG if is_text else 0)
        base = begin // 16 * 16
        end = min(-(-(begin + chunk) // 16) * 16, begin + c[1] - c[0])
        value = cot_ref[0, base:end, :].astype(jnp.float32)
        return padded(value[begin - base : begin - base + c[1] - c[0]])

    def at_slot(ref, slot):
        return ref.at[slot // slots, pl.ds(pl.multiple_of(slot % slots * T, T), T), :]

    extra = pl.ds(tile_rows, EXTRA)
    vec_count = VECS + MMROWS if is_text else VECS
    for i in range(vec_count):
        pltpu.make_async_copy(copies.at[first_vec + i, extra], vec_low.at[i], vec_sem).start()
    mats = [(wqkv, 0), (wqkv, D), (wqkv, 2 * D), (wo, 0), (wu, 0), (wd, 0), (wp, 0)]
    shapes = [(KB, KB)] * 4 + [(KB, FB), (FB, KB), (KB, KB)]
    starts = [0]
    for rb, cb in shapes:
        starts.append(starts[-1] + rb * cb)

    def load(which, sem):
        ref, shift = mats[which]
        rb, cb = shapes[which]

        def one(i, _):
            slot = slot_ref[first_tile + starts[which] + i]
            r, c = i // cb, i % cb
            pltpu.make_async_copy(
                at_slot(copies, slot),
                ref.at[pl.ds(pl.multiple_of(r * T, T), T), pl.ds(pl.multiple_of(shift + c * T, T), T)],
                wsem.at[sem],
            ).start()
            return 0

        lax.fori_loop(0, rb * cb, one, 0)

    def drain(ref, sem):
        pltpu.make_async_copy(ref, ref, sem).wait()

    for which, sem in enumerate((0, 0, 0, 1, 2, 3, 4)):
        load(which, sem)
    if not is_text:
        blank[...] = jnp.zeros(blank.shape, blank.dtype)

        def clear(i, _):
            pltpu.make_async_copy(blank, grads.at[i], blank_sem).start()
            return 0

        lax.fori_loop(0, grads.shape[0], clear, 0)

    def put(place, tiles):
        for n, (_, value) in enumerate(tiles):
            stage[place, n] = rounded(value)
        for n, (tile, _) in enumerate(tiles):
            slot = slot_ref[first_tile + tile]
            pltpu.make_async_copy(stage.at[place, n], at_slot(grads, slot), stage_sem.at[place]).start()

    def free(place, count):
        drain(stage.at[place, pl.ds(0, count)], stage_sem.at[place])

    def square(which, product):
        return [
            (starts[which] + r * KB + k, product[r * T : (r + 1) * T, k * T : (k + 1) * T])
            for r in range(KB)
            for k in range(KB)
        ]

    drain(vec_low.at[pl.ds(0, vec_count)], vec_sem)
    for i in range(vec_count):
        line = jnp.concatenate([vec_low[i, k : k + 1, :] for k in range(KB)], 1).astype(jnp.float32)
        vec_all[i : i + 1, :] = line
        if 7 <= i < 7 + FF // D:
            bias_up[:, (i - 7) * D : (i - 6) * D] = line

    def vec(i):
        return vec_all[i : i + 1, :]

    def vec_grad(i, line):
        line = rounded(line)
        parts = [line[:, k * T : (k + 1) * T] for k in range(KB)]
        parts.append(jnp.zeros((EXTRA - KB, T), jnp.bfloat16))
        vec_out[i] = jnp.concatenate(parts, 0)
        pltpu.make_async_copy(vec_out.at[i], grads.at[first_vec + i, extra], vec_out_sem).start()

    for c in chunks:
        normed, _ = stats(x_of(c))
        n1[c[0] : c[0] + chunk, :] = rounded(normed * vec(0) + vec(1))
    n1t[...] = n1[...].T
    drain(wqkv, wsem.at[0])
    scale = HEAD_DIM ** (-0.5)
    qkv[:, :D] = rounded((mm(n1[...], wqkv[:, :D]) + vec(2))) * jnp.asarray(scale, jnp.bfloat16)
    qkv[:, D : 2 * D] = rounded(mm(n1[...], wqkv[:, D : 2 * D]))
    qkv[:, 2 * D :] = rounded(mm(n1[...], wqkv[:, 2 * D :]) + vec(3))
    qt[...] = qkv[:, :D].T
    lane = lax.broadcasted_iota(jnp.int32, (rows, 2 * HEAD_DIM), 1)
    keys = lax.broadcasted_iota(jnp.int32, (rows, 2 * HEAD_DIM), 0)
    penalty = jnp.where(keys < length, 0.0, MASKED).astype(jnp.bfloat16)
    one = jnp.ones((rows, 2 * HEAD_DIM), jnp.bfloat16)
    zero = jnp.zeros((rows, 2 * HEAD_DIM), jnp.bfloat16)

    def pair_cols(p, base):
        return pl.ds(pl.multiple_of(base + p * 2 * HEAD_DIM, 2 * HEAD_DIM), 2 * HEAD_DIM)

    def beside(side, value, others):
        base = HEAD_DIM * (1 - side)
        result = zero
        for n, other in enumerate(others):
            result = jnp.where(lane == base + n, other, result)
        return jnp.where((lane < HEAD_DIM) if side == 0 else (lane >= HEAD_DIM), value, result)

    def attend(p, _):
        q = qkv[:, pair_cols(p, 0)]
        k = qkv[:, pair_cols(p, D)]
        v = qkv[:, pair_cols(p, 2 * D)]
        outs = []
        for side in range(2):
            s = mm(beside(side, q, [one]), beside(side, k, [penalty]), NT)
            top = jnp.max(s, -1, keepdims=True)
            s = jnp.exp(s - top)
            total = jnp.sum(s, -1, keepdims=True)
            logs[2 * p + side] = jnp.broadcast_to(top + jnp.log(total), (rows, 128))
            outs.append(mm(rounded(s * (1.0 / total)), v))
        o[:, pair_cols(p, 0)] = rounded(jnp.where(lane < HEAD_DIM, outs[0], outs[1]))
        return 0

    lax.fori_loop(0, HEADS // 2, attend, 0)
    ot[...] = o[...].T
    drain(wo, wsem.at[1])
    a[...] = mm(o[...], wo[...])
    for c in chunks:
        at = slice(c[0], c[0] + chunk)
        value = x_of(c) + (a[at, :] + vec(4))
        a[at, :] = value
        normed, _ = stats(value)
        n2[at, :] = rounded(normed * vec(5) + vec(6))
    n2t[...] = n2[...].T
    drain(wu, wsem.at[2])

    def up(i, _):
        cols = pl.ds(pl.multiple_of(i * WIDE, WIDE), WIDE)
        u = mm(n2[...], wu[:, cols]) + bias_up[:, cols]
        cumulative = 0.5 * (1.0 + lax.erf(u * 0.7071067811865476))
        hidden = rounded(u * cumulative)
        slope[:, cols] = cumulative + u * (jnp.exp(-0.5 * u * u) * 0.3989422804014327)
        h[:, cols] = hidden
        ht[cols, :] = hidden.T
        return 0

    lax.fori_loop(0, FF // WIDE, up, 0)
    drain(wd, wsem.at[3])
    y[...] = mm(h[...], wd[...])
    for c in chunks:
        at = slice(c[0], c[0] + chunk)
        value = a[at, :] + (y[at, :] + vec(11))
        y[at, :] = value
        normed, _ = stats(value)
        n3[at, :] = rounded(normed * vec(12) + vec(13))
    n3t[...] = n3[...].T
    drain(wp, wsem.at[4])
    keep = lax.broadcasted_iota(jnp.int32, (rows, 1), 0) < length
    z = jnp.where(keep, mm(n3[...], wp[...]) + vec(14), 0.0)
    if is_text:
        begin = MMROWS + IMG
        cat[:MMROWS, :] = vec_all[VECS : VECS + MMROWS, :]
        cat[MMROWS:begin, :] = zi_ref[0].astype(jnp.float32)
        cat[begin : begin + TXT, :] = z
        cat_ref[0] = rounded(cat[...])
    else:
        even = IMG // 16 * 16
        z_ref[0, :even, :] = rounded(z[:even])
        z_ref[0, even:IMG, :] = rounded(z[even:IMG])

    if not is_text:
        drain(grads, blank_sem)
    zeros = jnp.zeros((1, D), jnp.float32)
    total = zeros
    for c in chunks:
        at = slice(c[0], c[0] + chunk)
        g = jnp.where(keep[at, :], g_of(c), 0.0)
        total = total + jnp.sum(g, 0, keepdims=True)
        dyb[at, :] = rounded(g)
    vec_grad(14, total)
    put(1, square(6, mm(n3t[...], dyb[...])))
    dy[...] = mm(dyb[...], wp[...], NT)
    gain, shift, bias = zeros, zeros, zeros
    for c in chunks:
        at = slice(c[0], c[0] + chunk)
        normed, inverse = stats(y[at, :])
        g = dy[at, :]
        gain = gain + jnp.sum(g * normed, 0, keepdims=True)
        shift = shift + jnp.sum(g, 0, keepdims=True)
        g = norm_back(g * vec(12), normed, inverse)
        dy[at, :] = g
        low = rounded(g)
        dyb[at, :] = low
        bias = bias + jnp.sum(low.astype(jnp.float32), 0, keepdims=True)
    vec_grad(12, gain)
    vec_grad(13, shift)
    vec_grad(11, bias)

    def down(i, _):
        place = i % 2
        pl.when(i == 1)(functools.partial(free, 1, KB * KB))
        pl.when(i >= 2)(functools.partial(free, place, SET))
        cols = pl.ds(pl.multiple_of(i * WIDE, WIDE), WIDE)
        low = rounded(mm(dyb[...], wd[cols, :], NT) * slope[:, cols])
        du[:, cols] = low
        bias_up[:, cols] = jnp.sum(low.astype(jnp.float32), 0, keepdims=True)
        down_grad = mm(ht[cols, :], dyb[...])
        up_grad = mm(n2t[...], low)
        tiles = []
        for w in range(WIDE // T):
            band = slice(w * T, (w + 1) * T)
            number = i * (WIDE // T) + w
            for k in range(KB):
                other = slice(k * T, (k + 1) * T)
                tiles.append((starts[5] + number * KB + k, down_grad[band, other]))
                tiles.append((starts[4] + k * FB + number, up_grad[other, band]))
        put(place, tiles)
        return 0

    lax.fori_loop(0, FF // WIDE, down, 0)
    for i in range(FF // D):
        vec_grad(7 + i, bias_up[:, i * D : (i + 1) * D])
    da[...] = mm(du[...], wu[...], NT)
    gain, shift, bias = zeros, zeros, zeros
    for c in chunks:
        at = slice(c[0], c[0] + chunk)
        normed, inverse = stats(a[at, :])
        g = da[at, :]
        gain = gain + jnp.sum(g * normed, 0, keepdims=True)
        shift = shift + jnp.sum(g, 0, keepdims=True)
        g = dy[at, :] + norm_back(g * vec(5), normed, inverse)
        da[at, :] = g
        low = rounded(g)
        dab[at, :] = low
        bias = bias + jnp.sum(low.astype(jnp.float32), 0, keepdims=True)
    vec_grad(5, gain)
    vec_grad(6, shift)
    vec_grad(4, bias)
    dout = mm(dab[...], wo[...], NT)
    free(0, SET)
    put(0, square(3, mm(ot[...], dab[...])))
    low = rounded(dout)
    y[...] = low.astype(jnp.float32) * o[...].astype(jnp.float32)
    do[...] = low
    dot_[...] = low.T

    def attend_back(p, _):
        q = qkv[:, pair_cols(p, 0)]
        k = qkv[:, pair_cols(p, D)]
        v = qkv[:, pair_cols(p, 2 * D)]
        g = do[:, pair_cols(p, 0)]
        each = y[:, pair_cols(p, 0)]
        dqs, dks, dvs = [], [], []
        for side in range(2):
            half = pl.ds(pl.multiple_of((2 * p + side) * HEAD_DIM, HEAD_DIM), HEAD_DIM)
            mine = (lane < HEAD_DIM) if side == 0 else (lane >= HEAD_DIM)
            minus = [-one] * 3
            w = jnp.exp(
                mm(
                    beside(side, q, [one, *thirds(logs[2 * p + side])]),
                    beside(side, k, [penalty, *minus]),
                    NT,
                )
            )
            dvs.append(mm(dot_[half, :], rounded(w)))
            c = jnp.sum(jnp.where(mine, each, 0.0), -1, keepdims=True)
            dw = mm(
                beside(side, g, thirds(jnp.broadcast_to(c, (rows, 2 * HEAD_DIM)))),
                beside(side, v, minus),
                NT,
            )
            ds = rounded(w * dw)
            dqs.append(mm(ds, k))
            dks.append(mm(qt[half, :], ds))
        dqkv[:, pair_cols(p, 0)] = rounded(jnp.where(lane < HEAD_DIM, dqs[0], dqs[1]) * scale)
        dqkv[:, pair_cols(p, D)] = rounded(jnp.concatenate(dks, 0).T)
        dqkv[:, pair_cols(p, 2 * D)] = rounded(jnp.concatenate(dvs, 0).T)
        return 0

    lax.fori_loop(0, HEADS // 2, attend_back, 0)
    for m, number in ((0, 2), (2, 3)):
        vec_grad(number, jnp.sum(dqkv[:, m * D : (m + 1) * D].astype(jnp.float32), 0, keepdims=True))
    for m in range(3):
        free((1 + m) % 2, SET if m == 0 else KB * KB)
        put((1 + m) % 2, square(m, mm(n1t[...], dqkv[:, m * D : (m + 1) * D])))
    dy[...] = mm(dqkv[...], wqkv[...], NT)
    gain, shift = zeros, zeros
    for c in chunks:
        at = slice(c[0], c[0] + chunk)
        normed, inverse = stats(x_of(c))
        g = dy[at, :]
        gain = gain + jnp.sum(g * normed, 0, keepdims=True)
        shift = shift + jnp.sum(g, 0, keepdims=True)
        low = rounded(da[at, :] + norm_back(g * vec(0), normed, inverse))
        dx_ref[0, c[0] : c[1], :] = low[: c[1] - c[0]]
    vec_grad(0, gain)
    vec_grad(1, shift)
    if is_text:
        learned = cot_ref[0, :16, :].astype(jnp.float32)
        for i in range(MMROWS):
            vec_grad(VECS + i, learned[i : i + 1])
    free(0, KB * KB)
    free(1, KB * KB)
    drain(vec_out.at[pl.ds(0, vec_count)], vec_out_sem)


def tower(is_text, slots, tile_slot, lengths, x, cot, copies, before=()):
    bf, f32 = jnp.bfloat16, jnp.float32
    smem = pl.BlockSpec(memory_space=pltpu.SMEM)
    vmem = pl.BlockSpec(memory_space=pltpu.VMEM)
    hbm = pl.BlockSpec(memory_space=pl.ANY)
    dma = pltpu.SemaphoreType.DMA
    rows = -(-x.shape[1] // 16) * 16
    outs = [
        jax.ShapeDtypeStruct(cot.shape if is_text else x.shape, bf),
        jax.ShapeDtypeStruct(x.shape, bf),
        jax.ShapeDtypeStruct(copies.shape, bf),
    ]
    scratch = [
        pltpu.VMEM((D, 3 * D), bf), pltpu.VMEM((D, D), bf), pltpu.VMEM((D, FF), bf),
        pltpu.VMEM((FF, D), bf), pltpu.VMEM((D, D), bf),
        pltpu.VMEM((rows, D), bf), pltpu.VMEM((D, rows), bf),
        pltpu.VMEM((rows, 3 * D), bf), pltpu.VMEM((D, rows), bf),
        pltpu.VMEM((rows, D), bf), pltpu.VMEM((D, rows), bf),
        pltpu.VMEM((rows, D), f32),
        pltpu.VMEM((rows, D), bf), pltpu.VMEM((D, rows), bf),
        pltpu.VMEM((rows, FF), f32),
        pltpu.VMEM((rows, FF), bf), pltpu.VMEM((FF, rows), bf),
        pltpu.VMEM((rows, D), f32),
        pltpu.VMEM((rows, D), bf), pltpu.VMEM((D, rows), bf),
        pltpu.VMEM((cot.shape[1] if is_text else rows, D), f32),
        pltpu.VMEM((rows, D), f32),
        pltpu.VMEM((rows, 3 * D), bf),
        pltpu.VMEM((HEADS, rows, 128), f32),
        pltpu.VMEM((2, SET, T, T), bf),
        pltpu.VMEM((VECS + MMROWS, EXTRA, T), bf), pltpu.VMEM((VECS + MMROWS, D), f32),
        pltpu.VMEM((1, FF), f32), pltpu.VMEM((VECS + MMROWS, EXTRA, T), bf),
        dma((5,)), dma((2,)), dma, dma,
    ]
    if not is_text:
        scratch += [pltpu.VMEM((slots * T + EXTRA, T), bf), dma]
    return pl.pallas_call(
        functools.partial(tower_body, is_text, rows, slots),
        in_specs=[smem, smem, vmem, vmem, hbm] + ([vmem, hbm] if is_text else []),
        out_specs=[vmem, vmem, hbm],
        out_shape=outs,
        scratch_shapes=scratch,
        input_output_aliases={6: 2} if is_text else {},
        compiler_params=pltpu.CompilerParams(vmem_limit_bytes=63 << 20),
        name="text_tower" if is_text else "image_tower",
    )(tile_slot, lengths, x, cot, copies, *before)


def split(x):
    hi = x.astype(jnp.bfloat16)
    lo = (x - hi.astype(jnp.float32)).astype(jnp.bfloat16)
    return hi, lo


def dot(a, b, dims):
    return lax.dot_general(a, b, dims, preferred_element_type=jnp.float32)


def mm3(a, b, dims):
    return dot(a[0], b[0], dims) + (dot(a[0], b[1], dims) + dot(a[1], b[0], dims))


def adam_step(first, second):
    return (
        first
        / (1.0 - BETA_ONE**STEP)
        / (jnp.sqrt(second / (1.0 - BETA_TWO**STEP)) + EPSILON)
    )


B = 64
GROUP = 8
INS, OUTS = 7, 5


def eliminate_group(diag, jg):
    count = diag.shape[0]
    shape = (count, GROUP, 2 * B)
    subs = lax.broadcasted_iota(jnp.int32, shape, 1)
    top = slice(jg * GROUP, jg * GROUP + GROUP)
    tile = diag[:, top, :]
    for jj in range(0, GROUP, 2):
        j = jg * GROUP + jj
        first = jnp.broadcast_to(tile[:, :, j : j + 1], shape)
        second = jnp.broadcast_to(tile[:, :, j + 1 : j + 2], shape)
        p00, p01, p11 = first[:, jj : jj + 1], second[:, jj : jj + 1], second[:, jj + 1 : jj + 2]
        r0, r1 = tile[:, jj : jj + 1], tile[:, jj + 1 : jj + 2]
        inverse = 1.0 / (p00 * p11 - p01 * p01)
        cross = p01 * inverse
        t0 = (p11 * inverse) * r0 - cross * r1
        t1 = (p00 * inverse) * r1 - cross * r0
        lower = tile - first * t0 - second * t1
        tile = jnp.where(subs > jj + 1, lower, jnp.where(subs == jj + 1, tile - (p01 / p00) * r0, tile))
        if jg < B // GROUP - 1:
            rest = diag[:, jg * GROUP + GROUP :, :]
            diag[:, jg * GROUP + GROUP :, :] = (
                rest - rest[:, :, j : j + 1] * t0 - rest[:, :, j + 1 : j + 2] * t1
            )
    diag[:, top, :] = tile


class Update:
    def __init__(self, slots, begin, shift, sums, ins, outs, inbuf, outbuf, qbuf, work, diag, in_sem, out_sem, q_sem):
        self.slots, self.begin, self.shift = slots, begin, shift
        self.sums, self.ins, self.outs = sums, ins, outs
        self.inbuf, self.outbuf, self.qbuf, self.work, self.diag = inbuf, outbuf, qbuf, work, diag
        self.in_sem, self.out_sem, self.q_sem = in_sem, out_sem, q_sem

    def fetch(self):
        for s in range(self.slots):
            for n in range(INS):
                pltpu.make_async_copy(self.ins[n].at[self.begin + s], self.inbuf.at[s, n], self.in_sem.at[s]).start()

    def refine(self, s):
        pltpu.make_async_copy(self.inbuf.at[s], self.inbuf.at[s], self.in_sem.at[s]).wait()
        place = s % 2
        if s >= 2:
            pltpu.make_async_copy(self.outbuf.at[place], self.outbuf.at[place], self.out_sem.at[place]).wait()
        w, m1, m2, ls, rs, lb, rb = (self.inbuf.at[s, n] for n in range(INS))
        wn, m1n, m2n, lsn, rsn = (self.outbuf.at[place, n] for n in range(OUTS))
        e = split(self.sums[s * T : (s + 1) * T, :])
        ql = split(lb[...])
        qr = split(rb[...])
        left = BETA_TWO * ls[...] + (1.0 - BETA_TWO) * mm3(e, e, NT)
        right = BETA_TWO * rs[...] + (1.0 - BETA_TWO) * mm3(e, e, TN)
        lsn[...] = left
        rsn[...] = right
        turned = mm3(split(mm3(ql, e, TN)), qr, NN)
        first = BETA_ONE * m1[...] + (1.0 - BETA_ONE) * turned
        second = BETA_TWO * m2[...] + (1.0 - BETA_TWO) * turned * turned
        m1n[...] = first
        m2n[...] = second
        direction = mm3(split(mm3(ql, split(adam_step(first, second)), NN)), qr, NT)
        old = w[...]
        wn[...] = old - RATE_MATRIX * (direction + DECAY * old)
        for n in range(OUTS):
            pltpu.make_async_copy(self.outbuf.at[place, n], self.outs[n].at[self.shift + s], self.out_sem.at[place]).start()
        for side, (basis, stat) in enumerate(((ql, left), (qr, right))):
            y = mm3(basis, split(stat), TN)
            y = y * lax.rsqrt(jnp.sum(y * y, axis=1, keepdims=True))
            self.work[2 * s + side, :, T:] = y
            y = split(y)
            self.work[2 * s + side, :, :T] = mm3(y, y, NT)

    def load(self, k):
        low = k * B
        edge = low // (2 * B) * 2 * B
        row = lax.broadcasted_iota(jnp.int32, (B, 2 * B), 0)
        lane = lax.broadcasted_iota(jnp.int32, (B, 2 * B), 1)
        for m in range(2 * self.slots):
            block = self.work[m, low : low + B, edge : edge + 2 * B]
            if low % (2 * B):
                block = pltpu.roll(block, B, 1)
            self.diag[m] = jnp.where(lane < B, block, jnp.where(lane == row + B, 1.0, 0.0))

    def products(self, k, begin, end):
        low = k * B
        edge = low // (2 * B) * 2 * B
        row = lax.broadcasted_iota(jnp.int32, (B, 2 * B), 0)
        lane = lax.broadcasted_iota(jnp.int32, (B, 2 * B), 1)
        work = self.work

        def one(m):
            d = self.diag[m]
            pivots = jnp.sum(jnp.where(lane == row, d, 0.0), axis=1, keepdims=True)
            high, rest = split(d[:, B:] * lax.rsqrt(pivots))
            inverse = jnp.concatenate([high, rest, high], 1)
            high, rest = split(work[m, low : low + B, edge:])
            new = dot(inverse, jnp.concatenate([high, high, rest], 0), NN)
            work[m, low : low + B, edge:] = new
            if low + B < T:
                high, rest = split(new)
                after = low + B - edge
                start = (low + B) // (2 * B) * 2 * B
                left = jnp.concatenate([high, rest, high], 0)[:, after : T - edge]
                right = jnp.concatenate([high, high, rest], 0)[:, start - edge :]
                work[m, low + B :, start:] = work[m, low + B :, start:] - dot(left, right, TN)

        def pair(i, _):
            one(begin + 2 * i)
            one(begin + 2 * i + 1)
            return 0

        lax.fori_loop(0, (end - begin) // 2, pair, 0)

    def finish(self, s):
        for side in range(2):
            if s:
                pltpu.make_async_copy(self.qbuf.at[side], self.qbuf.at[side], self.q_sem.at[side]).wait()
            self.qbuf[side] = self.work[2 * s + side, :, T:].T
            pltpu.make_async_copy(self.qbuf.at[side], self.outs[OUTS + side].at[self.shift + s], self.q_sem.at[side]).start()

    def close(self):
        for side in range(2):
            pltpu.make_async_copy(self.qbuf.at[side], self.qbuf.at[side], self.q_sem.at[side]).wait()
        for place in range(min(2, self.slots)):
            pltpu.make_async_copy(self.outbuf.at[place], self.outbuf.at[place], self.out_sem.at[place]).wait()

    def steps(self):
        result = [functools.partial(self.refine, s) for s in range(self.slots)]
        for k in range(T // B):
            result.append(functools.partial(self.load, k))
            result += [functools.partial(eliminate_group, self.diag, jg) for jg in range(B // GROUP)]
            middle = self.slots // 2 * 2
            result += [functools.partial(self.products, k, a, b) for a, b in ((0, middle), (middle, 2 * self.slots)) if a < b]
        result += [functools.partial(self.finish, s) for s in range(self.slots)]
        result.append(self.close)
        return result


def update_scratch(slots):
    f32 = jnp.float32
    dma = pltpu.SemaphoreType.DMA
    return [
        pltpu.VMEM((slots, INS, T, T), f32),
        pltpu.VMEM((2, OUTS, T, T), f32),
        pltpu.VMEM((2, T, T), f32),
        pltpu.VMEM((2 * slots, T, 2 * T), f32),
        pltpu.VMEM((2 * slots, B, 2 * B), f32),
        dma((slots,)),
        dma((2,)),
        dma((2,)),
    ]


def rest_body(total, done, sums_ref, v_refs, ins, befores, outs, v_outs, scratch, passing, passing_sem):
    update = Update(total - done, done, done, sums_ref, ins, outs, *scratch)
    update.fetch()
    arrivals = [
        pltpu.make_async_copy(before, passing.at[n], passing_sem.at[0, n]) for n, before in enumerate(befores)
    ]
    departures = [
        pltpu.make_async_copy(passing.at[n], outs[n].at[pl.ds(0, done)], passing_sem.at[1, n])
        for n in range(len(befores))
    ]
    for copy in arrivals:
        copy.start()
    vw_ref, v1_ref, v2_ref = v_refs
    vwn_ref, v1n_ref, v2n_ref = v_outs
    for k in range(vw_ref.shape[1] // T):
        cols = slice(k * T, (k + 1) * T)
        row = (total - done) * T + k
        g = sums_ref[row : row + 1, :]
        first = BETA_ONE * v1_ref[:, cols] + (1.0 - BETA_ONE) * g
        second = BETA_TWO * v2_ref[:, cols] + (1.0 - BETA_TWO) * g * g
        v1n_ref[:, cols] = first
        v2n_ref[:, cols] = second
        vwn_ref[:, cols] = vw_ref[:, cols] - RATE_VECTOR * adam_step(first, second)
    for number, step in enumerate(update.steps()):
        step()
        if number == total - done - 1:
            for arrival, departure in zip(arrivals, departures):
                arrival.wait()
                departure.start()
    for copy in departures:
        copy.wait()


def optimizer(sums, states, vectors, befores=()):
    total = states[0].shape[0]
    done = befores[0].shape[0] if befores else 0
    hbm = pl.BlockSpec(memory_space=pl.ANY)
    vmem = pl.BlockSpec(memory_space=pltpu.VMEM)
    f32 = jnp.float32
    count = len(befores)

    def body(*refs):
        sums_ref, v_refs, refs = refs[0], refs[1:4], refs[4:]
        ins, befores, refs = refs[:INS], refs[INS : INS + count], refs[INS + count :]
        outs, v_outs, refs = refs[:INS], refs[INS : INS + 3], refs[INS + 3 :]
        rest_body(total, done, sums_ref, v_refs, ins, befores, outs, v_outs, refs[:-2], *refs[-2:])

    return pl.pallas_call(
        body,
        in_specs=[vmem] * 4 + [hbm] * (INS + count),
        out_specs=[hbm] * INS + [vmem] * 3,
        out_shape=[jax.ShapeDtypeStruct(v.shape, f32) for v in (*states, *vectors)],
        scratch_shapes=update_scratch(total - done)
        + [pltpu.VMEM((INS, max(done, 1), T, T), f32), pltpu.SemaphoreType.DMA((2, INS))],
        compiler_params=pltpu.CompilerParams(vmem_limit_bytes=60 << 20),
        name="optimizer",
    )(sums, *vectors, *states, *befores)


ORDERS = ("xzy", "yzx", "zxy", "zyx")


def part_rows(slots):
    quarter = slots * T // 4
    sizes = [quarter, quarter, quarter, quarter + EXTRA]
    return [(sum(sizes[:i]), sizes[i]) for i in range(4)]


def last_step(order, key):
    away = {"z": key[0], "x": key[1], "y": key[2]}
    steps = [i for i in range(3) if away[order[i]]]
    return steps[-1] if steps else -1


def plan_of(depth):
    cells = list(itertools.product(range(depth), range(2), range(2)))
    queues, free, events, arrived = {}, {}, [], {}
    ticket = itertools.count()

    def onward(cell, part, source, now):
        order = ORDERS[part]
        key = (source[0] - cell[0], source[1] ^ cell[1], source[2] ^ cell[2])
        step = last_step(order, key)
        for i in range(3):
            z, x, y = cell
            if order[i] == "z":
                if i > step:
                    ways = (1, -1)
                elif i == step:
                    ways = (1,) if key[0] < 0 else (-1,)
                else:
                    ways = ()
                targets = [(z + w, x, y) for w in ways if 0 <= z + w < depth]
            elif i > step:
                targets = [(z, 1 - x, y) if order[i] == "x" else (z, x, 1 - y)]
            else:
                targets = []
            for target in targets:
                heapq.heappush(queues.setdefault((cell, target), []), (now, next(ticket), part, source))
                heapq.heappush(events, (now, next(ticket), 0, (cell, target)))

    for cell in cells:
        for part in range(4):
            onward(cell, part, cell, 0.0)
    while events:
        now, _, kind, what = heapq.heappop(events)
        if kind == 0:
            if queues[what] and free.get(what, 0.0) <= now:
                _, _, part, source = heapq.heappop(queues[what])
                free[what] = now + 2.0
                heapq.heappush(events, (now + 2.0, next(ticket), 0, what))
                heapq.heappush(events, (now + 2.5, next(ticket), 1, (what[1], part, source)))
        else:
            cell, part, source = what
            key = (part, source[0] - cell[0], source[1] ^ cell[1], source[2] ^ cell[2])
            arrived.setdefault(key, []).append(now)
            onward(cell, part, source, now)
    times = {k: sum(v) / len(v) for k, v in arrived.items()}
    fixed = {}

    def time_of(key):
        if key not in fixed:
            part, dz, dx, dy = key
            step = last_step(ORDERS[part], key[1:])
            if step < 0:
                return 0.0
            dim = ORDERS[part][step]
            if dim == "z":
                parent = (part, dz - (1 if dz > 0 else -1), dx, dy)
            else:
                parent = (part, dz, 0 if dim == "x" else dx, 0 if dim == "y" else dy)
            fixed[key] = max(times[key], time_of(parent) + 0.01)
        return fixed[key]

    return sorted((time_of(k), k) for k in times)


class Place:
    def __init__(self, depth):
        tower = lax.axis_index("tower")
        self.depth = depth
        self.core = tower % 2
        self.x = tower // 2 % 2
        self.z = tower // 4
        self.y = lax.axis_index("batch")

    def at(self, dz=0, dx=0, dy=0):
        return (
            self.z + dz,
            1 - self.x if dx else self.x,
            1 - self.y if dy else self.y,
        )

    def device(self, cell, other=False):
        core = 1 - self.core if other else self.core
        return ((cell[0] * 2 + cell[1]) * 2 + core, cell[2])

    def block(self, cell, other=False):
        core = 1 - self.core if other else self.core
        return ((cell[0] * 2 + cell[1]) * 2 + core) * 2 + cell[2]

    def spot(self, cell):
        return (cell[0] * 2 + cell[1]) * 2 + cell[2]

    def inside(self, dz):
        if dz == 0:
            return None
        return self.z + dz < self.depth if dz > 0 else self.z + dz >= 0

    def meet(self):
        barrier = pltpu.get_barrier_semaphore()

        def greet(device):
            pl.semaphore_signal(barrier, inc=1, device_id=device, device_id_type=pl.DeviceIdType.MESH)

        greet(self.device(self.at(), True))
        greet(self.device(self.at(dx=1)))
        greet(self.device(self.at(dy=1)))
        for way in (1, -1):
            pl.when(self.inside(way))(functools.partial(greet, self.device(self.at(dz=way))))
        low = (self.z > 0).astype(jnp.int32)
        high = (self.z < self.depth - 1).astype(jnp.int32)
        pl.semaphore_wait(barrier, 3 + low + high)


def guarded(conditions, action):
    conditions = [c for c in conditions if c is not None]
    if not conditions:
        action()
    else:
        both = conditions[0]
        for c in conditions[1:]:
            both = jnp.logical_and(both, c)
        pl.when(both)(action)


def remote(src, dst, send, recv, device):
    return pltpu.make_async_remote_copy(
        src_ref=src, dst_ref=dst, send_sem=send, recv_sem=recv,
        device_id=device, device_id_type=pl.DeviceIdType.MESH,
    )


def drain(ref, sem):
    pltpu.make_async_copy(ref, ref, sem).wait()


def gather_body(
    depth, parts, plan, tiles_ref, vec_ref, out_ref, wide, own_ref, wide_sem, own_sem, z_sem, flat_sem, twin_sem, recv_sem
):
    slots = tiles_ref.shape[0]
    for slot in range(slots):
        pltpu.make_async_copy(tiles_ref.at[slot], wide.at[slot], wide_sem.at[slot]).start()
    here = Place(depth)
    here.meet()
    line = vec_ref[...].astype(jnp.bfloat16)
    pieces = [line[:, k * T : (k + 1) * T] for k in range(line.shape[1] // T)]
    pieces.append(jnp.zeros((EXTRA - len(pieces), T), jnp.bfloat16))
    own_ref[slots * T :, :] = jnp.concatenate(pieces, 0)
    for slot in range(slots):
        drain(wide.at[slot], wide_sem.at[slot])
        own_ref[slot * T : (slot + 1) * T, :] = wide[slot].astype(jnp.bfloat16)
    mine = pltpu.make_async_copy(own_ref, out_ref.at[here.block(here.at())], own_sem)
    mine.start()
    waits = []

    def handle(part, key):
        start, size = parts[part]
        rows = pl.ds(start, size)
        order = ORDERS[part]
        step = last_step(order, key)
        cell = here.at(*key)
        present = here.inside(key[0])
        block = here.block(cell)
        spot = here.spot(cell)
        place = out_ref.at[block, rows]
        source = own_ref.at[rows] if step < 0 else place

        def arrive():
            if step >= 0:
                drain(place, recv_sem.at[part, spot])

        guarded([present], arrive)
        for i in range(3):
            dim = order[i]
            if dim == "z":
                ways = (1, -1) if i > step else ()
                if i == step:
                    ways = (1,) if key[0] < 0 else (-1,)
                for way in ways:
                    sem = z_sem.at[part, spot, 0 if way > 0 else 1]
                    copy = remote(source, place, sem, recv_sem.at[part, spot], here.device(here.at(dz=way)))
                    conditions = [present, here.inside(way)]
                    guarded(conditions, copy.start)
                    waits.append((conditions, copy.wait_send))
            elif i > step:
                target = here.at(dx=1) if dim == "x" else here.at(dy=1)
                guarded(
                    [present],
                    remote(
                        source, place, flat_sem.at[part, 0 if dim == "x" else 1],
                        recv_sem.at[part, spot], here.device(target),
                    ).start,
                )
        guarded(
            [present],
            remote(source, place, twin_sem.at[0], twin_sem.at[1], here.device(here.at(), True)).start,
        )

    for part in range(4):
        handle(part, (0, 0, 0))
    for part, *key in plan:
        handle(part, tuple(key))
    for conditions, action in waits:
        guarded(conditions, action)
    for part in range(4):
        rows = pl.ds(*parts[part])
        sent = 1
        for dim in ORDERS[part]:
            if dim != "z":
                drain(out_ref.at[pl.ds(0, sent), rows], flat_sem.at[part, 0 if dim == "x" else 1])
            sent *= depth if dim == "z" else 2
    mine.wait()
    half = pl.ds(0, 4 * depth)
    drain(out_ref.at[half], twin_sem.at[0])
    drain(out_ref.at[half], twin_sem.at[1])


def gather(depth, tiles, vec):
    slots = tiles.shape[0]
    parts = part_rows(slots)
    rows = slots * T + EXTRA
    hbm = pl.BlockSpec(memory_space=pl.ANY)
    dma = pltpu.SemaphoreType.DMA
    return pl.pallas_call(
        functools.partial(gather_body, depth, parts, [key for _, key in plan_of(depth)]),
        in_specs=[hbm, pl.BlockSpec(memory_space=pltpu.VMEM)],
        out_specs=hbm,
        out_shape=jax.ShapeDtypeStruct((8 * depth, rows, T), jnp.bfloat16),
        scratch_shapes=[
            pltpu.VMEM(tiles.shape, jnp.float32),
            pltpu.VMEM((rows, T), jnp.bfloat16),
            dma((slots,)),
            dma,
            dma((4, 4 * depth, 2)),
            dma((4, 2)),
            dma((2,)),
            dma((4, 4 * depth)),
        ],
        compiler_params=pltpu.CompilerParams(
            collective_id=0, has_side_effects=True, vmem_limit_bytes=60 << 20
        ),
        name="gather",
    )(tiles, vec)


def add_rows(size, target, start, sources):
    def piece(at, count):
        total = sources[0][pl.ds(at, count), :].astype(jnp.float32)
        for source in sources[1:]:
            total = total + source[pl.ds(at, count), :].astype(jnp.float32)
        target[pl.ds(start + at, count), :] = total.astype(target.dtype)

    whole = size // 128

    def body(i, _):
        piece(pl.multiple_of(i * 128, 128), 128)
        return 0

    lax.fori_loop(0, whole, body, 0)
    if size % 128:
        piece(whole * 128, size % 128)


LOADS = 8


def wave_rows(slots, early):
    result = []
    for begin, count, extra in ((0, early, 0), (early * T, slots - early, EXTRA)):
        size = count * T // 4
        sizes = [size, size, size, size + extra]
        result += [(begin + sum(sizes[:i]), sizes[i]) for i in range(4)]
    return result


def wave_keys(depth, slots, early):
    timed = plan_of(depth)
    end = timed[-1][0]
    share = early / slots
    result = []
    for wave in range(2):
        for when, (part, *key) in timed + [(0.0, (part, 0, 0, 0)) for part in range(4)]:
            spent = end - when
            at = spent * share if wave == 0 else end * (share - 0.06) + spent * (1 - share)
            result.append((at, wave, -len(result), 4 * wave + part, tuple(key)))
    return [(part, key) for _, _, _, part, key in sorted(result)]


def reduce_body(depth, slots, early, parts, keys, grads_ref, *refs):
    ins, refs = refs[:INS], refs[INS:]
    late_ref, refs = refs[0], refs[1:]
    outs, refs = refs[:INS], refs[INS:]
    (own, twin, sums, flat0_a, flat0_b, flat1_a, flat1_b, line_a, line_b,
     load_sem, twin_send, twin_recv, flat0_send, flat0_recv, flat1_send, flat1_recv, line_send, line_recv) = refs[:18]
    update = Update(early, 0, 0, sums, ins, outs, *refs[18:])
    here = Place(depth)

    def load(number):
        part, key = keys[number]
        cell = here.at(*key)
        start, size = parts[part]
        place = number % LOADS
        guarded(
            [here.inside(key[0])],
            pltpu.make_async_copy(
                grads_ref.at[here.block(cell), pl.ds(start, size)], own.at[place, pl.ds(0, size)], load_sem.at[place]
            ).start,
        )

    for number in range(LOADS):
        load(number)
    here.meet()
    other = here.device(here.at(), True)
    for part, key in keys:
        cell = here.at(*key)
        rows = pl.ds(*parts[part])
        spot = here.spot(cell)
        guarded(
            [here.inside(key[0])],
            remote(
                grads_ref.at[here.block(cell, True), rows], twin.at[spot, rows], twin_send,
                twin_recv.at[part, spot], other,
            ).start,
        )
    update.fetch()
    for end, shift in ((0, 1), (depth - 1, 0)):

        def clear():
            for line in (line_a, line_b):
                for row in range(6):
                    for target in range(depth):
                        place = line.at[row * (depth + 1) + target + shift]
                        place[...] = jnp.zeros(place.shape, place.dtype)

        pl.when(here.z == end)(clear)
    waits = []

    def task(number):
        part, key = keys[number]
        wave, local = part // 4, part % 4
        flat0, flat1, line = (flat0_a, flat1_a, line_a) if wave == 0 else (flat0_b, flat1_b, line_b)
        start, size = parts[part]
        rows = pl.ds(start, size)
        short = pl.ds(0, size)
        order = ORDERS[local]
        cell = here.at(*key)
        spot = here.spot(cell)
        present = here.inside(key[0])
        step = last_step(order, key)
        middle = order[1] == "z"
        cross = order[2]
        index0 = local * 2 * depth + cell[0] * 2 + (cell[1] if cross == "y" else cell[2])
        if middle:
            row = local * 2 + (cell[1] if order[0] == "x" else cell[2])
            index1 = local
        else:
            row = local + 2
            index1 = 2 + (local - 2) * depth + cell[0]
        line0 = row * (depth + 1) + cell[0]
        sent = row * depth + cell[0]
        base0, base1, base_line, base_sent = (wave * n for n in (8 * depth, 2 + 2 * depth, 6 * (depth + 1), 6 * depth))

        def run():
            mine = own.at[number % LOADS, short]
            target = twin.at[spot, rows]
            drain(mine, load_sem.at[number % LOADS])
            drain(target, twin_recv.at[part, spot])
            sources = [mine, target]
            for i in (2, 1, 0):
                if i <= step - 1 or (i == step and order[i] != "z"):
                    break
                if order[i] == "z":
                    ways = (1, 0)
                    if i == step:
                        ways = (1,) if key[0] > 0 else (0,)
                    for way in ways:
                        place = line.at[line0 + way, short]
                        arrive = functools.partial(drain, place, line_recv.at[base_line + line0 + way])
                        pl.when(here.z > 0 if way else here.z < depth - 1)(arrive)
                        sources.append(place)
                    if i == step:
                        break
                elif i == 2:
                    drain(flat0.at[index0, short], flat0_recv.at[base0 + index0])
                    sources.append(flat0.at[index0, short])
                else:
                    drain(flat1.at[index1, short], flat1_recv.at[base1 + index1])
                    sources.append(flat1.at[index1, short])
            if step < 0:
                add_rows(size, sums, start, sources)
                return
            add_rows(size, twin.at[spot], start, sources)
            dim = order[step]
            if dim == "z":
                way = 1 if key[0] > 0 else 0
                remote(
                    target, line.at[line0 + way, short], line_send.at[base_sent + sent],
                    line_recv.at[base_line + line0 + way], here.device(here.at(dz=1 if way else -1)),
                ).start()
                return
            device = here.device(here.at(dx=1) if dim == "x" else here.at(dy=1))
            if step == 2:
                remote(
                    target, flat0.at[index0, short], flat0_send.at[part], flat0_recv.at[base0 + index0], device
                ).start()
            else:
                remote(
                    target, flat1.at[index1, short], flat1_send.at[part], flat1_recv.at[base1 + index1], device
                ).start()

        guarded([present], run)
        if number + LOADS < len(keys):
            load(number + LOADS)
        if step >= 0 and order[step] == "z":
            waits.append(
                ([present], functools.partial(drain, twin.at[spot, rows], line_send.at[base_sent + sent]))
            )

    ready = max(n for n, (part, key) in enumerate(keys) if part < 4)
    steps = update.steps()
    taken = 0
    for number in range(len(keys)):
        task(number)
        if number >= ready:
            due = len(steps) * (number - ready + 1) // (len(keys) - ready)
            for step in steps[taken:due]:
                step()
            taken = due
    late_ref[...] = sums[early * T :, :]
    for conditions, action in waits:
        guarded(conditions, action)
    for part in range(8):
        rows = pl.ds(*parts[part])
        order = ORDERS[part % 4]
        sent = 1
        for i, dim in enumerate(order):
            if dim != "z":
                sem = flat0_send if i == 2 else flat1_send
                drain(twin.at[pl.ds(0, sent), rows], sem.at[part])
            sent *= depth if dim == "z" else 2
    drain(twin, twin_send)


def reduce_and_start(depth, grads, states):
    slots = states[0].shape[0]
    early = slots * 5 // 8
    parts = wave_rows(slots, early)
    rows = grads.shape[1]
    long_a, long_b = parts[3][1], parts[7][1]
    dma = pltpu.SemaphoreType.DMA
    bf, f32 = jnp.bfloat16, jnp.float32
    hbm = pl.BlockSpec(memory_space=pl.ANY)
    return pl.pallas_call(
        functools.partial(reduce_body, depth, slots, early, parts, wave_keys(depth, slots, early)),
        in_specs=[hbm] * (1 + INS),
        out_specs=[pl.BlockSpec(memory_space=pltpu.VMEM)] + [hbm] * INS,
        out_shape=[jax.ShapeDtypeStruct((rows - early * T, T), f32)]
        + [jax.ShapeDtypeStruct((early, T, T), f32)] * INS,
        scratch_shapes=[
            pltpu.VMEM((LOADS, max(long_a, long_b), T), bf),
            pltpu.VMEM((4 * depth, rows, T), bf),
            pltpu.VMEM((rows, T), f32),
            pltpu.VMEM((8 * depth, long_a, T), bf),
            pltpu.VMEM((8 * depth, long_b, T), bf),
            pltpu.VMEM((2 + 2 * depth, long_a, T), bf),
            pltpu.VMEM((2 + 2 * depth, long_b, T), bf),
            pltpu.VMEM((6 * (depth + 1), long_a, T), bf),
            pltpu.VMEM((6 * (depth + 1), long_b, T), bf),
            dma((LOADS,)),
            dma,
            dma((8, 4 * depth)),
            dma((8,)),
            dma((16 * depth,)),
            dma((8,)),
            dma((4 + 4 * depth,)),
            dma((12 * depth,)),
            dma((12 * (depth + 1),)),
        ]
        + update_scratch(early),
        compiler_params=pltpu.CompilerParams(
            collective_id=1, has_side_effects=True, vmem_limit_bytes=63 << 20
        ),
        name="reduce_and_start",
    )(grads, *states)


def grid_depth():
    towers = lax.axis_size("tower")
    if lax.axis_size("batch") != 2 or towers % 4 or towers > 16 or towers < 8:
        return None
    return towers // 4


def all_blocks(tiles, vec):
    depth = grid_depth()
    if depth is not None:
        return gather(depth, tiles, vec)
    own = jnp.concatenate([tiles.reshape(-1, T), vec.reshape(-1, T)], 0)
    own = jnp.pad(own, ((0, EXTRA - vec.size // T), (0, 0))).astype(jnp.bfloat16)
    return lax.all_gather(own, ("tower", "batch"), axis=0)


def per_device(
    image_rows,
    text_rows,
    caption_lengths,
    concat_cot,
    tile_slot,
    tile_weight,
    tile_first,
    tile_second,
    left_stat,
    right_stat,
    left_basis,
    right_basis,
    vec_weight,
    vec_first,
    vec_second,
):
    slots = tile_weight.shape[0]
    copies = all_blocks(tile_weight, vec_weight)
    projected, image_grad, grads = tower(
        False, slots, tile_slot, caption_lengths, image_rows, concat_cot, copies
    )
    concat, text_grad, grads = tower(
        True, slots, tile_slot, caption_lengths, text_rows, concat_cot, copies, (projected, grads)
    )
    states = (tile_weight, tile_first, tile_second, left_stat, right_stat, left_basis, right_basis)
    depth = grid_depth()
    if depth is not None:
        sums, *befores = reduce_and_start(depth, grads, states)
    else:
        sums = lax.psum_scatter(grads, ("tower", "batch"), scatter_dimension=0).astype(jnp.float32)
        befores = ()
    news = optimizer(sums, states, (vec_weight, vec_first, vec_second), befores)
    return (concat, image_grad, text_grad, *news)


def solution(mesh):
    return jax.shard_map(
        per_device,
        mesh=mesh,
        in_specs=(
            P(("tower", "batch"), None, None),
            P(("tower", "batch"), None, None),
            P(),
            P(("tower", "batch"), None, None),
            P(),
            P(("tower", "batch"), None, None),
            P(("tower", "batch"), None, None),
            P(("tower", "batch"), None, None),
            P(("tower", "batch"), None, None),
            P(("tower", "batch"), None, None),
            P(("tower", "batch"), None, None),
            P(("tower", "batch"), None, None),
            P(("tower", "batch"), None),
            P(("tower", "batch"), None),
            P(("tower", "batch"), None),
        ),
        out_specs=(
            P(("tower", "batch"), None, None),
            P(("tower", "batch"), None, None),
            P(("tower", "batch"), None, None),
            P(("tower", "batch"), None, None),
            P(("tower", "batch"), None, None),
            P(("tower", "batch"), None, None),
            P(("tower", "batch"), None, None),
            P(("tower", "batch"), None, None),
            P(("tower", "batch"), None, None),
            P(("tower", "batch"), None, None),
            P(("tower", "batch"), None),
            P(("tower", "batch"), None),
            P(("tower", "batch"), None),
        ),
        check_vma=False,
    )
```

```python
import functools
import heapq
import itertools

import jax
import jax.numpy as jnp
from jax import lax
from jax.experimental import pallas as pl
from jax.experimental.pallas import tpu as pltpu
from jax.sharding import PartitionSpec as P

BETA_ONE = 0.9
BETA_TWO = 0.95
EPSILON = 1e-08
RATE_MATRIX = 0.05
RATE_VECTOR = 0.6
DECAY = 0.01
STEP = 10
D = 768
FF = 3072
HEADS = 12
HEAD_DIM = 64
IMG = 197
TXT = 512
MMROWS = 2
T = 256
EXTRA = 16
VECS = 11 + FF // D
MASKED = -1000000000.0
NN = (((1,), (0,)), ((), ()))
NT = (((1,), (1,)), ((), ()))
TN = (((0,), (0,)), ((), ()))
KB = D // T
FB = FF // T
WIDE = 2 * T
SET = 2 * KB * WIDE // T


def mm(a, b, dims=NN):
    return lax.dot_general(a, b, dims, preferred_element_type=jnp.float32)


def rounded(v):
    return v.astype(jnp.bfloat16)


def stats(v):
    center = v - jnp.mean(v, -1, keepdims=True)
    inverse = lax.rsqrt(jnp.mean(center * center, -1, keepdims=True) + 1e-05)
    return center * inverse, inverse


def norm_back(grad, normed, inverse):
    return inverse * (
        grad
        - jnp.mean(grad, -1, keepdims=True)
        - normed * jnp.mean(grad * normed, -1, keepdims=True)
    )


def thirds(v):
    high = rounded(v)
    v = v - high.astype(jnp.float32)
    middle = rounded(v)
    return high, middle, rounded(v - middle.astype(jnp.float32))


def tower_body(is_text, rows, slots, slot_ref, length_ref, x_ref, cot_ref, copies, *rest):
    if is_text:
        zi_ref, _, cat_ref, dx_ref, grads = rest[:5]
        z_ref = None
    else:
        z_ref, dx_ref, grads = rest[:3]
        blank, blank_sem = rest[-2:]
        rest = rest[:-2]
    (wqkv, wo, wu, wd, wp, n1, n1t, qkv, qt, o, ot, a, n2, n2t, slope, h, ht, y, n3, n3t,
     cat, da, dqkv, logs, stage, vec_low, vec_all, bias_up, vec_out,
     wsem, stage_sem, vec_sem, vec_out_sem) = rest[5 if is_text else 3 :]
    dy = cat.at[pl.ds(0, rows)]
    dyb, dab, do, dot_, du = n3, n2, o, n3t, h
    first_tile = slot_ref.shape[0] // 2 if is_text else 0
    first_vec = VECS if is_text else 0
    real = TXT if is_text else IMG
    chunk = 64 if is_text else 16
    chunks = [(i * chunk, min((i + 1) * chunk, real)) for i in range(rows // chunk)]
    if is_text:
        length = length_ref[lax.axis_index("tower") * lax.axis_size("batch") + lax.axis_index("batch")]
    else:
        length = IMG
    tile_rows = slots * T

    def padded(value):
        short = chunk - value.shape[0]
        if short:
            value = jnp.concatenate([value, jnp.zeros((short, D), value.dtype)], 0)
        return value

    def x_of(c):
        return padded(x_ref[0, c[0] : c[1], :].astype(jnp.float32))

    def g_of(c):
        begin = c[0] + MMROWS + (IMG if is_text else 0)
        base = begin // 16 * 16
        end = min(-(-(begin + chunk) // 16) * 16, begin + c[1] - c[0])
        value = cot_ref[0, base:end, :].astype(jnp.float32)
        return padded(value[begin - base : begin - base + c[1] - c[0]])

    def at_slot(ref, slot):
        return ref.at[slot // slots, pl.ds(pl.multiple_of(slot % slots * T, T), T), :]

    extra = pl.ds(tile_rows, EXTRA)
    vec_count = VECS + MMROWS if is_text else VECS
    for i in range(vec_count):
        pltpu.make_async_copy(copies.at[first_vec + i, extra], vec_low.at[i], vec_sem).start()
    mats = [(wqkv, 0), (wqkv, D), (wqkv, 2 * D), (wo, 0), (wu, 0), (wd, 0), (wp, 0)]
    shapes = [(KB, KB)] * 4 + [(KB, FB), (FB, KB), (KB, KB)]
    starts = [0]
    for rb, cb in shapes:
        starts.append(starts[-1] + rb * cb)

    def load(which, sem):
        ref, shift = mats[which]
        rb, cb = shapes[which]

        def one(i, _):
            slot = slot_ref[first_tile + starts[which] + i]
            r, c = i // cb, i % cb
            pltpu.make_async_copy(
                at_slot(copies, slot),
                ref.at[pl.ds(pl.multiple_of(r * T, T), T), pl.ds(pl.multiple_of(shift + c * T, T), T)],
                wsem.at[sem],
            ).start()
            return 0

        lax.fori_loop(0, rb * cb, one, 0)

    def drain(ref, sem):
        pltpu.make_async_copy(ref, ref, sem).wait()

    for which, sem in enumerate((0, 0, 0, 1, 2, 3, 4)):
        load(which, sem)
    if not is_text:
        blank[...] = jnp.zeros(blank.shape, blank.dtype)

        def clear(i, _):
            pltpu.make_async_copy(blank, grads.at[i], blank_sem).start()
            return 0

        lax.fori_loop(0, grads.shape[0], clear, 0)

    def put(place, tiles):
        for n, (_, value) in enumerate(tiles):
            stage[place, n] = rounded(value)
        for n, (tile, _) in enumerate(tiles):
            slot = slot_ref[first_tile + tile]
            pltpu.make_async_copy(stage.at[place, n], at_slot(grads, slot), stage_sem.at[place]).start()

    def free(place, count):
        drain(stage.at[place, pl.ds(0, count)], stage_sem.at[place])

    def square(which, product):
        return [
            (starts[which] + r * KB + k, product[r * T : (r + 1) * T, k * T : (k + 1) * T])
            for r in range(KB)
            for k in range(KB)
        ]

    drain(vec_low.at[pl.ds(0, vec_count)], vec_sem)
    for i in range(vec_count):
        line = jnp.concatenate([vec_low[i, k : k + 1, :] for k in range(KB)], 1).astype(jnp.float32)
        vec_all[i : i + 1, :] = line
        if 7 <= i < 7 + FF // D:
            bias_up[:, (i - 7) * D : (i - 6) * D] = line

    def vec(i):
        return vec_all[i : i + 1, :]

    def vec_grad(i, line):
        line = rounded(line)
        parts = [line[:, k * T : (k + 1) * T] for k in range(KB)]
        parts.append(jnp.zeros((EXTRA - KB, T), jnp.bfloat16))
        vec_out[i] = jnp.concatenate(parts, 0)
        pltpu.make_async_copy(vec_out.at[i], grads.at[first_vec + i, extra], vec_out_sem).start()

    for c in chunks:
        normed, _ = stats(x_of(c))
        n1[c[0] : c[0] + chunk, :] = rounded(normed * vec(0) + vec(1))
    n1t[...] = n1[...].T
    drain(wqkv, wsem.at[0])
    scale = HEAD_DIM ** (-0.5)
    qkv[:, :D] = rounded((mm(n1[...], wqkv[:, :D]) + vec(2))) * jnp.asarray(scale, jnp.bfloat16)
    qkv[:, D : 2 * D] = rounded(mm(n1[...], wqkv[:, D : 2 * D]))
    qkv[:, 2 * D :] = rounded(mm(n1[...], wqkv[:, 2 * D :]) + vec(3))
    qt[...] = qkv[:, :D].T
    lane = lax.broadcasted_iota(jnp.int32, (rows, 2 * HEAD_DIM), 1)
    keys = lax.broadcasted_iota(jnp.int32, (rows, 2 * HEAD_DIM), 0)
    penalty = jnp.where(keys < length, 0.0, MASKED).astype(jnp.bfloat16)
    one = jnp.ones((rows, 2 * HEAD_DIM), jnp.bfloat16)
    zero = jnp.zeros((rows, 2 * HEAD_DIM), jnp.bfloat16)

    def pair_cols(p, base):
        return pl.ds(pl.multiple_of(base + p * 2 * HEAD_DIM, 2 * HEAD_DIM), 2 * HEAD_DIM)

    def beside(side, value, others):
        base = HEAD_DIM * (1 - side)
        result = zero
        for n, other in enumerate(others):
            result = jnp.where(lane == base + n, other, result)
        return jnp.where((lane < HEAD_DIM) if side == 0 else (lane >= HEAD_DIM), value, result)

    def attend(p, _):
        q = qkv[:, pair_cols(p, 0)]
        k = qkv[:, pair_cols(p, D)]
        v = qkv[:, pair_cols(p, 2 * D)]
        outs = []
        for side in range(2):
            s = mm(beside(side, q, [one]), beside(side, k, [penalty]), NT)
            top = jnp.max(s, -1, keepdims=True)
            s = jnp.exp(s - top)
            total = jnp.sum(s, -1, keepdims=True)
            logs[2 * p + side] = jnp.broadcast_to(top + jnp.log(total), (rows, 128))
            outs.append(mm(rounded(s * (1.0 / total)), v))
        o[:, pair_cols(p, 0)] = rounded(jnp.where(lane < HEAD_DIM, outs[0], outs[1]))
        return 0

    lax.fori_loop(0, HEADS // 2, attend, 0, unroll=True)
    ot[...] = o[...].T
    drain(wo, wsem.at[1])
    a[...] = mm(o[...], wo[...])
    for c in chunks:
        at = slice(c[0], c[0] + chunk)
        value = x_of(c) + (a[at, :] + vec(4))
        a[at, :] = value
        normed, _ = stats(value)
        n2[at, :] = rounded(normed * vec(5) + vec(6))
    n2t[...] = n2[...].T
    drain(wu, wsem.at[2])

    def up(i, _):
        cols = pl.ds(pl.multiple_of(i * WIDE, WIDE), WIDE)
        u = mm(n2[...], wu[:, cols]) + bias_up[:, cols]
        cumulative = 0.5 * (1.0 + lax.erf(u * 0.7071067811865476))
        hidden = rounded(u * cumulative)
        slope[:, cols] = cumulative + u * (jnp.exp(-0.5 * u * u) * 0.3989422804014327)
        h[:, cols] = hidden
        ht[cols, :] = hidden.T
        return 0

    lax.fori_loop(0, FF // WIDE, up, 0, unroll=2)
    drain(wd, wsem.at[3])
    y[...] = mm(h[...], wd[...])
    for c in chunks:
        at = slice(c[0], c[0] + chunk)
        value = a[at, :] + (y[at, :] + vec(11))
        y[at, :] = value
        normed, _ = stats(value)
        n3[at, :] = rounded(normed * vec(12) + vec(13))
    n3t[...] = n3[...].T
    drain(wp, wsem.at[4])
    keep = lax.broadcasted_iota(jnp.int32, (rows, 1), 0) < length
    z = jnp.where(keep, mm(n3[...], wp[...]) + vec(14), 0.0)
    if is_text:
        begin = MMROWS + IMG
        cat[:MMROWS, :] = vec_all[VECS : VECS + MMROWS, :]
        cat[MMROWS:begin, :] = zi_ref[0].astype(jnp.float32)
        cat[begin : begin + TXT, :] = z
        cat_ref[0] = rounded(cat[...])
    else:
        even = IMG // 16 * 16
        z_ref[0, :even, :] = rounded(z[:even])
        z_ref[0, even:IMG, :] = rounded(z[even:IMG])

    if not is_text:
        drain(grads, blank_sem)
    zeros = jnp.zeros((1, D), jnp.float32)
    total = zeros
    for c in chunks:
        at = slice(c[0], c[0] + chunk)
        g = jnp.where(keep[at, :], g_of(c), 0.0)
        total = total + jnp.sum(g, 0, keepdims=True)
        dyb[at, :] = rounded(g)
    vec_grad(14, total)
    put(1, square(6, mm(n3t[...], dyb[...])))
    dy[...] = mm(dyb[...], wp[...], NT)
    gain, shift, bias = zeros, zeros, zeros
    for c in chunks:
        at = slice(c[0], c[0] + chunk)
        normed, inverse = stats(y[at, :])
        g = dy[at, :]
        gain = gain + jnp.sum(g * normed, 0, keepdims=True)
        shift = shift + jnp.sum(g, 0, keepdims=True)
        g = norm_back(g * vec(12), normed, inverse)
        dy[at, :] = g
        low = rounded(g)
        dyb[at, :] = low
        bias = bias + jnp.sum(low.astype(jnp.float32), 0, keepdims=True)
    vec_grad(12, gain)
    vec_grad(13, shift)
    vec_grad(11, bias)

    def down(i, _):
        place = i % 2
        pl.when(i == 1)(functools.partial(free, 1, KB * KB))
        pl.when(i >= 2)(functools.partial(free, place, SET))
        cols = pl.ds(pl.multiple_of(i * WIDE, WIDE), WIDE)
        low = rounded(mm(dyb[...], wd[cols, :], NT) * slope[:, cols])
        du[:, cols] = low
        bias_up[:, cols] = jnp.sum(low.astype(jnp.float32), 0, keepdims=True)
        down_grad = mm(ht[cols, :], dyb[...])
        up_grad = mm(n2t[...], low)
        tiles = []
        for w in range(WIDE // T):
            band = slice(w * T, (w + 1) * T)
            number = i * (WIDE // T) + w
            for k in range(KB):
                other = slice(k * T, (k + 1) * T)
                tiles.append((starts[5] + number * KB + k, down_grad[band, other]))
                tiles.append((starts[4] + k * FB + number, up_grad[other, band]))
        put(place, tiles)
        return 0

    lax.fori_loop(0, FF // WIDE, down, 0, unroll=True)
    for i in range(FF // D):
        vec_grad(7 + i, bias_up[:, i * D : (i + 1) * D])
    da[...] = mm(du[...], wu[...], NT)
    gain, shift, bias = zeros, zeros, zeros
    for c in chunks:
        at = slice(c[0], c[0] + chunk)
        normed, inverse = stats(a[at, :])
        g = da[at, :]
        gain = gain + jnp.sum(g * normed, 0, keepdims=True)
        shift = shift + jnp.sum(g, 0, keepdims=True)
        g = dy[at, :] + norm_back(g * vec(5), normed, inverse)
        da[at, :] = g
        low = rounded(g)
        dab[at, :] = low
        bias = bias + jnp.sum(low.astype(jnp.float32), 0, keepdims=True)
    vec_grad(5, gain)
    vec_grad(6, shift)
    vec_grad(4, bias)
    dout = mm(dab[...], wo[...], NT)
    free(0, SET)
    put(0, square(3, mm(ot[...], dab[...])))
    low = rounded(dout)
    y[...] = low.astype(jnp.float32) * o[...].astype(jnp.float32)
    do[...] = low
    dot_[...] = low.T

    def attend_back(p, _):
        q = qkv[:, pair_cols(p, 0)]
        k = qkv[:, pair_cols(p, D)]
        v = qkv[:, pair_cols(p, 2 * D)]
        g = do[:, pair_cols(p, 0)]
        each = y[:, pair_cols(p, 0)]
        dqs, dks, dvs = [], [], []
        for side in range(2):
            half = pl.ds(pl.multiple_of((2 * p + side) * HEAD_DIM, HEAD_DIM), HEAD_DIM)
            mine = (lane < HEAD_DIM) if side == 0 else (lane >= HEAD_DIM)
            minus = [-one] * 3
            w = jnp.exp(
                mm(
                    beside(side, q, [one, *thirds(logs[2 * p + side])]),
                    beside(side, k, [penalty, *minus]),
                    NT,
                )
            )
            dvs.append(mm(dot_[half, :], rounded(w)))
            c = jnp.sum(jnp.where(mine, each, 0.0), -1, keepdims=True)
            dw = mm(
                beside(side, g, thirds(jnp.broadcast_to(c, (rows, 2 * HEAD_DIM)))),
                beside(side, v, minus),
                NT,
            )
            ds = rounded(w * dw)
            dqs.append(mm(ds, k))
            dks.append(mm(qt[half, :], ds))
        dqkv[:, pair_cols(p, 0)] = rounded(jnp.where(lane < HEAD_DIM, dqs[0], dqs[1]) * scale)
        dqkv[:, pair_cols(p, D)] = rounded(jnp.concatenate(dks, 0).T)
        dqkv[:, pair_cols(p, 2 * D)] = rounded(jnp.concatenate(dvs, 0).T)
        return 0

    lax.fori_loop(0, HEADS // 2, attend_back, 0, unroll=True)
    for m, number in ((0, 2), (2, 3)):
        vec_grad(number, jnp.sum(dqkv[:, m * D : (m + 1) * D].astype(jnp.float32), 0, keepdims=True))
    for m in range(3):
        free((1 + m) % 2, SET if m == 0 else KB * KB)
        put((1 + m) % 2, square(m, mm(n1t[...], dqkv[:, m * D : (m + 1) * D])))
    dy[...] = mm(dqkv[...], wqkv[...], NT)
    gain, shift = zeros, zeros
    for c in chunks:
        at = slice(c[0], c[0] + chunk)
        normed, inverse = stats(x_of(c))
        g = dy[at, :]
        gain = gain + jnp.sum(g * normed, 0, keepdims=True)
        shift = shift + jnp.sum(g, 0, keepdims=True)
        low = rounded(da[at, :] + norm_back(g * vec(0), normed, inverse))
        dx_ref[0, c[0] : c[1], :] = low[: c[1] - c[0]]
    vec_grad(0, gain)
    vec_grad(1, shift)
    if is_text:
        learned = cot_ref[0, :16, :].astype(jnp.float32)
        for i in range(MMROWS):
            vec_grad(VECS + i, learned[i : i + 1])
    free(0, KB * KB)
    free(1, KB * KB)
    drain(vec_out.at[pl.ds(0, vec_count)], vec_out_sem)


def tower(is_text, slots, tile_slot, lengths, x, cot, copies, before=()):
    bf, f32 = jnp.bfloat16, jnp.float32
    smem = pl.BlockSpec(memory_space=pltpu.SMEM)
    vmem = pl.BlockSpec(memory_space=pltpu.VMEM)
    hbm = pl.BlockSpec(memory_space=pl.ANY)
    dma = pltpu.SemaphoreType.DMA
    rows = -(-x.shape[1] // 16) * 16
    outs = [
        jax.ShapeDtypeStruct(cot.shape if is_text else x.shape, bf),
        jax.ShapeDtypeStruct(x.shape, bf),
        jax.ShapeDtypeStruct(copies.shape, bf),
    ]
    scratch = [
        pltpu.VMEM((D, 3 * D), bf), pltpu.VMEM((D, D), bf), pltpu.VMEM((D, FF), bf),
        pltpu.VMEM((FF, D), bf), pltpu.VMEM((D, D), bf),
        pltpu.VMEM((rows, D), bf), pltpu.VMEM((D, rows), bf),
        pltpu.VMEM((rows, 3 * D), bf), pltpu.VMEM((D, rows), bf),
        pltpu.VMEM((rows, D), bf), pltpu.VMEM((D, rows), bf),
        pltpu.VMEM((rows, D), f32),
        pltpu.VMEM((rows, D), bf), pltpu.VMEM((D, rows), bf),
        pltpu.VMEM((rows, FF), f32),
        pltpu.VMEM((rows, FF), bf), pltpu.VMEM((FF, rows), bf),
        pltpu.VMEM((rows, D), f32),
        pltpu.VMEM((rows, D), bf), pltpu.VMEM((D, rows), bf),
        pltpu.VMEM((cot.shape[1] if is_text else rows, D), f32),
        pltpu.VMEM((rows, D), f32),
        pltpu.VMEM((rows, 3 * D), bf),
        pltpu.VMEM((HEADS, rows, 128), f32),
        pltpu.VMEM((2, SET, T, T), bf),
        pltpu.VMEM((VECS + MMROWS, EXTRA, T), bf), pltpu.VMEM((VECS + MMROWS, D), f32),
        pltpu.VMEM((1, FF), f32), pltpu.VMEM((VECS + MMROWS, EXTRA, T), bf),
        dma((5,)), dma((2,)), dma, dma,
    ]
    if not is_text:
        scratch += [pltpu.VMEM((slots * T + EXTRA, T), bf), dma]
    return pl.pallas_call(
        functools.partial(tower_body, is_text, rows, slots),
        in_specs=[smem, smem, vmem, vmem, hbm] + ([vmem, hbm] if is_text else []),
        out_specs=[vmem, vmem, hbm],
        out_shape=outs,
        scratch_shapes=scratch,
        input_output_aliases={6: 2} if is_text else {},
        compiler_params=pltpu.CompilerParams(vmem_limit_bytes=63 << 20),
        name="text_tower" if is_text else "image_tower",
    )(tile_slot, lengths, x, cot, copies, *before)


def split(x):
    hi = x.astype(jnp.bfloat16)
    lo = (x - hi.astype(jnp.float32)).astype(jnp.bfloat16)
    return hi, lo


def dot(a, b, dims):
    return lax.dot_general(a, b, dims, preferred_element_type=jnp.float32)


def mm3(a, b, dims):
    return dot(a[0], b[0], dims) + (dot(a[0], b[1], dims) + dot(a[1], b[0], dims))


def adam_step(first, second):
    return (
        first
        / (1.0 - BETA_ONE**STEP)
        / (jnp.sqrt(second / (1.0 - BETA_TWO**STEP)) + EPSILON)
    )


B = 64
GROUP = 8
INS, OUTS = 7, 5


def eliminate_group(diag, jg):
    count = diag.shape[0]
    shape = (count, GROUP, 2 * B)
    subs = lax.broadcasted_iota(jnp.int32, shape, 1)
    top = slice(jg * GROUP, jg * GROUP + GROUP)
    tile = diag[:, top, :]
    for jj in range(0, GROUP, 2):
        j = jg * GROUP + jj
        first = jnp.broadcast_to(tile[:, :, j : j + 1], shape)
        second = jnp.broadcast_to(tile[:, :, j + 1 : j + 2], shape)
        p00, p01, p11 = first[:, jj : jj + 1], second[:, jj : jj + 1], second[:, jj + 1 : jj + 2]
        r0, r1 = tile[:, jj : jj + 1], tile[:, jj + 1 : jj + 2]
        inverse = 1.0 / (p00 * p11 - p01 * p01)
        cross = p01 * inverse
        t0 = (p11 * inverse) * r0 - cross * r1
        t1 = (p00 * inverse) * r1 - cross * r0
        lower = tile - first * t0 - second * t1
        tile = jnp.where(subs > jj + 1, lower, jnp.where(subs == jj + 1, tile - (p01 / p00) * r0, tile))
        if jg < B // GROUP - 1:
            rest = diag[:, jg * GROUP + GROUP :, :]
            diag[:, jg * GROUP + GROUP :, :] = (
                rest - rest[:, :, j : j + 1] * t0 - rest[:, :, j + 1 : j + 2] * t1
            )
    diag[:, top, :] = tile


class Update:
    def __init__(self, slots, begin, shift, sums, ins, outs, inbuf, outbuf, qbuf, work, diag, in_sem, out_sem, q_sem):
        self.slots, self.begin, self.shift = slots, begin, shift
        self.sums, self.ins, self.outs = sums, ins, outs
        self.inbuf, self.outbuf, self.qbuf, self.work, self.diag = inbuf, outbuf, qbuf, work, diag
        self.in_sem, self.out_sem, self.q_sem = in_sem, out_sem, q_sem

    def fetch(self):
        for s in range(self.slots):
            for n in range(INS):
                pltpu.make_async_copy(self.ins[n].at[self.begin + s], self.inbuf.at[s, n], self.in_sem.at[s]).start()

    def refine(self, s):
        pltpu.make_async_copy(self.inbuf.at[s], self.inbuf.at[s], self.in_sem.at[s]).wait()
        place = s % 2
        if s >= 2:
            pltpu.make_async_copy(self.outbuf.at[place], self.outbuf.at[place], self.out_sem.at[place]).wait()
        w, m1, m2, ls, rs, lb, rb = (self.inbuf.at[s, n] for n in range(INS))
        wn, m1n, m2n, lsn, rsn = (self.outbuf.at[place, n] for n in range(OUTS))
        e = split(self.sums[s * T : (s + 1) * T, :])
        ql = split(lb[...])
        qr = split(rb[...])
        left = BETA_TWO * ls[...] + (1.0 - BETA_TWO) * mm3(e, e, NT)
        right = BETA_TWO * rs[...] + (1.0 - BETA_TWO) * mm3(e, e, TN)
        lsn[...] = left
        rsn[...] = right
        turned = mm3(split(mm3(ql, e, TN)), qr, NN)
        first = BETA_ONE * m1[...] + (1.0 - BETA_ONE) * turned
        second = BETA_TWO * m2[...] + (1.0 - BETA_TWO) * turned * turned
        m1n[...] = first
        m2n[...] = second
        direction = mm3(split(mm3(ql, split(adam_step(first, second)), NN)), qr, NT)
        old = w[...]
        wn[...] = old - RATE_MATRIX * (direction + DECAY * old)
        for n in range(OUTS):
            pltpu.make_async_copy(self.outbuf.at[place, n], self.outs[n].at[self.shift + s], self.out_sem.at[place]).start()
        for side, (basis, stat) in enumerate(((ql, left), (qr, right))):
            y = mm3(basis, split(stat), TN)
            y = y * lax.rsqrt(jnp.sum(y * y, axis=1, keepdims=True))
            self.work[2 * s + side, :, T:] = y
            y = split(y)
            self.work[2 * s + side, :, :T] = mm3(y, y, NT)

    def load(self, k):
        low = k * B
        edge = low // (2 * B) * 2 * B
        row = lax.broadcasted_iota(jnp.int32, (B, 2 * B), 0)
        lane = lax.broadcasted_iota(jnp.int32, (B, 2 * B), 1)
        for m in range(2 * self.slots):
            block = self.work[m, low : low + B, edge : edge + 2 * B]
            if low % (2 * B):
                block = pltpu.roll(block, B, 1)
            self.diag[m] = jnp.where(lane < B, block, jnp.where(lane == row + B, 1.0, 0.0))

    def products(self, k, begin, end):
        low = k * B
        edge = low // (2 * B) * 2 * B
        row = lax.broadcasted_iota(jnp.int32, (B, 2 * B), 0)
        lane = lax.broadcasted_iota(jnp.int32, (B, 2 * B), 1)
        work = self.work

        def one(m):
            d = self.diag[m]
            pivots = jnp.sum(jnp.where(lane == row, d, 0.0), axis=1, keepdims=True)
            high, rest = split(d[:, B:] * lax.rsqrt(pivots))
            inverse = jnp.concatenate([high, rest, high], 1)
            high, rest = split(work[m, low : low + B, edge:])
            new = dot(inverse, jnp.concatenate([high, high, rest], 0), NN)
            work[m, low : low + B, edge:] = new
            if low + B < T:
                high, rest = split(new)
                after = low + B - edge
                start = (low + B) // (2 * B) * 2 * B
                left = jnp.concatenate([high, rest, high], 0)[:, after : T - edge]
                right = jnp.concatenate([high, high, rest], 0)[:, start - edge :]
                work[m, low + B :, start:] = work[m, low + B :, start:] - dot(left, right, TN)

        def pair(i, _):
            one(begin + 2 * i)
            one(begin + 2 * i + 1)
            return 0

        lax.fori_loop(0, (end - begin) // 2, pair, 0, unroll=True)

    def finish(self, s):
        for side in range(2):
            if s:
                pltpu.make_async_copy(self.qbuf.at[side], self.qbuf.at[side], self.q_sem.at[side]).wait()
            self.qbuf[side] = self.work[2 * s + side, :, T:].T
            pltpu.make_async_copy(self.qbuf.at[side], self.outs[OUTS + side].at[self.shift + s], self.q_sem.at[side]).start()

    def close(self):
        for side in range(2):
            pltpu.make_async_copy(self.qbuf.at[side], self.qbuf.at[side], self.q_sem.at[side]).wait()
        for place in range(min(2, self.slots)):
            pltpu.make_async_copy(self.outbuf.at[place], self.outbuf.at[place], self.out_sem.at[place]).wait()

    def steps(self):
        result = [functools.partial(self.refine, s) for s in range(self.slots)]
        for k in range(T // B):
            result.append(functools.partial(self.load, k))
            result += [functools.partial(eliminate_group, self.diag, jg) for jg in range(B // GROUP)]
            middle = self.slots // 2 * 2
            result += [functools.partial(self.products, k, a, b) for a, b in ((0, middle), (middle, 2 * self.slots)) if a < b]
        result += [functools.partial(self.finish, s) for s in range(self.slots)]
        result.append(self.close)
        return result


def update_scratch(slots):
    f32 = jnp.float32
    dma = pltpu.SemaphoreType.DMA
    return [
        pltpu.VMEM((slots, INS, T, T), f32),
        pltpu.VMEM((2, OUTS, T, T), f32),
        pltpu.VMEM((2, T, T), f32),
        pltpu.VMEM((2 * slots, T, 2 * T), f32),
        pltpu.VMEM((2 * slots, B, 2 * B), f32),
        dma((slots,)),
        dma((2,)),
        dma((2,)),
    ]


def rest_body(total, done, sums_ref, v_refs, ins, befores, outs, v_outs, scratch, passing, passing_sem):
    update = Update(total - done, done, done, sums_ref, ins, outs, *scratch)
    update.fetch()
    arrivals = [
        pltpu.make_async_copy(before, passing.at[n], passing_sem.at[0, n]) for n, before in enumerate(befores)
    ]
    departures = [
        pltpu.make_async_copy(passing.at[n], outs[n].at[pl.ds(0, done)], passing_sem.at[1, n])
        for n in range(len(befores))
    ]
    for copy in arrivals:
        copy.start()
    vw_ref, v1_ref, v2_ref = v_refs
    vwn_ref, v1n_ref, v2n_ref = v_outs
    for k in range(vw_ref.shape[1] // T):
        cols = slice(k * T, (k + 1) * T)
        row = (total - done) * T + k
        g = sums_ref[row : row + 1, :]
        first = BETA_ONE * v1_ref[:, cols] + (1.0 - BETA_ONE) * g
        second = BETA_TWO * v2_ref[:, cols] + (1.0 - BETA_TWO) * g * g
        v1n_ref[:, cols] = first
        v2n_ref[:, cols] = second
        vwn_ref[:, cols] = vw_ref[:, cols] - RATE_VECTOR * adam_step(first, second)
    for number, step in enumerate(update.steps()):
        step()
        if number == total - done - 1:
            for arrival, departure in zip(arrivals, departures):
                arrival.wait()
                departure.start()
    for copy in departures:
        copy.wait()


def optimizer(sums, states, vectors, befores=()):
    total = states[0].shape[0]
    done = befores[0].shape[0] if befores else 0
    hbm = pl.BlockSpec(memory_space=pl.ANY)
    vmem = pl.BlockSpec(memory_space=pltpu.VMEM)
    f32 = jnp.float32
    count = len(befores)

    def body(*refs):
        sums_ref, v_refs, refs = refs[0], refs[1:4], refs[4:]
        ins, befores, refs = refs[:INS], refs[INS : INS + count], refs[INS + count :]
        outs, v_outs, refs = refs[:INS], refs[INS : INS + 3], refs[INS + 3 :]
        rest_body(total, done, sums_ref, v_refs, ins, befores, outs, v_outs, refs[:-2], *refs[-2:])

    return pl.pallas_call(
        body,
        in_specs=[vmem] * 4 + [hbm] * (INS + count),
        out_specs=[hbm] * INS + [vmem] * 3,
        out_shape=[jax.ShapeDtypeStruct(v.shape, f32) for v in (*states, *vectors)],
        scratch_shapes=update_scratch(total - done)
        + [pltpu.VMEM((INS, max(done, 1), T, T), f32), pltpu.SemaphoreType.DMA((2, INS))],
        compiler_params=pltpu.CompilerParams(vmem_limit_bytes=60 << 20),
        name="optimizer",
    )(sums, *vectors, *states, *befores)


ORDERS = ("xzy", "yzx", "zxy", "zyx")


def part_rows(slots):
    quarter = slots * T // 4
    sizes = [quarter, quarter, quarter, quarter + EXTRA]
    return [(sum(sizes[:i]), sizes[i]) for i in range(4)]


def last_step(order, key):
    away = {"z": key[0], "x": key[1], "y": key[2]}
    steps = [i for i in range(3) if away[order[i]]]
    return steps[-1] if steps else -1


def plan_of(depth):
    cells = list(itertools.product(range(depth), range(2), range(2)))
    queues, free, events, arrived = {}, {}, [], {}
    ticket = itertools.count()

    def onward(cell, part, source, now):
        order = ORDERS[part]
        key = (source[0] - cell[0], source[1] ^ cell[1], source[2] ^ cell[2])
        step = last_step(order, key)
        for i in range(3):
            z, x, y = cell
            if order[i] == "z":
                if i > step:
                    ways = (1, -1)
                elif i == step:
                    ways = (1,) if key[0] < 0 else (-1,)
                else:
                    ways = ()
                targets = [(z + w, x, y) for w in ways if 0 <= z + w < depth]
            elif i > step:
                targets = [(z, 1 - x, y) if order[i] == "x" else (z, x, 1 - y)]
            else:
                targets = []
            for target in targets:
                heapq.heappush(queues.setdefault((cell, target), []), (now, next(ticket), part, source))
                heapq.heappush(events, (now, next(ticket), 0, (cell, target)))

    for cell in cells:
        for part in range(4):
            onward(cell, part, cell, 0.0)
    while events:
        now, _, kind, what = heapq.heappop(events)
        if kind == 0:
            if queues[what] and free.get(what, 0.0) <= now:
                _, _, part, source = heapq.heappop(queues[what])
                free[what] = now + 2.0
                heapq.heappush(events, (now + 2.0, next(ticket), 0, what))
                heapq.heappush(events, (now + 2.5, next(ticket), 1, (what[1], part, source)))
        else:
            cell, part, source = what
            key = (part, source[0] - cell[0], source[1] ^ cell[1], source[2] ^ cell[2])
            arrived.setdefault(key, []).append(now)
            onward(cell, part, source, now)
    times = {k: sum(v) / len(v) for k, v in arrived.items()}
    fixed = {}

    def time_of(key):
        if key not in fixed:
            part, dz, dx, dy = key
            step = last_step(ORDERS[part], key[1:])
            if step < 0:
                return 0.0
            dim = ORDERS[part][step]
            if dim == "z":
                parent = (part, dz - (1 if dz > 0 else -1), dx, dy)
            else:
                parent = (part, dz, 0 if dim == "x" else dx, 0 if dim == "y" else dy)
            fixed[key] = max(times[key], time_of(parent) + 0.01)
        return fixed[key]

    return sorted((time_of(k), k) for k in times)


class Place:
    def __init__(self, depth):
        tower = lax.axis_index("tower")
        self.depth = depth
        self.core = tower % 2
        self.x = tower // 2 % 2
        self.z = tower // 4
        self.y = lax.axis_index("batch")

    def at(self, dz=0, dx=0, dy=0):
        return (
            self.z + dz,
            1 - self.x if dx else self.x,
            1 - self.y if dy else self.y,
        )

    def device(self, cell, other=False):
        core = 1 - self.core if other else self.core
        return ((cell[0] * 2 + cell[1]) * 2 + core, cell[2])

    def block(self, cell, other=False):
        core = 1 - self.core if other else self.core
        return ((cell[0] * 2 + cell[1]) * 2 + core) * 2 + cell[2]

    def spot(self, cell):
        return (cell[0] * 2 + cell[1]) * 2 + cell[2]

    def inside(self, dz):
        if dz == 0:
            return None
        return self.z + dz < self.depth if dz > 0 else self.z + dz >= 0

    def meet(self):
        barrier = pltpu.get_barrier_semaphore()

        def greet(device):
            pl.semaphore_signal(barrier, inc=1, device_id=device, device_id_type=pl.DeviceIdType.MESH)

        greet(self.device(self.at(), True))
        greet(self.device(self.at(dx=1)))
        greet(self.device(self.at(dy=1)))
        for way in (1, -1):
            pl.when(self.inside(way))(functools.partial(greet, self.device(self.at(dz=way))))
        low = (self.z > 0).astype(jnp.int32)
        high = (self.z < self.depth - 1).astype(jnp.int32)
        pl.semaphore_wait(barrier, 3 + low + high)


def guarded(conditions, action):
    conditions = [c for c in conditions if c is not None]
    if not conditions:
        action()
    else:
        both = conditions[0]
        for c in conditions[1:]:
            both = jnp.logical_and(both, c)
        pl.when(both)(action)


def remote(src, dst, send, recv, device):
    return pltpu.make_async_remote_copy(
        src_ref=src, dst_ref=dst, send_sem=send, recv_sem=recv,
        device_id=device, device_id_type=pl.DeviceIdType.MESH,
    )


def drain(ref, sem):
    pltpu.make_async_copy(ref, ref, sem).wait()


def gather_body(
    depth, parts, plan, tiles_ref, vec_ref, out_ref, wide, own_ref, wide_sem, own_sem, z_sem, flat_sem, twin_sem, recv_sem
):
    slots = tiles_ref.shape[0]
    for slot in range(slots):
        pltpu.make_async_copy(tiles_ref.at[slot], wide.at[slot], wide_sem.at[slot]).start()
    here = Place(depth)
    here.meet()
    line = vec_ref[...].astype(jnp.bfloat16)
    pieces = [line[:, k * T : (k + 1) * T] for k in range(line.shape[1] // T)]
    pieces.append(jnp.zeros((EXTRA - len(pieces), T), jnp.bfloat16))
    own_ref[slots * T :, :] = jnp.concatenate(pieces, 0)
    for slot in range(slots):
        drain(wide.at[slot], wide_sem.at[slot])
        own_ref[slot * T : (slot + 1) * T, :] = wide[slot].astype(jnp.bfloat16)
    mine = pltpu.make_async_copy(own_ref, out_ref.at[here.block(here.at())], own_sem)
    mine.start()
    waits = []

    def handle(part, key):
        start, size = parts[part]
        rows = pl.ds(start, size)
        order = ORDERS[part]
        step = last_step(order, key)
        cell = here.at(*key)
        present = here.inside(key[0])
        block = here.block(cell)
        spot = here.spot(cell)
        place = out_ref.at[block, rows]
        source = own_ref.at[rows] if step < 0 else place

        def arrive():
            if step >= 0:
                drain(place, recv_sem.at[part, spot])

        guarded([present], arrive)
        for i in range(3):
            dim = order[i]
            if dim == "z":
                ways = (1, -1) if i > step else ()
                if i == step:
                    ways = (1,) if key[0] < 0 else (-1,)
                for way in ways:
                    sem = z_sem.at[part, spot, 0 if way > 0 else 1]
                    copy = remote(source, place, sem, recv_sem.at[part, spot], here.device(here.at(dz=way)))
                    conditions = [present, here.inside(way)]
                    guarded(conditions, copy.start)
                    waits.append((conditions, copy.wait_send))
            elif i > step:
                target = here.at(dx=1) if dim == "x" else here.at(dy=1)
                guarded(
                    [present],
                    remote(
                        source, place, flat_sem.at[part, 0 if dim == "x" else 1],
                        recv_sem.at[part, spot], here.device(target),
                    ).start,
                )
        guarded(
            [present],
            remote(source, place, twin_sem.at[0], twin_sem.at[1], here.device(here.at(), True)).start,
        )

    for part in range(4):
        handle(part, (0, 0, 0))
    for part, *key in plan:
        handle(part, tuple(key))
    for conditions, action in waits:
        guarded(conditions, action)
    for part in range(4):
        rows = pl.ds(*parts[part])
        sent = 1
        for dim in ORDERS[part]:
            if dim != "z":
                drain(out_ref.at[pl.ds(0, sent), rows], flat_sem.at[part, 0 if dim == "x" else 1])
            sent *= depth if dim == "z" else 2
    mine.wait()
    half = pl.ds(0, 4 * depth)
    drain(out_ref.at[half], twin_sem.at[0])
    drain(out_ref.at[half], twin_sem.at[1])


def gather(depth, tiles, vec):
    slots = tiles.shape[0]
    parts = part_rows(slots)
    rows = slots * T + EXTRA
    hbm = pl.BlockSpec(memory_space=pl.ANY)
    dma = pltpu.SemaphoreType.DMA
    return pl.pallas_call(
        functools.partial(gather_body, depth, parts, [key for _, key in plan_of(depth)]),
        in_specs=[hbm, pl.BlockSpec(memory_space=pltpu.VMEM)],
        out_specs=hbm,
        out_shape=jax.ShapeDtypeStruct((8 * depth, rows, T), jnp.bfloat16),
        scratch_shapes=[
            pltpu.VMEM(tiles.shape, jnp.float32),
            pltpu.VMEM((rows, T), jnp.bfloat16),
            dma((slots,)),
            dma,
            dma((4, 4 * depth, 2)),
            dma((4, 2)),
            dma((2,)),
            dma((4, 4 * depth)),
        ],
        compiler_params=pltpu.CompilerParams(
            collective_id=0, has_side_effects=True, vmem_limit_bytes=60 << 20
        ),
        name="gather",
    )(tiles, vec)


def add_rows(size, target, start, sources):
    def piece(at, count):
        total = sources[0][pl.ds(at, count), :].astype(jnp.float32)
        for source in sources[1:]:
            total = total + source[pl.ds(at, count), :].astype(jnp.float32)
        target[pl.ds(start + at, count), :] = total.astype(target.dtype)

    whole = size // 128

    def body(i, _):
        piece(pl.multiple_of(i * 128, 128), 128)
        return 0

    lax.fori_loop(0, whole, body, 0)
    if size % 128:
        piece(whole * 128, size % 128)


LOADS = 8


def wave_rows(slots, early):
    result = []
    for begin, count, extra in ((0, early, 0), (early * T, slots - early, EXTRA)):
        size = count * T // 4
        sizes = [size, size, size, size + extra]
        result += [(begin + sum(sizes[:i]), sizes[i]) for i in range(4)]
    return result


def wave_keys(depth, slots, early):
    timed = plan_of(depth)
    end = timed[-1][0]
    share = early / slots
    result = []
    for wave in range(2):
        for when, (part, *key) in timed + [(0.0, (part, 0, 0, 0)) for part in range(4)]:
            spent = end - when
            at = spent * share if wave == 0 else end * (share - 0.06) + spent * (1 - share)
            result.append((at, wave, -len(result), 4 * wave + part, tuple(key)))
    return [(part, key) for _, _, _, part, key in sorted(result)]


def reduce_body(depth, slots, early, parts, keys, grads_ref, *refs):
    ins, refs = refs[:INS], refs[INS:]
    late_ref, refs = refs[0], refs[1:]
    outs, refs = refs[:INS], refs[INS:]
    (own, twin, sums, flat0_a, flat0_b, flat1_a, flat1_b, line_a, line_b,
     load_sem, twin_send, twin_recv, flat0_send, flat0_recv, flat1_send, flat1_recv, line_send, line_recv) = refs[:18]
    update = Update(early, 0, 0, sums, ins, outs, *refs[18:])
    here = Place(depth)

    def load(number):
        part, key = keys[number]
        cell = here.at(*key)
        start, size = parts[part]
        place = number % LOADS
        guarded(
            [here.inside(key[0])],
            pltpu.make_async_copy(
                grads_ref.at[here.block(cell), pl.ds(start, size)], own.at[place, pl.ds(0, size)], load_sem.at[place]
            ).start,
        )

    for number in range(LOADS):
        load(number)
    here.meet()
    other = here.device(here.at(), True)
    for part, key in keys:
        cell = here.at(*key)
        rows = pl.ds(*parts[part])
        spot = here.spot(cell)
        guarded(
            [here.inside(key[0])],
            remote(
                grads_ref.at[here.block(cell, True), rows], twin.at[spot, rows], twin_send,
                twin_recv.at[part, spot], other,
            ).start,
        )
    update.fetch()
    for end, shift in ((0, 1), (depth - 1, 0)):

        def clear():
            for line in (line_a, line_b):
                for row in range(6):
                    for target in range(depth):
                        place = line.at[row * (depth + 1) + target + shift]
                        place[...] = jnp.zeros(place.shape, place.dtype)

        pl.when(here.z == end)(clear)
    waits = []

    def task(number):
        part, key = keys[number]
        wave, local = part // 4, part % 4
        flat0, flat1, line = (flat0_a, flat1_a, line_a) if wave == 0 else (flat0_b, flat1_b, line_b)
        start, size = parts[part]
        rows = pl.ds(start, size)
        short = pl.ds(0, size)
        order = ORDERS[local]
        cell = here.at(*key)
        spot = here.spot(cell)
        present = here.inside(key[0])
        step = last_step(order, key)
        middle = order[1] == "z"
        cross = order[2]
        index0 = local * 2 * depth + cell[0] * 2 + (cell[1] if cross == "y" else cell[2])
        if middle:
            row = local * 2 + (cell[1] if order[0] == "x" else cell[2])
            index1 = local
        else:
            row = local + 2
            index1 = 2 + (local - 2) * depth + cell[0]
        line0 = row * (depth + 1) + cell[0]
        sent = row * depth + cell[0]
        base0, base1, base_line, base_sent = (wave * n for n in (8 * depth, 2 + 2 * depth, 6 * (depth + 1), 6 * depth))

        def run():
            mine = own.at[number % LOADS, short]
            target = twin.at[spot, rows]
            drain(mine, load_sem.at[number % LOADS])
            drain(target, twin_recv.at[part, spot])
            sources = [mine, target]
            for i in (2, 1, 0):
                if i <= step - 1 or (i == step and order[i] != "z"):
                    break
                if order[i] == "z":
                    ways = (1, 0)
                    if i == step:
                        ways = (1,) if key[0] > 0 else (0,)
                    for way in ways:
                        place = line.at[line0 + way, short]
                        arrive = functools.partial(drain, place, line_recv.at[base_line + line0 + way])
                        pl.when(here.z > 0 if way else here.z < depth - 1)(arrive)
                        sources.append(place)
                    if i == step:
                        break
                elif i == 2:
                    drain(flat0.at[index0, short], flat0_recv.at[base0 + index0])
                    sources.append(flat0.at[index0, short])
                else:
                    drain(flat1.at[index1, short], flat1_recv.at[base1 + index1])
                    sources.append(flat1.at[index1, short])
            if step < 0:
                add_rows(size, sums, start, sources)
                return
            add_rows(size, twin.at[spot], start, sources)
            dim = order[step]
            if dim == "z":
                way = 1 if key[0] > 0 else 0
                remote(
                    target, line.at[line0 + way, short], line_send.at[base_sent + sent],
                    line_recv.at[base_line + line0 + way], here.device(here.at(dz=1 if way else -1)),
                ).start()
                return
            device = here.device(here.at(dx=1) if dim == "x" else here.at(dy=1))
            if step == 2:
                remote(
                    target, flat0.at[index0, short], flat0_send.at[part], flat0_recv.at[base0 + index0], device
                ).start()
            else:
                remote(
                    target, flat1.at[index1, short], flat1_send.at[part], flat1_recv.at[base1 + index1], device
                ).start()

        guarded([present], run)
        if number + LOADS < len(keys):
            load(number + LOADS)
        if step >= 0 and order[step] == "z":
            waits.append(
                ([present], functools.partial(drain, twin.at[spot, rows], line_send.at[base_sent + sent]))
            )

    ready = max(n for n, (part, key) in enumerate(keys) if part < 4)
    steps = update.steps()
    taken = 0
    for number in range(len(keys)):
        task(number)
        if number >= ready:
            due = len(steps) * (number - ready + 1) // (len(keys) - ready)
            for step in steps[taken:due]:
                step()
            taken = due
    late_ref[...] = sums[early * T :, :]
    for conditions, action in waits:
        guarded(conditions, action)
    for part in range(8):
        rows = pl.ds(*parts[part])
        order = ORDERS[part % 4]
        sent = 1
        for i, dim in enumerate(order):
            if dim != "z":
                sem = flat0_send if i == 2 else flat1_send
                drain(twin.at[pl.ds(0, sent), rows], sem.at[part])
            sent *= depth if dim == "z" else 2
    drain(twin, twin_send)


def reduce_and_start(depth, grads, states):
    slots = states[0].shape[0]
    early = slots * 5 // 8
    parts = wave_rows(slots, early)
    rows = grads.shape[1]
    long_a, long_b = parts[3][1], parts[7][1]
    dma = pltpu.SemaphoreType.DMA
    bf, f32 = jnp.bfloat16, jnp.float32
    hbm = pl.BlockSpec(memory_space=pl.ANY)
    return pl.pallas_call(
        functools.partial(reduce_body, depth, slots, early, parts, wave_keys(depth, slots, early)),
        in_specs=[hbm] * (1 + INS),
        out_specs=[pl.BlockSpec(memory_space=pltpu.VMEM)] + [hbm] * INS,
        out_shape=[jax.ShapeDtypeStruct((rows - early * T, T), f32)]
        + [jax.ShapeDtypeStruct((early, T, T), f32)] * INS,
        scratch_shapes=[
            pltpu.VMEM((LOADS, max(long_a, long_b), T), bf),
            pltpu.VMEM((4 * depth, rows, T), bf),
            pltpu.VMEM((rows, T), f32),
            pltpu.VMEM((8 * depth, long_a, T), bf),
            pltpu.VMEM((8 * depth, long_b, T), bf),
            pltpu.VMEM((2 + 2 * depth, long_a, T), bf),
            pltpu.VMEM((2 + 2 * depth, long_b, T), bf),
            pltpu.VMEM((6 * (depth + 1), long_a, T), bf),
            pltpu.VMEM((6 * (depth + 1), long_b, T), bf),
            dma((LOADS,)),
            dma,
            dma((8, 4 * depth)),
            dma((8,)),
            dma((16 * depth,)),
            dma((8,)),
            dma((4 + 4 * depth,)),
            dma((12 * depth,)),
            dma((12 * (depth + 1),)),
        ]
        + update_scratch(early),
        compiler_params=pltpu.CompilerParams(
            collective_id=1, has_side_effects=True, vmem_limit_bytes=63 << 20
        ),
        name="reduce_and_start",
    )(grads, *states)


def grid_depth():
    towers = lax.axis_size("tower")
    if lax.axis_size("batch") != 2 or towers % 4 or towers > 16 or towers < 8:
        return None
    return towers // 4


def all_blocks(tiles, vec):
    depth = grid_depth()
    if depth is not None:
        return gather(depth, tiles, vec)
    own = jnp.concatenate([tiles.reshape(-1, T), vec.reshape(-1, T)], 0)
    own = jnp.pad(own, ((0, EXTRA - vec.size // T), (0, 0))).astype(jnp.bfloat16)
    return lax.all_gather(own, ("tower", "batch"), axis=0)


def per_device(
    image_rows,
    text_rows,
    caption_lengths,
    concat_cot,
    tile_slot,
    tile_weight,
    tile_first,
    tile_second,
    left_stat,
    right_stat,
    left_basis,
    right_basis,
    vec_weight,
    vec_first,
    vec_second,
):
    slots = tile_weight.shape[0]
    copies = all_blocks(tile_weight, vec_weight)
    projected, image_grad, grads = tower(
        False, slots, tile_slot, caption_lengths, image_rows, concat_cot, copies
    )
    concat, text_grad, grads = tower(
        True, slots, tile_slot, caption_lengths, text_rows, concat_cot, copies, (projected, grads)
    )
    states = (tile_weight, tile_first, tile_second, left_stat, right_stat, left_basis, right_basis)
    depth = grid_depth()
    if depth is not None:
        sums, *befores = reduce_and_start(depth, grads, states)
    else:
        sums = lax.psum_scatter(grads, ("tower", "batch"), scatter_dimension=0).astype(jnp.float32)
        befores = ()
    news = optimizer(sums, states, (vec_weight, vec_first, vec_second), befores)
    return (concat, image_grad, text_grad, *news)


def solution(mesh):
    return jax.shard_map(
        per_device,
        mesh=mesh,
        in_specs=(
            P(("tower", "batch"), None, None),
            P(("tower", "batch"), None, None),
            P(),
            P(("tower", "batch"), None, None),
            P(),
            P(("tower", "batch"), None, None),
            P(("tower", "batch"), None, None),
            P(("tower", "batch"), None, None),
            P(("tower", "batch"), None, None),
            P(("tower", "batch"), None, None),
            P(("tower", "batch"), None, None),
            P(("tower", "batch"), None, None),
            P(("tower", "batch"), None),
            P(("tower", "batch"), None),
            P(("tower", "batch"), None),
        ),
        out_specs=(
            P(("tower", "batch"), None, None),
            P(("tower", "batch"), None, None),
            P(("tower", "batch"), None, None),
            P(("tower", "batch"), None, None),
            P(("tower", "batch"), None, None),
            P(("tower", "batch"), None, None),
            P(("tower", "batch"), None, None),
            P(("tower", "batch"), None, None),
            P(("tower", "batch"), None, None),
            P(("tower", "batch"), None, None),
            P(("tower", "batch"), None),
            P(("tower", "batch"), None),
            P(("tower", "batch"), None),
        ),
        check_vma=False,
    )
```

```python
import functools
import heapq
import itertools

import jax
import jax.numpy as jnp
from jax import lax
from jax.experimental import pallas as pl
from jax.experimental.pallas import tpu as pltpu
from jax.sharding import PartitionSpec as P

BETA_ONE = 0.9
BETA_TWO = 0.95
EPSILON = 1e-08
RATE_MATRIX = 0.05
RATE_VECTOR = 0.6
DECAY = 0.01
STEP = 10
D = 768
FF = 3072
HEADS = 12
HEAD_DIM = 64
IMG = 197
TXT = 512
MMROWS = 2
T = 256
EXTRA = 16
VECS = 11 + FF // D
MASKED = -1000000000.0
NN = (((1,), (0,)), ((), ()))
NT = (((1,), (1,)), ((), ()))
TN = (((0,), (0,)), ((), ()))
KB = D // T
FB = FF // T
WIDE = 2 * T
SET = 2 * KB * WIDE // T


def mm(a, b, dims=NN):
    return lax.dot_general(a, b, dims, preferred_element_type=jnp.float32)


def rounded(v):
    return v.astype(jnp.bfloat16)


def stats(v):
    center = v - jnp.mean(v, -1, keepdims=True)
    inverse = lax.rsqrt(jnp.mean(center * center, -1, keepdims=True) + 1e-05)
    return center * inverse, inverse


def norm_back(grad, normed, inverse):
    return inverse * (
        grad
        - jnp.mean(grad, -1, keepdims=True)
        - normed * jnp.mean(grad * normed, -1, keepdims=True)
    )


def thirds(v):
    high = rounded(v)
    v = v - high.astype(jnp.float32)
    middle = rounded(v)
    return high, middle, rounded(v - middle.astype(jnp.float32))


def tower_body(is_text, rows, slots, slot_ref, length_ref, x_ref, cot_ref, copies, *rest):
    if is_text:
        zi_ref, _, cat_ref, dx_ref, grads = rest[:5]
        z_ref = None
    else:
        z_ref, dx_ref, grads = rest[:3]
        blank, blank_sem = rest[-2:]
        rest = rest[:-2]
    (wqkv, wo, wu, wd, wp, n1, n1t, qkv, qt, o, ot, a, n2, n2t, slope, h, ht, y, n3, n3t,
     cat, da, dqkv, logs, stage, vec_low, vec_all, bias_up, vec_out,
     wsem, stage_sem, vec_sem, vec_out_sem) = rest[5 if is_text else 3 :]
    dy = cat.at[pl.ds(0, rows)]
    dyb, dab, do, dot_, du = n3, n2, o, n3t, h
    first_tile = slot_ref.shape[0] // 2 if is_text else 0
    first_vec = VECS if is_text else 0
    real = TXT if is_text else IMG
    chunk = 64 if is_text else 16
    chunks = [(i * chunk, min((i + 1) * chunk, real)) for i in range(rows // chunk)]
    if is_text:
        length = length_ref[lax.axis_index("tower") * lax.axis_size("batch") + lax.axis_index("batch")]
    else:
        length = IMG
    tile_rows = slots * T

    def padded(value):
        short = chunk - value.shape[0]
        if short:
            value = jnp.concatenate([value, jnp.zeros((short, D), value.dtype)], 0)
        return value

    def x_of(c):
        return padded(x_ref[0, c[0] : c[1], :].astype(jnp.float32))

    def g_of(c):
        begin = c[0] + MMROWS + (IMG if is_text else 0)
        base = begin // 16 * 16
        end = min(-(-(begin + chunk) // 16) * 16, begin + c[1] - c[0])
        value = cot_ref[0, base:end, :].astype(jnp.float32)
        return padded(value[begin - base : begin - base + c[1] - c[0]])

    def at_slot(ref, slot):
        return ref.at[slot // slots, pl.ds(pl.multiple_of(slot % slots * T, T), T), :]

    extra = pl.ds(tile_rows, EXTRA)
    vec_count = VECS + MMROWS if is_text else VECS
    for i in range(vec_count):
        pltpu.make_async_copy(copies.at[first_vec + i, extra], vec_low.at[i], vec_sem).start()
    mats = [(wqkv, 0), (wqkv, D), (wqkv, 2 * D), (wo, 0), (wu, 0), (wd, 0), (wp, 0)]
    shapes = [(KB, KB)] * 4 + [(KB, FB), (FB, KB), (KB, KB)]
    starts = [0]
    for rb, cb in shapes:
        starts.append(starts[-1] + rb * cb)

    def load(which, sem):
        ref, shift = mats[which]
        rb, cb = shapes[which]

        def one(i, _):
            slot = slot_ref[first_tile + starts[which] + i]
            r, c = i // cb, i % cb
            pltpu.make_async_copy(
                at_slot(copies, slot),
                ref.at[pl.ds(pl.multiple_of(r * T, T), T), pl.ds(pl.multiple_of(shift + c * T, T), T)],
                wsem.at[sem],
            ).start()
            return 0

        lax.fori_loop(0, rb * cb, one, 0)

    def drain(ref, sem):
        pltpu.make_async_copy(ref, ref, sem).wait()

    for which, sem in enumerate((0, 0, 0, 1, 2, 3, 4)):
        load(which, sem)
    if not is_text:
        blank[...] = jnp.zeros(blank.shape, blank.dtype)

        def clear(i, _):
            pltpu.make_async_copy(blank, grads.at[i], blank_sem).start()
            return 0

        lax.fori_loop(0, grads.shape[0], clear, 0)

    def put(place, tiles):
        for n, (_, value) in enumerate(tiles):
            stage[place, n] = rounded(value)
        for n, (tile, _) in enumerate(tiles):
            slot = slot_ref[first_tile + tile]
            pltpu.make_async_copy(stage.at[place, n], at_slot(grads, slot), stage_sem.at[place]).start()

    def free(place, count):
        drain(stage.at[place, pl.ds(0, count)], stage_sem.at[place])

    def square(which, product):
        return [
            (starts[which] + r * KB + k, product[r * T : (r + 1) * T, k * T : (k + 1) * T])
            for r in range(KB)
            for k in range(KB)
        ]

    drain(vec_low.at[pl.ds(0, vec_count)], vec_sem)
    for i in range(vec_count):
        line = jnp.concatenate([vec_low[i, k : k + 1, :] for k in range(KB)], 1).astype(jnp.float32)
        vec_all[i : i + 1, :] = line
        if 7 <= i < 7 + FF // D:
            bias_up[:, (i - 7) * D : (i - 6) * D] = line

    def vec(i):
        return vec_all[i : i + 1, :]

    def vec_grad(i, line):
        line = rounded(line)
        parts = [line[:, k * T : (k + 1) * T] for k in range(KB)]
        parts.append(jnp.zeros((EXTRA - KB, T), jnp.bfloat16))
        vec_out[i] = jnp.concatenate(parts, 0)
        pltpu.make_async_copy(vec_out.at[i], grads.at[first_vec + i, extra], vec_out_sem).start()

    for c in chunks:
        normed, _ = stats(x_of(c))
        n1[c[0] : c[0] + chunk, :] = rounded(normed * vec(0) + vec(1))
    n1t[...] = n1[...].T
    drain(wqkv, wsem.at[0])
    scale = HEAD_DIM ** (-0.5)
    qkv[:, :D] = rounded((mm(n1[...], wqkv[:, :D]) + vec(2))) * jnp.asarray(scale, jnp.bfloat16)
    qkv[:, D : 2 * D] = rounded(mm(n1[...], wqkv[:, D : 2 * D]))
    qkv[:, 2 * D :] = rounded(mm(n1[...], wqkv[:, 2 * D :]) + vec(3))
    qt[...] = qkv[:, :D].T
    lane = lax.broadcasted_iota(jnp.int32, (rows, 2 * HEAD_DIM), 1)
    keys = lax.broadcasted_iota(jnp.int32, (rows, 2 * HEAD_DIM), 0)
    penalty = jnp.where(keys < length, 0.0, MASKED).astype(jnp.bfloat16)
    one = jnp.ones((rows, 2 * HEAD_DIM), jnp.bfloat16)
    zero = jnp.zeros((rows, 2 * HEAD_DIM), jnp.bfloat16)

    def pair_cols(p, base):
        return pl.ds(pl.multiple_of(base + p * 2 * HEAD_DIM, 2 * HEAD_DIM), 2 * HEAD_DIM)

    def beside(side, value, others):
        base = HEAD_DIM * (1 - side)
        result = zero
        for n, other in enumerate(others):
            result = jnp.where(lane == base + n, other, result)
        return jnp.where((lane < HEAD_DIM) if side == 0 else (lane >= HEAD_DIM), value, result)

    def attend(p, _):
        q = qkv[:, pair_cols(p, 0)]
        k = qkv[:, pair_cols(p, D)]
        v = qkv[:, pair_cols(p, 2 * D)]
        outs = []
        for side in range(2):
            s = mm(beside(side, q, [one]), beside(side, k, [penalty]), NT)
            top = jnp.max(s, -1, keepdims=True)
            s = jnp.exp(s - top)
            total = jnp.sum(s, -1, keepdims=True)
            logs[2 * p + side] = jnp.broadcast_to(top + jnp.log(total), (rows, 128))
            outs.append(mm(rounded(s * (1.0 / total)), v))
        o[:, pair_cols(p, 0)] = rounded(jnp.where(lane < HEAD_DIM, outs[0], outs[1]))
        return 0

    lax.fori_loop(0, HEADS // 2, attend, 0, unroll=True)
    ot[...] = o[...].T
    drain(wo, wsem.at[1])
    a[...] = mm(o[...], wo[...])
    for c in chunks:
        at = slice(c[0], c[0] + chunk)
        value = x_of(c) + (a[at, :] + vec(4))
        a[at, :] = value
        normed, _ = stats(value)
        n2[at, :] = rounded(normed * vec(5) + vec(6))
    n2t[...] = n2[...].T
    drain(wu, wsem.at[2])

    def up(i, _):
        cols = pl.ds(pl.multiple_of(i * WIDE, WIDE), WIDE)
        u = mm(n2[...], wu[:, cols]) + bias_up[:, cols]
        cumulative = 0.5 * (1.0 + lax.erf(u * 0.7071067811865476))
        hidden = rounded(u * cumulative)
        slope[:, cols] = cumulative + u * (jnp.exp(-0.5 * u * u) * 0.3989422804014327)
        h[:, cols] = hidden
        ht[cols, :] = hidden.T
        return 0

    lax.fori_loop(0, FF // WIDE, up, 0, unroll=2)
    drain(wd, wsem.at[3])
    y[...] = mm(h[...], wd[...])
    for c in chunks:
        at = slice(c[0], c[0] + chunk)
        value = a[at, :] + (y[at, :] + vec(11))
        y[at, :] = value
        normed, _ = stats(value)
        n3[at, :] = rounded(normed * vec(12) + vec(13))
    n3t[...] = n3[...].T
    drain(wp, wsem.at[4])
    keep = lax.broadcasted_iota(jnp.int32, (rows, 1), 0) < length
    z = jnp.where(keep, mm(n3[...], wp[...]) + vec(14), 0.0)
    if is_text:
        begin = MMROWS + IMG
        cat[:MMROWS, :] = vec_all[VECS : VECS + MMROWS, :]
        cat[MMROWS:begin, :] = zi_ref[0].astype(jnp.float32)
        cat[begin : begin + TXT, :] = z
        cat_ref[0] = rounded(cat[...])
    else:
        even = IMG // 16 * 16
        z_ref[0, :even, :] = rounded(z[:even])
        z_ref[0, even:IMG, :] = rounded(z[even:IMG])

    if not is_text:
        drain(grads, blank_sem)
    zeros = jnp.zeros((1, D), jnp.float32)
    total = zeros
    for c in chunks:
        at = slice(c[0], c[0] + chunk)
        g = jnp.where(keep[at, :], g_of(c), 0.0)
        total = total + jnp.sum(g, 0, keepdims=True)
        dyb[at, :] = rounded(g)
    vec_grad(14, total)
    put(1, square(6, mm(n3t[...], dyb[...])))
    dy[...] = mm(dyb[...], wp[...], NT)
    gain, shift, bias = zeros, zeros, zeros
    for c in chunks:
        at = slice(c[0], c[0] + chunk)
        normed, inverse = stats(y[at, :])
        g = dy[at, :]
        gain = gain + jnp.sum(g * normed, 0, keepdims=True)
        shift = shift + jnp.sum(g, 0, keepdims=True)
        g = norm_back(g * vec(12), normed, inverse)
        dy[at, :] = g
        low = rounded(g)
        dyb[at, :] = low
        bias = bias + jnp.sum(low.astype(jnp.float32), 0, keepdims=True)
    vec_grad(12, gain)
    vec_grad(13, shift)
    vec_grad(11, bias)

    def down(i, _):
        place = i % 2
        pl.when(i == 1)(functools.partial(free, 1, KB * KB))
        pl.when(i >= 2)(functools.partial(free, place, SET))
        cols = pl.ds(pl.multiple_of(i * WIDE, WIDE), WIDE)
        low = rounded(mm(dyb[...], wd[cols, :], NT) * slope[:, cols])
        du[:, cols] = low
        bias_up[:, cols] = jnp.sum(low.astype(jnp.float32), 0, keepdims=True)
        down_grad = mm(ht[cols, :], dyb[...])
        up_grad = mm(n2t[...], low)
        tiles = []
        for w in range(WIDE // T):
            band = slice(w * T, (w + 1) * T)
            number = i * (WIDE // T) + w
            for k in range(KB):
                other = slice(k * T, (k + 1) * T)
                tiles.append((starts[5] + number * KB + k, down_grad[band, other]))
                tiles.append((starts[4] + k * FB + number, up_grad[other, band]))
        put(place, tiles)
        return 0

    lax.fori_loop(0, FF // WIDE, down, 0, unroll=True)
    for i in range(FF // D):
        vec_grad(7 + i, bias_up[:, i * D : (i + 1) * D])
    da[...] = mm(du[...], wu[...], NT)
    gain, shift, bias = zeros, zeros, zeros
    for c in chunks:
        at = slice(c[0], c[0] + chunk)
        normed, inverse = stats(a[at, :])
        g = da[at, :]
        gain = gain + jnp.sum(g * normed, 0, keepdims=True)
        shift = shift + jnp.sum(g, 0, keepdims=True)
        g = dy[at, :] + norm_back(g * vec(5), normed, inverse)
        da[at, :] = g
        low = rounded(g)
        dab[at, :] = low
        bias = bias + jnp.sum(low.astype(jnp.float32), 0, keepdims=True)
    vec_grad(5, gain)
    vec_grad(6, shift)
    vec_grad(4, bias)
    dout = mm(dab[...], wo[...], NT)
    free(0, SET)
    put(0, square(3, mm(ot[...], dab[...])))
    low = rounded(dout)
    y[...] = low.astype(jnp.float32) * o[...].astype(jnp.float32)
    do[...] = low
    dot_[...] = low.T

    def attend_back(p, _):
        q = qkv[:, pair_cols(p, 0)]
        k = qkv[:, pair_cols(p, D)]
        v = qkv[:, pair_cols(p, 2 * D)]
        g = do[:, pair_cols(p, 0)]
        each = y[:, pair_cols(p, 0)]
        dqs, dks, dvs = [], [], []
        for side in range(2):
            half = pl.ds(pl.multiple_of((2 * p + side) * HEAD_DIM, HEAD_DIM), HEAD_DIM)
            mine = (lane < HEAD_DIM) if side == 0 else (lane >= HEAD_DIM)
            minus = [-one] * 3
            w = jnp.exp(
                mm(
                    beside(side, q, [one, *thirds(logs[2 * p + side])]),
                    beside(side, k, [penalty, *minus]),
                    NT,
                )
            )
            dvs.append(mm(dot_[half, :], rounded(w)))
            c = jnp.sum(jnp.where(mine, each, 0.0), -1, keepdims=True)
            dw = mm(
                beside(side, g, thirds(jnp.broadcast_to(c, (rows, 2 * HEAD_DIM)))),
                beside(side, v, minus),
                NT,
            )
            ds = rounded(w * dw)
            dqs.append(mm(ds, k))
            dks.append(mm(qt[half, :], ds))
        dqkv[:, pair_cols(p, 0)] = rounded(jnp.where(lane < HEAD_DIM, dqs[0], dqs[1]) * scale)
        dqkv[:, pair_cols(p, D)] = rounded(jnp.concatenate(dks, 0).T)
        dqkv[:, pair_cols(p, 2 * D)] = rounded(jnp.concatenate(dvs, 0).T)
        return 0

    lax.fori_loop(0, HEADS // 2, attend_back, 0, unroll=True)
    for m, number in ((0, 2), (2, 3)):
        vec_grad(number, jnp.sum(dqkv[:, m * D : (m + 1) * D].astype(jnp.float32), 0, keepdims=True))
    for m in range(3):
        free((1 + m) % 2, SET if m == 0 else KB * KB)
        put((1 + m) % 2, square(m, mm(n1t[...], dqkv[:, m * D : (m + 1) * D])))
    dy[...] = mm(dqkv[...], wqkv[...], NT)
    gain, shift = zeros, zeros
    for c in chunks:
        at = slice(c[0], c[0] + chunk)
        normed, inverse = stats(x_of(c))
        g = dy[at, :]
        gain = gain + jnp.sum(g * normed, 0, keepdims=True)
        shift = shift + jnp.sum(g, 0, keepdims=True)
        low = rounded(da[at, :] + norm_back(g * vec(0), normed, inverse))
        dx_ref[0, c[0] : c[1], :] = low[: c[1] - c[0]]
    vec_grad(0, gain)
    vec_grad(1, shift)
    if is_text:
        learned = cot_ref[0, :16, :].astype(jnp.float32)
        for i in range(MMROWS):
            vec_grad(VECS + i, learned[i : i + 1])
    free(0, KB * KB)
    free(1, KB * KB)
    drain(vec_out.at[pl.ds(0, vec_count)], vec_out_sem)


def tower(is_text, slots, tile_slot, lengths, x, cot, copies, before=()):
    bf, f32 = jnp.bfloat16, jnp.float32
    smem = pl.BlockSpec(memory_space=pltpu.SMEM)
    vmem = pl.BlockSpec(memory_space=pltpu.VMEM)
    hbm = pl.BlockSpec(memory_space=pl.ANY)
    dma = pltpu.SemaphoreType.DMA
    rows = -(-x.shape[1] // 16) * 16
    outs = [
        jax.ShapeDtypeStruct(cot.shape if is_text else x.shape, bf),
        jax.ShapeDtypeStruct(x.shape, bf),
        jax.ShapeDtypeStruct(copies.shape, bf),
    ]
    scratch = [
        pltpu.VMEM((D, 3 * D), bf), pltpu.VMEM((D, D), bf), pltpu.VMEM((D, FF), bf),
        pltpu.VMEM((FF, D), bf), pltpu.VMEM((D, D), bf),
        pltpu.VMEM((rows, D), bf), pltpu.VMEM((D, rows), bf),
        pltpu.VMEM((rows, 3 * D), bf), pltpu.VMEM((D, rows), bf),
        pltpu.VMEM((rows, D), bf), pltpu.VMEM((D, rows), bf),
        pltpu.VMEM((rows, D), f32),
        pltpu.VMEM((rows, D), bf), pltpu.VMEM((D, rows), bf),
        pltpu.VMEM((rows, FF), f32),
        pltpu.VMEM((rows, FF), bf), pltpu.VMEM((FF, rows), bf),
        pltpu.VMEM((rows, D), f32),
        pltpu.VMEM((rows, D), bf), pltpu.VMEM((D, rows), bf),
        pltpu.VMEM((cot.shape[1] if is_text else rows, D), f32),
        pltpu.VMEM((rows, D), f32),
        pltpu.VMEM((rows, 3 * D), bf),
        pltpu.VMEM((HEADS, rows, 128), f32),
        pltpu.VMEM((2, SET, T, T), bf),
        pltpu.VMEM((VECS + MMROWS, EXTRA, T), bf), pltpu.VMEM((VECS + MMROWS, D), f32),
        pltpu.VMEM((1, FF), f32), pltpu.VMEM((VECS + MMROWS, EXTRA, T), bf),
        dma((5,)), dma((2,)), dma, dma,
    ]
    if not is_text:
        scratch += [pltpu.VMEM((slots * T + EXTRA, T), bf), dma]
    return pl.pallas_call(
        functools.partial(tower_body, is_text, rows, slots),
        in_specs=[smem, smem, vmem, vmem, hbm] + ([vmem, hbm] if is_text else []),
        out_specs=[vmem, vmem, hbm],
        out_shape=outs,
        scratch_shapes=scratch,
        input_output_aliases={6: 2} if is_text else {},
        compiler_params=pltpu.CompilerParams(vmem_limit_bytes=63 << 20),
        name="text_tower" if is_text else "image_tower",
    )(tile_slot, lengths, x, cot, copies, *before)


def split(x):
    hi = x.astype(jnp.bfloat16)
    lo = (x - hi.astype(jnp.float32)).astype(jnp.bfloat16)
    return hi, lo


def dot(a, b, dims):
    return lax.dot_general(a, b, dims, preferred_element_type=jnp.float32)


def mm3(a, b, dims):
    return dot(a[0], b[0], dims) + (dot(a[0], b[1], dims) + dot(a[1], b[0], dims))


def adam_step(first, second):
    return (
        first
        / (1.0 - BETA_ONE**STEP)
        / (jnp.sqrt(second / (1.0 - BETA_TWO**STEP)) + EPSILON)
    )


B = 64
GROUP = 8
INS, OUTS = 7, 5


def eliminate_group(diag, jg):
    count = diag.shape[0]
    shape = (count, GROUP, 2 * B)
    subs = lax.broadcasted_iota(jnp.int32, shape, 1)
    top = slice(jg * GROUP, jg * GROUP + GROUP)
    tile = diag[:, top, :]
    for jj in range(0, GROUP, 2):
        j = jg * GROUP + jj
        first = jnp.broadcast_to(tile[:, :, j : j + 1], shape)
        second = jnp.broadcast_to(tile[:, :, j + 1 : j + 2], shape)
        p00, p01, p11 = first[:, jj : jj + 1], second[:, jj : jj + 1], second[:, jj + 1 : jj + 2]
        r0, r1 = tile[:, jj : jj + 1], tile[:, jj + 1 : jj + 2]
        inverse = 1.0 / (p00 * p11 - p01 * p01)
        cross = p01 * inverse
        t0 = (p11 * inverse) * r0 - cross * r1
        t1 = (p00 * inverse) * r1 - cross * r0
        lower = tile - first * t0 - second * t1
        tile = jnp.where(subs > jj + 1, lower, jnp.where(subs == jj + 1, tile - (p01 / p00) * r0, tile))
        if jg < B // GROUP - 1:
            rest = diag[:, jg * GROUP + GROUP :, :]
            diag[:, jg * GROUP + GROUP :, :] = (
                rest - rest[:, :, j : j + 1] * t0 - rest[:, :, j + 1 : j + 2] * t1
            )
    diag[:, top, :] = tile


class Update:
    def __init__(self, slots, begin, shift, sums, ins, outs, inbuf, outbuf, qbuf, work, diag, in_sem, out_sem, q_sem):
        self.slots, self.begin, self.shift = slots, begin, shift
        self.sums, self.ins, self.outs = sums, ins, outs
        self.inbuf, self.outbuf, self.qbuf, self.work, self.diag = inbuf, outbuf, qbuf, work, diag
        self.in_sem, self.out_sem, self.q_sem = in_sem, out_sem, q_sem

    def fetch(self):
        for s in range(self.slots):
            for n in range(INS):
                pltpu.make_async_copy(self.ins[n].at[self.begin + s], self.inbuf.at[s, n], self.in_sem.at[s]).start()

    def refine(self, s):
        pltpu.make_async_copy(self.inbuf.at[s], self.inbuf.at[s], self.in_sem.at[s]).wait()
        place = s % 2
        if s >= 2:
            pltpu.make_async_copy(self.outbuf.at[place], self.outbuf.at[place], self.out_sem.at[place]).wait()
        w, m1, m2, ls, rs, lb, rb = (self.inbuf.at[s, n] for n in range(INS))
        wn, m1n, m2n, lsn, rsn = (self.outbuf.at[place, n] for n in range(OUTS))
        e = split(self.sums[s * T : (s + 1) * T, :])
        ql = split(lb[...])
        qr = split(rb[...])
        left = BETA_TWO * ls[...] + (1.0 - BETA_TWO) * mm3(e, e, NT)
        right = BETA_TWO * rs[...] + (1.0 - BETA_TWO) * mm3(e, e, TN)
        lsn[...] = left
        rsn[...] = right
        turned = mm3(split(mm3(ql, e, TN)), qr, NN)
        first = BETA_ONE * m1[...] + (1.0 - BETA_ONE) * turned
        second = BETA_TWO * m2[...] + (1.0 - BETA_TWO) * turned * turned
        m1n[...] = first
        m2n[...] = second
        direction = mm3(split(mm3(ql, split(adam_step(first, second)), NN)), qr, NT)
        old = w[...]
        wn[...] = old - RATE_MATRIX * (direction + DECAY * old)
        for n in range(OUTS):
            pltpu.make_async_copy(self.outbuf.at[place, n], self.outs[n].at[self.shift + s], self.out_sem.at[place]).start()
        for side, (basis, stat) in enumerate(((ql, left), (qr, right))):
            y = mm3(basis, split(stat), TN)
            y = y * lax.rsqrt(jnp.sum(y * y, axis=1, keepdims=True))
            self.work[2 * s + side, :, T:] = y
            y = split(y)
            self.work[2 * s + side, :, :T] = mm3(y, y, NT)

    def load(self, k):
        low = k * B
        edge = low // (2 * B) * 2 * B
        row = lax.broadcasted_iota(jnp.int32, (B, 2 * B), 0)
        lane = lax.broadcasted_iota(jnp.int32, (B, 2 * B), 1)
        for m in range(2 * self.slots):
            block = self.work[m, low : low + B, edge : edge + 2 * B]
            if low % (2 * B):
                block = pltpu.roll(block, B, 1)
            self.diag[m] = jnp.where(lane < B, block, jnp.where(lane == row + B, 1.0, 0.0))

    def products(self, k, begin, end):
        low = k * B
        edge = low // (2 * B) * 2 * B
        row = lax.broadcasted_iota(jnp.int32, (B, 2 * B), 0)
        lane = lax.broadcasted_iota(jnp.int32, (B, 2 * B), 1)
        work = self.work

        def one(m):
            d = self.diag[m]
            pivots = jnp.sum(jnp.where(lane == row, d, 0.0), axis=1, keepdims=True)
            high, rest = split(d[:, B:] * lax.rsqrt(pivots))
            inverse = jnp.concatenate([high, rest, high], 1)
            high, rest = split(work[m, low : low + B, edge:])
            new = dot(inverse, jnp.concatenate([high, high, rest], 0), NN)
            work[m, low : low + B, edge:] = new
            if low + B < T:
                high, rest = split(new)
                after = low + B - edge
                start = (low + B) // (2 * B) * 2 * B
                left = jnp.concatenate([high, rest, high], 0)[:, after : T - edge]
                right = jnp.concatenate([high, high, rest], 0)[:, start - edge :]
                work[m, low + B :, start:] = work[m, low + B :, start:] - dot(left, right, TN)

        def pair(i, _):
            one(begin + 2 * i)
            one(begin + 2 * i + 1)
            return 0

        lax.fori_loop(0, (end - begin) // 2, pair, 0, unroll=True)

    def finish(self, s):
        for side in range(2):
            if s:
                pltpu.make_async_copy(self.qbuf.at[side], self.qbuf.at[side], self.q_sem.at[side]).wait()
            self.qbuf[side] = self.work[2 * s + side, :, T:].T
            pltpu.make_async_copy(self.qbuf.at[side], self.outs[OUTS + side].at[self.shift + s], self.q_sem.at[side]).start()

    def close(self):
        for side in range(2):
            pltpu.make_async_copy(self.qbuf.at[side], self.qbuf.at[side], self.q_sem.at[side]).wait()
        for place in range(min(2, self.slots)):
            pltpu.make_async_copy(self.outbuf.at[place], self.outbuf.at[place], self.out_sem.at[place]).wait()

    def steps(self):
        result = [functools.partial(self.refine, s) for s in range(self.slots)]
        for k in range(T // B):
            result.append(functools.partial(self.load, k))
            result += [functools.partial(eliminate_group, self.diag, jg) for jg in range(B // GROUP)]
            middle = self.slots // 2 * 2
            result += [functools.partial(self.products, k, a, b) for a, b in ((0, middle), (middle, 2 * self.slots)) if a < b]
        result += [functools.partial(self.finish, s) for s in range(self.slots)]
        result.append(self.close)
        return result


def update_scratch(slots):
    f32 = jnp.float32
    dma = pltpu.SemaphoreType.DMA
    return [
        pltpu.VMEM((slots, INS, T, T), f32),
        pltpu.VMEM((2, OUTS, T, T), f32),
        pltpu.VMEM((2, T, T), f32),
        pltpu.VMEM((2 * slots, T, 2 * T), f32),
        pltpu.VMEM((2 * slots, B, 2 * B), f32),
        dma((slots,)),
        dma((2,)),
        dma((2,)),
    ]


def rest_body(total, done, sums_ref, v_refs, ins, befores, outs, v_outs, scratch, passing, passing_sem):
    update = Update(total - done, done, done, sums_ref, ins, outs, *scratch)
    update.fetch()
    arrivals = [
        pltpu.make_async_copy(before, passing.at[n], passing_sem.at[0, n]) for n, before in enumerate(befores)
    ]
    departures = [
        pltpu.make_async_copy(passing.at[n], outs[n].at[pl.ds(0, done)], passing_sem.at[1, n])
        for n in range(len(befores))
    ]
    for copy in arrivals:
        copy.start()
    vw_ref, v1_ref, v2_ref = v_refs
    vwn_ref, v1n_ref, v2n_ref = v_outs
    for k in range(vw_ref.shape[1] // T):
        cols = slice(k * T, (k + 1) * T)
        row = (total - done) * T + k
        g = sums_ref[row : row + 1, :]
        first = BETA_ONE * v1_ref[:, cols] + (1.0 - BETA_ONE) * g
        second = BETA_TWO * v2_ref[:, cols] + (1.0 - BETA_TWO) * g * g
        v1n_ref[:, cols] = first
        v2n_ref[:, cols] = second
        vwn_ref[:, cols] = vw_ref[:, cols] - RATE_VECTOR * adam_step(first, second)
    for number, step in enumerate(update.steps()):
        step()
        if number == total - done - 1:
            for arrival, departure in zip(arrivals, departures):
                arrival.wait()
                departure.start()
    for copy in departures:
        copy.wait()


def optimizer(sums, states, vectors, befores=()):
    total = states[0].shape[0]
    done = befores[0].shape[0] if befores else 0
    hbm = pl.BlockSpec(memory_space=pl.ANY)
    vmem = pl.BlockSpec(memory_space=pltpu.VMEM)
    f32 = jnp.float32
    count = len(befores)

    def body(*refs):
        sums_ref, v_refs, refs = refs[0], refs[1:4], refs[4:]
        ins, befores, refs = refs[:INS], refs[INS : INS + count], refs[INS + count :]
        outs, v_outs, refs = refs[:INS], refs[INS : INS + 3], refs[INS + 3 :]
        rest_body(total, done, sums_ref, v_refs, ins, befores, outs, v_outs, refs[:-2], *refs[-2:])

    return pl.pallas_call(
        body,
        in_specs=[vmem] * 4 + [hbm] * (INS + count),
        out_specs=[hbm] * INS + [vmem] * 3,
        out_shape=[jax.ShapeDtypeStruct(v.shape, f32) for v in (*states, *vectors)],
        scratch_shapes=update_scratch(total - done)
        + [pltpu.VMEM((INS, max(done, 1), T, T), f32), pltpu.SemaphoreType.DMA((2, INS))],
        compiler_params=pltpu.CompilerParams(vmem_limit_bytes=60 << 20),
        name="optimizer",
    )(sums, *vectors, *states, *befores)


ORDERS = ("xzy", "yzx", "zxy", "zyx")


def part_rows(slots):
    quarter = slots * T // 4
    sizes = [quarter, quarter, quarter, quarter + EXTRA]
    return [(sum(sizes[:i]), sizes[i]) for i in range(4)]


def last_step(order, key):
    away = {"z": key[0], "x": key[1], "y": key[2]}
    steps = [i for i in range(3) if away[order[i]]]
    return steps[-1] if steps else -1


def plan_of(depth):
    cells = list(itertools.product(range(depth), range(2), range(2)))
    queues, free, events, arrived = {}, {}, [], {}
    ticket = itertools.count()

    def onward(cell, part, source, now):
        order = ORDERS[part]
        key = (source[0] - cell[0], source[1] ^ cell[1], source[2] ^ cell[2])
        step = last_step(order, key)
        for i in range(3):
            z, x, y = cell
            if order[i] == "z":
                if i > step:
                    ways = (1, -1)
                elif i == step:
                    ways = (1,) if key[0] < 0 else (-1,)
                else:
                    ways = ()
                targets = [(z + w, x, y) for w in ways if 0 <= z + w < depth]
            elif i > step:
                targets = [(z, 1 - x, y) if order[i] == "x" else (z, x, 1 - y)]
            else:
                targets = []
            for target in targets:
                heapq.heappush(queues.setdefault((cell, target), []), (now, next(ticket), part, source))
                heapq.heappush(events, (now, next(ticket), 0, (cell, target)))

    for cell in cells:
        for part in range(4):
            onward(cell, part, cell, 0.0)
    while events:
        now, _, kind, what = heapq.heappop(events)
        if kind == 0:
            if queues[what] and free.get(what, 0.0) <= now:
                _, _, part, source = heapq.heappop(queues[what])
                free[what] = now + 2.0
                heapq.heappush(events, (now + 2.0, next(ticket), 0, what))
                heapq.heappush(events, (now + 2.5, next(ticket), 1, (what[1], part, source)))
        else:
            cell, part, source = what
            key = (part, source[0] - cell[0], source[1] ^ cell[1], source[2] ^ cell[2])
            arrived.setdefault(key, []).append(now)
            onward(cell, part, source, now)
    times = {k: sum(v) / len(v) for k, v in arrived.items()}
    fixed = {}

    def time_of(key):
        if key not in fixed:
            part, dz, dx, dy = key
            step = last_step(ORDERS[part], key[1:])
            if step < 0:
                return 0.0
            dim = ORDERS[part][step]
            if dim == "z":
                parent = (part, dz - (1 if dz > 0 else -1), dx, dy)
            else:
                parent = (part, dz, 0 if dim == "x" else dx, 0 if dim == "y" else dy)
            fixed[key] = max(times[key], time_of(parent) + 0.01)
        return fixed[key]

    return sorted((time_of(k), k) for k in times)


class Place:
    def __init__(self, depth):
        tower = lax.axis_index("tower")
        self.depth = depth
        self.core = tower % 2
        self.x = tower // 2 % 2
        self.z = tower // 4
        self.y = lax.axis_index("batch")

    def at(self, dz=0, dx=0, dy=0):
        return (
            self.z + dz,
            1 - self.x if dx else self.x,
            1 - self.y if dy else self.y,
        )

    def device(self, cell, other=False):
        core = 1 - self.core if other else self.core
        return ((cell[0] * 2 + cell[1]) * 2 + core, cell[2])

    def block(self, cell, other=False):
        core = 1 - self.core if other else self.core
        return ((cell[0] * 2 + cell[1]) * 2 + core) * 2 + cell[2]

    def spot(self, cell):
        return (cell[0] * 2 + cell[1]) * 2 + cell[2]

    def inside(self, dz):
        if dz == 0:
            return None
        return self.z + dz < self.depth if dz > 0 else self.z + dz >= 0

    def meet(self):
        barrier = pltpu.get_barrier_semaphore()

        def greet(device):
            pl.semaphore_signal(barrier, inc=1, device_id=device, device_id_type=pl.DeviceIdType.MESH)

        greet(self.device(self.at(), True))
        greet(self.device(self.at(dx=1)))
        greet(self.device(self.at(dy=1)))
        for way in (1, -1):
            pl.when(self.inside(way))(functools.partial(greet, self.device(self.at(dz=way))))
        low = (self.z > 0).astype(jnp.int32)
        high = (self.z < self.depth - 1).astype(jnp.int32)
        pl.semaphore_wait(barrier, 3 + low + high)


def guarded(conditions, action):
    conditions = [c for c in conditions if c is not None]
    if not conditions:
        action()
    else:
        both = conditions[0]
        for c in conditions[1:]:
            both = jnp.logical_and(both, c)
        pl.when(both)(action)


def remote(src, dst, send, recv, device):
    return pltpu.make_async_remote_copy(
        src_ref=src, dst_ref=dst, send_sem=send, recv_sem=recv,
        device_id=device, device_id_type=pl.DeviceIdType.MESH,
    )


def drain(ref, sem):
    pltpu.make_async_copy(ref, ref, sem).wait()


def gather_body(
    depth, parts, plan, tiles_ref, vec_ref, out_ref, wide, own_ref, wide_sem, own_sem, z_sem, flat_sem, twin_sem, recv_sem
):
    slots = tiles_ref.shape[0]
    for slot in range(slots):
        pltpu.make_async_copy(tiles_ref.at[slot], wide.at[slot], wide_sem.at[slot]).start()
    here = Place(depth)
    here.meet()
    line = vec_ref[...].astype(jnp.bfloat16)
    pieces = [line[:, k * T : (k + 1) * T] for k in range(line.shape[1] // T)]
    pieces.append(jnp.zeros((EXTRA - len(pieces), T), jnp.bfloat16))
    own_ref[slots * T :, :] = jnp.concatenate(pieces, 0)
    for slot in range(slots):
        drain(wide.at[slot], wide_sem.at[slot])
        own_ref[slot * T : (slot + 1) * T, :] = wide[slot].astype(jnp.bfloat16)
    mine = pltpu.make_async_copy(own_ref, out_ref.at[here.block(here.at())], own_sem)
    mine.start()
    waits = []

    def handle(part, key):
        start, size = parts[part]
        rows = pl.ds(start, size)
        order = ORDERS[part]
        step = last_step(order, key)
        cell = here.at(*key)
        present = here.inside(key[0])
        block = here.block(cell)
        spot = here.spot(cell)
        place = out_ref.at[block, rows]
        source = own_ref.at[rows] if step < 0 else place

        def arrive():
            if step >= 0:
                drain(place, recv_sem.at[part, spot])

        guarded([present], arrive)
        for i in range(3):
            dim = order[i]
            if dim == "z":
                ways = (1, -1) if i > step else ()
                if i == step:
                    ways = (1,) if key[0] < 0 else (-1,)
                for way in ways:
                    sem = z_sem.at[part, spot, 0 if way > 0 else 1]
                    copy = remote(source, place, sem, recv_sem.at[part, spot], here.device(here.at(dz=way)))
                    conditions = [present, here.inside(way)]
                    guarded(conditions, copy.start)
                    waits.append((conditions, copy.wait_send))
            elif i > step:
                target = here.at(dx=1) if dim == "x" else here.at(dy=1)
                guarded(
                    [present],
                    remote(
                        source, place, flat_sem.at[part, 0 if dim == "x" else 1],
                        recv_sem.at[part, spot], here.device(target),
                    ).start,
                )
        guarded(
            [present],
            remote(source, place, twin_sem.at[0], twin_sem.at[1], here.device(here.at(), True)).start,
        )

    for part in range(4):
        handle(part, (0, 0, 0))
    for part, *key in plan:
        handle(part, tuple(key))
    for conditions, action in waits:
        guarded(conditions, action)
    for part in range(4):
        rows = pl.ds(*parts[part])
        sent = 1
        for dim in ORDERS[part]:
            if dim != "z":
                drain(out_ref.at[pl.ds(0, sent), rows], flat_sem.at[part, 0 if dim == "x" else 1])
            sent *= depth if dim == "z" else 2
    mine.wait()
    half = pl.ds(0, 4 * depth)
    drain(out_ref.at[half], twin_sem.at[0])
    drain(out_ref.at[half], twin_sem.at[1])


def gather(depth, tiles, vec):
    slots = tiles.shape[0]
    parts = part_rows(slots)
    rows = slots * T + EXTRA
    hbm = pl.BlockSpec(memory_space=pl.ANY)
    dma = pltpu.SemaphoreType.DMA
    return pl.pallas_call(
        functools.partial(gather_body, depth, parts, [key for _, key in plan_of(depth)]),
        in_specs=[hbm, pl.BlockSpec(memory_space=pltpu.VMEM)],
        out_specs=hbm,
        out_shape=jax.ShapeDtypeStruct((8 * depth, rows, T), jnp.bfloat16),
        scratch_shapes=[
            pltpu.VMEM(tiles.shape, jnp.float32),
            pltpu.VMEM((rows, T), jnp.bfloat16),
            dma((slots,)),
            dma,
            dma((4, 4 * depth, 2)),
            dma((4, 2)),
            dma((2,)),
            dma((4, 4 * depth)),
        ],
        compiler_params=pltpu.CompilerParams(
            collective_id=0, has_side_effects=True, vmem_limit_bytes=60 << 20
        ),
        name="gather",
    )(tiles, vec)


def add_rows(size, target, start, sources):
    def piece(at, count):
        total = sources[0][pl.ds(at, count), :].astype(jnp.float32)
        for source in sources[1:]:
            total = total + source[pl.ds(at, count), :].astype(jnp.float32)
        target[pl.ds(start + at, count), :] = total.astype(target.dtype)

    whole = size // 128

    def body(i, _):
        piece(pl.multiple_of(i * 128, 128), 128)
        return 0

    lax.fori_loop(0, whole, body, 0)
    if size % 128:
        piece(whole * 128, size % 128)


LOADS = 8


def wave_rows(slots, early):
    result = []
    for begin, count, extra in ((0, early, 0), (early * T, slots - early, EXTRA)):
        size = count * T // 4
        sizes = [size, size, size, size + extra]
        result += [(begin + sum(sizes[:i]), sizes[i]) for i in range(4)]
    return result


def wave_keys(depth, slots, early):
    timed = plan_of(depth)
    end = timed[-1][0]
    share = early / slots
    result = []
    for wave in range(2):
        for when, (part, *key) in timed + [(0.0, (part, 0, 0, 0)) for part in range(4)]:
            spent = end - when
            at = spent * share if wave == 0 else end * (share - 0.03) + spent * (1 - share)
            result.append((at, wave, -len(result), 4 * wave + part, tuple(key)))
    return [(part, key) for _, _, _, part, key in sorted(result)]


def reduce_body(depth, slots, early, parts, keys, grads_ref, *refs):
    ins, refs = refs[:INS], refs[INS:]
    late_ref, refs = refs[0], refs[1:]
    outs, refs = refs[:INS], refs[INS:]
    (own, twin, sums, flat0_a, flat0_b, flat1_a, flat1_b, line_a, line_b,
     load_sem, twin_send, twin_recv, flat0_send, flat0_recv, flat1_send, flat1_recv, line_send, line_recv) = refs[:18]
    update = Update(early, 0, 0, sums, ins, outs, *refs[18:])
    here = Place(depth)

    def load(number):
        part, key = keys[number]
        cell = here.at(*key)
        start, size = parts[part]
        place = number % LOADS
        guarded(
            [here.inside(key[0])],
            pltpu.make_async_copy(
                grads_ref.at[here.block(cell), pl.ds(start, size)], own.at[place, pl.ds(0, size)], load_sem.at[place]
            ).start,
        )

    for number in range(LOADS):
        load(number)
    here.meet()
    other = here.device(here.at(), True)
    for part, key in keys:
        cell = here.at(*key)
        rows = pl.ds(*parts[part])
        spot = here.spot(cell)
        guarded(
            [here.inside(key[0])],
            remote(
                grads_ref.at[here.block(cell, True), rows], twin.at[spot, rows], twin_send,
                twin_recv.at[part, spot], other,
            ).start,
        )
    update.fetch()
    for end, shift in ((0, 1), (depth - 1, 0)):

        def clear():
            for line in (line_a, line_b):
                for row in range(6):
                    for target in range(depth):
                        place = line.at[row * (depth + 1) + target + shift]
                        place[...] = jnp.zeros(place.shape, place.dtype)

        pl.when(here.z == end)(clear)
    waits = []

    def task(number):
        part, key = keys[number]
        wave, local = part // 4, part % 4
        flat0, flat1, line = (flat0_a, flat1_a, line_a) if wave == 0 else (flat0_b, flat1_b, line_b)
        start, size = parts[part]
        rows = pl.ds(start, size)
        short = pl.ds(0, size)
        order = ORDERS[local]
        cell = here.at(*key)
        spot = here.spot(cell)
        present = here.inside(key[0])
        step = last_step(order, key)
        middle = order[1] == "z"
        cross = order[2]
        index0 = local * 2 * depth + cell[0] * 2 + (cell[1] if cross == "y" else cell[2])
        if middle:
            row = local * 2 + (cell[1] if order[0] == "x" else cell[2])
            index1 = local
        else:
            row = local + 2
            index1 = 2 + (local - 2) * depth + cell[0]
        line0 = row * (depth + 1) + cell[0]
        sent = row * depth + cell[0]
        base0, base1, base_line, base_sent = (wave * n for n in (8 * depth, 2 + 2 * depth, 6 * (depth + 1), 6 * depth))

        def run():
            mine = own.at[number % LOADS, short]
            target = twin.at[spot, rows]
            drain(mine, load_sem.at[number % LOADS])
            drain(target, twin_recv.at[part, spot])
            sources = [mine, target]
            for i in (2, 1, 0):
                if i <= step - 1 or (i == step and order[i] != "z"):
                    break
                if order[i] == "z":
                    ways = (1, 0)
                    if i == step:
                        ways = (1,) if key[0] > 0 else (0,)
                    for way in ways:
                        place = line.at[line0 + way, short]
                        arrive = functools.partial(drain, place, line_recv.at[base_line + line0 + way])
                        pl.when(here.z > 0 if way else here.z < depth - 1)(arrive)
                        sources.append(place)
                    if i == step:
                        break
                elif i == 2:
                    drain(flat0.at[index0, short], flat0_recv.at[base0 + index0])
                    sources.append(flat0.at[index0, short])
                else:
                    drain(flat1.at[index1, short], flat1_recv.at[base1 + index1])
                    sources.append(flat1.at[index1, short])
            if step < 0:
                add_rows(size, sums, start, sources)
                return
            add_rows(size, twin.at[spot], start, sources)
            dim = order[step]
            if dim == "z":
                way = 1 if key[0] > 0 else 0
                remote(
                    target, line.at[line0 + way, short], line_send.at[base_sent + sent],
                    line_recv.at[base_line + line0 + way], here.device(here.at(dz=1 if way else -1)),
                ).start()
                return
            device = here.device(here.at(dx=1) if dim == "x" else here.at(dy=1))
            if step == 2:
                remote(
                    target, flat0.at[index0, short], flat0_send.at[part], flat0_recv.at[base0 + index0], device
                ).start()
            else:
                remote(
                    target, flat1.at[index1, short], flat1_send.at[part], flat1_recv.at[base1 + index1], device
                ).start()

        guarded([present], run)
        if number + LOADS < len(keys):
            load(number + LOADS)
        if step >= 0 and order[step] == "z":
            waits.append(
                ([present], functools.partial(drain, twin.at[spot, rows], line_send.at[base_sent + sent]))
            )

    ready = max(n for n, (part, key) in enumerate(keys) if part < 4)
    steps = update.steps()
    taken = 0
    for number in range(len(keys)):
        task(number)
        if number >= ready:
            due = len(steps) * (number - ready + 1) // (len(keys) - ready)
            for step in steps[taken:due]:
                step()
            taken = due
    late_ref[...] = sums[early * T :, :]
    for conditions, action in waits:
        guarded(conditions, action)
    for part in range(8):
        rows = pl.ds(*parts[part])
        order = ORDERS[part % 4]
        sent = 1
        for i, dim in enumerate(order):
            if dim != "z":
                sem = flat0_send if i == 2 else flat1_send
                drain(twin.at[pl.ds(0, sent), rows], sem.at[part])
            sent *= depth if dim == "z" else 2
    drain(twin, twin_send)


def reduce_and_start(depth, grads, states):
    slots = states[0].shape[0]
    early = slots * 5 // 8
    parts = wave_rows(slots, early)
    rows = grads.shape[1]
    long_a, long_b = parts[3][1], parts[7][1]
    dma = pltpu.SemaphoreType.DMA
    bf, f32 = jnp.bfloat16, jnp.float32
    hbm = pl.BlockSpec(memory_space=pl.ANY)
    return pl.pallas_call(
        functools.partial(reduce_body, depth, slots, early, parts, wave_keys(depth, slots, early)),
        in_specs=[hbm] * (1 + INS),
        out_specs=[pl.BlockSpec(memory_space=pltpu.VMEM)] + [hbm] * INS,
        out_shape=[jax.ShapeDtypeStruct((rows - early * T, T), f32)]
        + [jax.ShapeDtypeStruct((early, T, T), f32)] * INS,
        scratch_shapes=[
            pltpu.VMEM((LOADS, max(long_a, long_b), T), bf),
            pltpu.VMEM((4 * depth, rows, T), bf),
            pltpu.VMEM((rows, T), f32),
            pltpu.VMEM((8 * depth, long_a, T), bf),
            pltpu.VMEM((8 * depth, long_b, T), bf),
            pltpu.VMEM((2 + 2 * depth, long_a, T), bf),
            pltpu.VMEM((2 + 2 * depth, long_b, T), bf),
            pltpu.VMEM((6 * (depth + 1), long_a, T), bf),
            pltpu.VMEM((6 * (depth + 1), long_b, T), bf),
            dma((LOADS,)),
            dma,
            dma((8, 4 * depth)),
            dma((8,)),
            dma((16 * depth,)),
            dma((8,)),
            dma((4 + 4 * depth,)),
            dma((12 * depth,)),
            dma((12 * (depth + 1),)),
        ]
        + update_scratch(early),
        compiler_params=pltpu.CompilerParams(
            collective_id=1, has_side_effects=True, vmem_limit_bytes=63 << 20
        ),
        name="reduce_and_start",
    )(grads, *states)


def grid_depth():
    towers = lax.axis_size("tower")
    if lax.axis_size("batch") != 2 or towers % 4 or towers > 16 or towers < 8:
        return None
    return towers // 4


def all_blocks(tiles, vec):
    depth = grid_depth()
    if depth is not None:
        return gather(depth, tiles, vec)
    own = jnp.concatenate([tiles.reshape(-1, T), vec.reshape(-1, T)], 0)
    own = jnp.pad(own, ((0, EXTRA - vec.size // T), (0, 0))).astype(jnp.bfloat16)
    return lax.all_gather(own, ("tower", "batch"), axis=0)


def per_device(
    image_rows,
    text_rows,
    caption_lengths,
    concat_cot,
    tile_slot,
    tile_weight,
    tile_first,
    tile_second,
    left_stat,
    right_stat,
    left_basis,
    right_basis,
    vec_weight,
    vec_first,
    vec_second,
):
    slots = tile_weight.shape[0]
    copies = all_blocks(tile_weight, vec_weight)
    projected, image_grad, grads = tower(
        False, slots, tile_slot, caption_lengths, image_rows, concat_cot, copies
    )
    concat, text_grad, grads = tower(
        True, slots, tile_slot, caption_lengths, text_rows, concat_cot, copies, (projected, grads)
    )
    states = (tile_weight, tile_first, tile_second, left_stat, right_stat, left_basis, right_basis)
    depth = grid_depth()
    if depth is not None:
        sums, *befores = reduce_and_start(depth, grads, states)
    else:
        sums = lax.psum_scatter(grads, ("tower", "batch"), scatter_dimension=0).astype(jnp.float32)
        befores = ()
    news = optimizer(sums, states, (vec_weight, vec_first, vec_second), befores)
    return (concat, image_grad, text_grad, *news)


def solution(mesh):
    return jax.shard_map(
        per_device,
        mesh=mesh,
        in_specs=(
            P(("tower", "batch"), None, None),
            P(("tower", "batch"), None, None),
            P(),
            P(("tower", "batch"), None, None),
            P(),
            P(("tower", "batch"), None, None),
            P(("tower", "batch"), None, None),
            P(("tower", "batch"), None, None),
            P(("tower", "batch"), None, None),
            P(("tower", "batch"), None, None),
            P(("tower", "batch"), None, None),
            P(("tower", "batch"), None, None),
            P(("tower", "batch"), None),
            P(("tower", "batch"), None),
            P(("tower", "batch"), None),
        ),
        out_specs=(
            P(("tower", "batch"), None, None),
            P(("tower", "batch"), None, None),
            P(("tower", "batch"), None, None),
            P(("tower", "batch"), None, None),
            P(("tower", "batch"), None, None),
            P(("tower", "batch"), None, None),
            P(("tower", "batch"), None, None),
            P(("tower", "batch"), None, None),
            P(("tower", "batch"), None, None),
            P(("tower", "batch"), None, None),
            P(("tower", "batch"), None),
            P(("tower", "batch"), None),
            P(("tower", "batch"), None),
        ),
        check_vma=False,
    )
```
